32 devices in a mesh: dp: 8 (over z, x), tensor: 4 (over y, core).
Axes of the slice: x: 2, y: 2, z: 4, core: 2. Of those that a mesh axis runs over, the one named last changes fastest.
Arguments:
- inputs: bfloat16 [8, 1024, 1024], P('dp', 'tensor'), may hold values from -6 to 6
- cotangent: bfloat16 [8, 1024, 1024], P('dp', 'tensor'), may hold values from -6 to 6
- segment_ids: int32 [8, 1024], P('dp'), may hold values from 0 to 256, as said below
- norm_gains: bfloat16 [2, 2, 1024], P(None, None, ('dp', 'tensor')), may hold values from 0.5 to 1.5
- w_query: bfloat16 [2, 1024, 512], P(None, 'dp', 'tensor'), may hold values from -0.1875 to 0.1875
- key_value_weight: bfloat16 [2, 1024, 256], P(None, ('dp', 'tensor')), may hold values from -0.1875 to 0.1875
- w_gate_in: bfloat16 [2, 1024, 2, 1536], P(None, 'dp', None, 'tensor'), may hold values from -0.1875 to 0.1875
- w_state_in: bfloat16 [2, 1024, 256], P(None, ('dp', 'tensor')), may hold values from -0.1875 to 0.1875
- w_step: bfloat16 [2, 1024, 24], P(None, 'dp', 'tensor'), may hold values from -0.1875 to 0.1875
- ssm_channel: float32 [2, 6, 1536], P(None, None, 'tensor'), as said below
- conv_state: bfloat16 [2, 1280], P(None, ('dp', 'tensor')), as said below
- head_params: float32 [2, 3, 24], P(None, None, 'tensor'), as said below
- w_attn_out: bfloat16 [2, 512, 1024], P(None, 'tensor', 'dp'), may hold values from -0.75 to 0.75
- w_ssm_out: bfloat16 [2, 1536, 1024], P(None, 'tensor', 'dp'), may hold values from -0.15625 to 0.15625
- w_gate_up: bfloat16 [2, 1024, 2, 2048], P(None, 'dp', None, 'tensor'), may hold values from -0.1875 to 0.1875
- w_down: bfloat16 [2, 2048, 1024], P(None, 'tensor', 'dp'), may hold values from -0.125 to 0.125
Outputs:
- output: bfloat16 [8, 1024, 1024], P('dp', 'tensor')
- input_grad: float32 [8, 1024, 1024], P('dp', 'tensor')
- grad_gains: float32 [2, 2, 1024], P(None, None, ('dp', 'tensor'))
- grad_query: float32 [2, 1024, 512], P(None, 'dp', 'tensor')
- grad_keyval: float32 [2, 1024, 256], P(None, ('dp', 'tensor'))
- grad_gate_in: float32 [2, 1024, 2, 1536], P(None, 'dp', None, 'tensor')
- grad_state_in: float32 [2, 1024, 256], P(None, ('dp', 'tensor'))
- grad_step: float32 [2, 1024, 24], P(None, 'dp', 'tensor')
- grad_channel: float32 [2, 6, 1536], P(None, None, 'tensor')
- grad_conv_state: float32 [2, 1280], P(None, ('dp', 'tensor'))
- grad_head_params: float32 [2, 3, 24], P(None, None, 'tensor')
- grad_attn_out: float32 [2, 512, 1024], P(None, 'tensor', 'dp')
- grad_ssm_out: float32 [2, 1536, 1024], P(None, 'tensor', 'dp')
- grad_gate_up: float32 [2, 1024, 2, 2048], P(None, 'dp', None, 'tensor')
- grad_down: float32 [2, 2048, 1024], P(None, 'tensor', 'dp')
The draws below stay inside these ranges and needn't reach their ends.
Inputs may be any that keep to these rules, and one draw needn't show every extreme that they name: `segment_ids`: in each row the ids start at 0 and rise by at most one from a position to the next; each row holds one document of exactly 768 positions that starts after position 0 and within the row's first quarter; outside it a new document may start at any position, and in one row it starts at every one. `ssm_channel`: rows 0 to 3 are taps, row 4 a bias, the last row a gain. `conv_state`: entries 0 to 1023 are taps, the rest a bias. `head_params`: row 0 holds log decay rates, row 1 step biases, row 2 skip weights.
All inputs are finite; a program needn't handle non-finite values.
Results may differ from the reference program's by a relative error of at most 0.033.
Values may be sent and summed in bfloat16 or wider, within the bound.
No kernel may reach another device: no remote copies, remote signals or barrier semaphores. Data moves between devices by JAX's collectives and lax.ppermute only.
A program may use at most 256 MiB of HBM per device.

```python
import jax
import jax.numpy as jnp
from jax import lax

MODEL_DIM = 1024
HQ = 8
KEY_VALUE_HEADS = 2
HEAD_SIZE = 64
HS = 24
PH = 64
NS = 128
KCONV = 4
FF = 2048
SEQ = 1024
LAYER_COUNT = 2
ROWS = 8


def draw_segment_ids(key, part):
    key = jax.random.fold_in(key, 11)
    start_key, cut_key, row_key = jax.random.split(key, 3)
    long_start = jax.random.randint(start_key, (ROWS, 1), 1, SEQ // 4)
    position_ids = jnp.arange(SEQ, dtype=jnp.int32)[None, :]
    row_ids = jnp.arange(ROWS, dtype=jnp.int32)[:, None]
    dense_row = jax.random.randint(row_key, (), 0, ROWS)
    long_end = long_start + 3 * SEQ // 4
    cuts = (jax.random.randint(cut_key, (ROWS, SEQ), 0, 12) == 0) | (row_ids == dense_row)
    inside = (position_ids > long_start) & (position_ids < long_end)
    cuts = cuts & ~inside | (position_ids == long_start) | (position_ids == long_end) | (position_ids == 0)
    return (jnp.cumsum(cuts.astype(jnp.int32), axis=1) - 1).astype(jnp.int32)


def draw_ssm_channel(key, part):
    key = jax.random.fold_in(key, 23)
    shape_all = (LAYER_COUNT, KCONV + 2, HS * PH)
    noise = jnp.clip(jax.random.normal(key, shape_all, jnp.float32), -4.0, 4.0)
    row_ids = jnp.arange(KCONV + 2)[None, :, None]
    taps = 0.5 * noise
    bias_row = 0.3 * noise
    gain_row = 1.0 + 0.1 * noise
    return jnp.where(row_ids < KCONV, taps, jnp.where(row_ids == KCONV, bias_row, gain_row)).astype(jnp.float32)


def draw_conv_state(key, part):
    key = jax.random.fold_in(key, 37)
    shape_all = (LAYER_COUNT, (KCONV + 1) * 2 * NS)
    noise = jnp.clip(jax.random.normal(key, shape_all, jnp.float32), -4.0, 4.0)
    entry_ids = jnp.arange((KCONV + 1) * 2 * NS)[None, :]
    return jnp.where(entry_ids < KCONV * 2 * NS, 0.5 * noise, 0.3 * noise).astype(jnp.bfloat16)


def draw_head_params(key, part):
    key = jax.random.fold_in(key, 41)
    shape_all = (LAYER_COUNT, 3, HS)
    unit = jax.random.uniform(key, shape_all, jnp.float32, 0.0, 1.0)
    row_ids = jnp.arange(3)[None, :, None]
    decay_log = 2.7 * unit
    step_bias = -7.0 + 4.5 * unit
    skip_weight = 0.5 + unit
    return jnp.where(row_ids == 0, decay_log, jnp.where(row_ids == 1, step_bias, skip_weight)).astype(jnp.float32)


def block_levels(stream_key, shape, cuts, smallest, high):
    level = 1.0
    for dim, shards_of in cuts:
        steps = jax.random.uniform(jax.random.fold_in(jax.random.fold_in(stream_key, 6), dim), (shards_of,), jnp.float32, smallest / len(cuts), high / len(cuts))
        level = level * jnp.repeat(jnp.exp(steps), shape[dim] // shards_of).reshape((-1,) + (1,) * (len(shape) - 1 - dim))
    return level


def scatter_about(stream_key, shape, spread, most, cuts=(), kind=jnp.bfloat16):
    gain = block_levels(stream_key, shape, cuts, -0.22, 0.18) if cuts else 1.0
    drawn = jax.random.normal(stream_key, shape, jnp.float32) * spread * gain
    return jnp.minimum(jnp.maximum(drawn, -most), most).astype(kind)


def setup_inputs(seed: int = 0) -> dict:
    arg_keys = jax.random.split(jax.random.key(seed), 17)
    inputs = scatter_about(arg_keys[0], (ROWS, SEQ, MODEL_DIM), 1.0, 6.0, ((0, 8), (1, 4)))
    cotangent = scatter_about(arg_keys[1], (ROWS, SEQ, MODEL_DIM), 1.0, 6.0, ((0, 8), (1, 4)))
    segment_ids = draw_segment_ids(jax.random.fold_in(arg_keys[16], 71), 0)
    norm_gains = jnp.clip(1.0 + 0.1 * jax.random.normal(arg_keys[3], (LAYER_COUNT, 2, MODEL_DIM), jnp.float32), 0.5, 1.5).astype(jnp.bfloat16)
    w_query = scatter_about(arg_keys[4], (LAYER_COUNT, MODEL_DIM, HQ * HEAD_SIZE), MODEL_DIM ** -0.5, 0.1875, ((1, 8), (2, 4)))
    key_value_weight = scatter_about(arg_keys[5], (LAYER_COUNT, MODEL_DIM, 2 * KEY_VALUE_HEADS * HEAD_SIZE), MODEL_DIM ** -0.5, 0.1875, ((1, 32),))
    w_gate_in = scatter_about(arg_keys[6], (LAYER_COUNT, MODEL_DIM, 2, HS * PH), MODEL_DIM ** -0.5, 0.1875, ((1, 8), (3, 4)))
    w_state_in = scatter_about(arg_keys[7], (LAYER_COUNT, MODEL_DIM, 2 * NS), MODEL_DIM ** -0.5, 0.1875, ((1, 32),))
    w_step = scatter_about(arg_keys[8], (LAYER_COUNT, MODEL_DIM, HS), MODEL_DIM ** -0.5, 0.1875, ((1, 8), (2, 4)))
    ssm_channel = draw_ssm_channel(jax.random.fold_in(arg_keys[16], 71), 0)
    conv_state = draw_conv_state(jax.random.fold_in(arg_keys[16], 71), 0)
    head_params = draw_head_params(jax.random.fold_in(arg_keys[16], 71), 0)
    w_attn_out = scatter_about(arg_keys[12], (LAYER_COUNT, HQ * HEAD_SIZE, MODEL_DIM), (HQ * HEAD_SIZE // 8) ** -0.5, 0.75, ((1, 4), (2, 8)))
    w_ssm_out = scatter_about(arg_keys[13], (LAYER_COUNT, HS * PH, MODEL_DIM), (HS * PH) ** -0.5, 0.15625, ((1, 4), (2, 8)))
    w_gate_up = scatter_about(arg_keys[14], (LAYER_COUNT, MODEL_DIM, 2, FF), MODEL_DIM ** -0.5, 0.1875, ((1, 8), (3, 4)))
    w_down = scatter_about(arg_keys[15], (LAYER_COUNT, FF, MODEL_DIM), FF ** -0.5, 0.125, ((1, 4), (2, 8)))
    return {"inputs": inputs, "cotangent": cotangent, "segment_ids": segment_ids, "norm_gains": norm_gains, "w_query": w_query, "key_value_weight": key_value_weight, "w_gate_in": w_gate_in, "w_state_in": w_state_in, "w_step": w_step, "ssm_channel": ssm_channel, "conv_state": conv_state, "head_params": head_params, "w_attn_out": w_attn_out, "w_ssm_out": w_ssm_out, "w_gate_up": w_gate_up, "w_down": w_down}


@jax.custom_vjp
def low(v):
    return lax.optimization_barrier(v.astype(jnp.bfloat16)).astype(jnp.float32)

@jax.custom_vjp
def reduced_pullback(v):
    return v

def low_keep(v):
    return (low(v), None)

def low_pass(kept, grad):
    return (grad,)

def back_keep(v):
    return (v, None)

def back_low(kept, grad):
    return (low(grad),)
low.defvjp(low_keep, low_pass)
reduced_pullback.defvjp(back_keep, back_low)
EPSILON = 1e-05
ROPE_BASE = 100000000000.0
HIGHEST_PRECISION = lax.Precision.HIGHEST

def matrix_product(left, right):
    return jnp.dot(left, right, precision=HIGHEST_PRECISION, preferred_element_type=jnp.float32)

def norm_rows(values, scale_gain):
    factor = lax.rsqrt(lax.optimization_barrier(jnp.mean(values * values, axis=-1, keepdims=True)) + EPSILON)
    return values * factor * scale_gain

def positions_of(segment_row):
    position_ids = jnp.arange(segment_row.shape[0], dtype=jnp.int32)
    earlier = jnp.concatenate([segment_row[:1] - 1, segment_row[:-1]])
    first_pos = jnp.where(segment_row != earlier, position_ids, 0)
    return position_ids - lax.cummax(first_pos, axis=0)

def rotate_pairs(values, places, sign_value):
    half_width = values.shape[-1] // 2
    frequency = ROPE_BASE ** (-jnp.arange(half_width, dtype=jnp.float32) / half_width)
    angles = sign_value * places.astype(jnp.float32)[:, None] * frequency[None, :]
    cosine = jnp.cos(angles)[:, None, :]
    sine_of = jnp.sin(angles)[:, None, :]
    first_half = values[..., :half_width]
    second_half = values[..., half_width:]
    return jnp.concatenate([first_half * cosine - second_half * sine_of, second_half * cosine + first_half * sine_of], axis=-1)

def convolve(values, conv_taps, conv_bias, segment_row):
    sequence_length = values.shape[0]
    tap_count = conv_taps.shape[0]
    summed = jnp.zeros_like(values) + conv_bias[None, :]
    for shift_by in range(tap_count):
        shifted = jnp.pad(values, ((shift_by, 0), (0, 0)))[:sequence_length]
        segment_shift = jnp.pad(segment_row, (shift_by, 0), constant_values=-1)[:sequence_length]
        same_doc = (segment_shift == segment_row)[:, None]
        summed = summed + jnp.where(same_doc, shifted, 0.0) * conv_taps[tap_count - 1 - shift_by][None, :]
    return summed

def state_space(inputs, b_matrix, c_matrix, step, rate, segment_row):
    sequence_length, head_count, head_width = inputs.shape
    state_size = b_matrix.shape[1]
    block_len = min(128, sequence_length)
    block_count = sequence_length // block_len
    log_step = step * rate[None, :]
    pieces = (inputs.reshape(block_count, block_len, head_count, head_width), b_matrix.reshape(block_count, block_len, state_size), c_matrix.reshape(block_count, block_len, state_size), step.reshape(block_count, block_len, head_count), log_step.reshape(block_count, block_len, head_count), segment_row.reshape(block_count, block_len), jnp.concatenate([jnp.full((1,), -1, jnp.int32), segment_row.reshape(block_count, block_len)[:-1, -1].astype(jnp.int32)]))

    def one_block(memory, piece):
        piece_in, piece_b, piece_c, piece_step, piece_log, piece_seg, before = piece
        cumulative = jnp.cumsum(piece_log, axis=0)
        inner_prod = jnp.dot(piece_c, piece_b.T, precision=HIGHEST_PRECISION)
        log_gap = cumulative[:, None, :] - cumulative[None, :, :]
        position_ids = jnp.arange(block_len)
        allowed = (position_ids[None, :] <= position_ids[:, None]) & (piece_seg[None, :] == piece_seg[:, None])
        weights = jnp.where(allowed[:, :, None], jnp.exp(jnp.minimum(log_gap, 0.0)), 0.0) * inner_prod[:, :, None] * piece_step[None, :, :]
        intra_out = jnp.einsum('tsh,shp->thp', weights, piece_in, precision=HIGHEST_PRECISION)
        carried = jnp.where((piece_seg == before)[:, None], jnp.exp(cumulative), 0.0)
        inter_out = jnp.einsum('tn,hnp->thp', piece_c, memory, precision=HIGHEST_PRECISION) * carried[:, :, None]
        tail_log = cumulative[-1]
        tail_keep = jnp.where((piece_seg == piece_seg[-1])[:, None], jnp.exp(jnp.minimum(tail_log[None, :] - cumulative, 0.0)), 0.0) * piece_step
        fresh_state = jnp.einsum('sn,sh,shp->hnp', piece_b, tail_keep, piece_in, precision=HIGHEST_PRECISION)
        kept_state = jnp.where(piece_seg[-1] == before, 1.0, 0.0) * jnp.exp(tail_log)[:, None, None] * memory
        return (kept_state + fresh_state, intra_out + inter_out)
    start_state = jnp.zeros((head_count, state_size, head_width), jnp.float32)
    final_state, outputs = lax.scan(jax.checkpoint(one_block), start_state, pieces)
    return outputs.reshape(sequence_length, head_count, head_width)

def ssm_core(x_in, bc_in, step_raw, gate_z, conv_chan, conv_flat, head_par, segment_row):
    sequence_length = x_in.shape[0]
    head_count = step_raw.shape[-1]
    head_width = x_in.shape[-1] // head_count
    state_size = bc_in.shape[-1] // 2
    taps_state = conv_flat.reshape(-1, 2 * state_size)
    conv_x = jax.nn.silu(convolve(x_in, conv_chan[:-1], conv_chan[-1], segment_row))
    conv_bc = jax.nn.silu(convolve(bc_in, taps_state[:-1], taps_state[-1], segment_row))
    step = jax.nn.softplus(step_raw + head_par[1][None, :])
    rate = -jnp.exp(head_par[0])
    heads_in = conv_x.reshape(sequence_length, head_count, head_width)
    result = state_space(heads_in, conv_bc[:, :state_size], conv_bc[:, state_size:], step, rate, segment_row)
    result = result + head_par[2][None, :, None] * heads_in
    return result.reshape(sequence_length, head_count * head_width) * jax.nn.silu(gate_z)

def attend(queries, keys_rot, values_low, segment_row):
    sequence_length = queries.shape[0]
    block_len = min(512, sequence_length)
    group_size = queries.shape[1] // keys_rot.shape[1]
    keys_all = jnp.repeat(keys_rot, group_size, axis=1)
    values_all = jnp.repeat(values_low, group_size, axis=1)
    key_index = jnp.arange(sequence_length, dtype=jnp.int32)
    score_scale = queries.shape[2] ** (-0.5)

    def one_block(block_start):
        query_rows = lax.dynamic_slice_in_dim(queries, block_start, block_len, 0)
        row_index = block_start + jnp.arange(block_len, dtype=jnp.int32)
        row_segment = lax.dynamic_slice_in_dim(segment_row, block_start, block_len, 0)
        raw_scores = jnp.einsum('qhd,khd->hqk', query_rows, keys_all, precision=HIGHEST_PRECISION)
        scores = reduced_pullback(raw_scores * score_scale)
        allowed = (key_index[None, :] <= row_index[:, None]) & (segment_row[None, :] == row_segment[:, None])
        probs = jax.nn.softmax(jnp.where(allowed[None], scores, -1e+30), axis=-1)
        return jnp.einsum('hqk,khd->qhd', low(probs), values_all, precision=HIGHEST_PRECISION)
    starts = (jnp.arange(sequence_length // block_len) * block_len).astype(jnp.int32)
    outputs = lax.map(jax.checkpoint(one_block), starts)
    return outputs.reshape(sequence_length, queries.shape[1], queries.shape[2])

def run_layer(x_row, layer_params, segment_row, places):
    gain_pair, w_query, key_value_weight, w_gate_in, w_state_in, w_step, ssm_channel, conv_state, head_params, w_attn_out, w_ssm_out, w_gate_up, w_down = layer_params
    sequence_length = x_row.shape[0]
    hidden_rows = low(norm_rows(x_row, gain_pair[0]))
    queries = reduced_pullback(matrix_product(hidden_rows, w_query)).reshape(sequence_length, HQ, HEAD_SIZE)
    key_value_rows = reduced_pullback(matrix_product(hidden_rows, key_value_weight)).reshape(sequence_length, 2, KEY_VALUE_HEADS, HEAD_SIZE)
    query_rot = low(rotate_pairs(queries, places, 1.0))
    key_rot = low(rotate_pairs(key_value_rows[:, 0], places, 1.0))
    values_low = low(key_value_rows[:, 1])
    attended = attend(query_rot, key_rot, values_low, segment_row).reshape(sequence_length, HQ * HEAD_SIZE)
    attended = low(reduced_pullback(attended))
    gate_in = reduced_pullback(matrix_product(hidden_rows, w_gate_in.reshape(MODEL_DIM, 2 * HS * PH))).reshape(sequence_length, 2, HS * PH)
    state_in = reduced_pullback(matrix_product(hidden_rows, w_state_in))
    step_raw = reduced_pullback(matrix_product(hidden_rows, w_step))
    gated_out = ssm_core(gate_in[:, 1], state_in, step_raw, gate_in[:, 0], ssm_channel[:KCONV + 1], conv_state, head_params, segment_row)
    factor = lax.rsqrt(lax.optimization_barrier(jnp.mean(gated_out * gated_out, axis=-1, keepdims=True)) + EPSILON)
    normed = low(gated_out * factor * ssm_channel[KCONV + 1][None, :])
    mixed_out = reduced_pullback(matrix_product(attended, w_attn_out) + matrix_product(normed, w_ssm_out))
    middle = x_row + mixed_out
    second = low(norm_rows(middle, gain_pair[1]))
    gate_up = reduced_pullback(matrix_product(second, w_gate_up.reshape(MODEL_DIM, 2 * FF))).reshape(sequence_length, 2, FF)
    active = low(jax.nn.silu(gate_up[:, 0]) * gate_up[:, 1])
    return middle + reduced_pullback(matrix_product(active, w_down))

def forward(inputs_all, weight_list, segment_ids):

    def one_row(pair):
        x_row, segment_row = pair
        places = positions_of(segment_row)
        for layer_index in range(LAYER_COUNT):
            x_row = run_layer(x_row, [member[layer_index] for member in weight_list], segment_row, places)
        return x_row
    return lax.map(jax.checkpoint(one_row), (inputs_all, segment_ids))

def reference(inputs, cotangent, segment_ids, norm_gains, w_query, key_value_weight, w_gate_in, w_state_in, w_step, ssm_channel, conv_state, head_params, w_attn_out, w_ssm_out, w_gate_up, w_down):
    params = [member.astype(jnp.float32) for member in (norm_gains, w_query, key_value_weight, w_gate_in, w_state_in, w_step, ssm_channel, conv_state, head_params, w_attn_out, w_ssm_out, w_gate_up, w_down)]

    def whole(inputs_all, *weight_list):
        return forward(inputs_all, weight_list, segment_ids)
    output, pullback = jax.vjp(whole, inputs.astype(jnp.float32), *params)
    gradients = pullback(cotangent.astype(jnp.float32))
    return (output.astype(jnp.bfloat16), gradients[0], gradients[1], gradients[2], gradients[3], gradients[4], gradients[5], gradients[6], gradients[7], gradients[8], gradients[9], gradients[10], gradients[11], gradients[12], gradients[13])
```

```python
import functools

import jax
import jax.numpy as jnp
from jax import lax
from jax.experimental import pallas as pl
from jax.experimental.pallas import tpu as pltpu
from jax.sharding import PartitionSpec as P

HQ = 8
HD = 64
HS = 24
PH = 64
NS = 128
LAYERS = 2
EPS = 1e-05
ROPE_BASE = 100000000000.0
CHUNK = 128
QBLOCK = 256
F32 = jnp.float32
BF16 = jnp.bfloat16
EXACT = lax.Precision.HIGHEST
NEG = -1e30
VMEM_BYTES = 48 * 1024 * 1024


def dot_nn(left, right, **kw):
    return lax.dot_general(
        left, right, (((1,), (0,)), ((), ())), preferred_element_type=F32, **kw
    )


def dot_nt(left, right, **kw):
    return lax.dot_general(
        left, right, (((1,), (1,)), ((), ())), preferred_element_type=F32, **kw
    )


def dot_tn(left, right, **kw):
    return lax.dot_general(
        left, right, (((0,), (0,)), ((), ())), preferred_element_type=F32, **kw
    )


def iota(shape, dim):
    return lax.broadcasted_iota(jnp.int32, shape, dim)


def softplus(v):
    return jnp.maximum(v, 0.0) + jnp.log1p(jnp.exp(-jnp.abs(v)))


def partner(v, lane):
    return jnp.where(lane % HD < HD // 2, pltpu.roll(v, 96, 1), pltpu.roll(v, 32, 1))


def chunk_terms(act, raw_step, tok, seg_row, par):
    shape = (CHUNK, CHUNK)
    row, lane = iota(shape, 0), iota(shape, 1)
    b, c = act[:, 384:512], act[:, 512:640]
    bb, cb = b.astype(BF16), c.astype(BF16)
    dt = softplus(raw_step + par[1:2])
    tri = (row >= lane).astype(F32)
    cum = dot_nn(tri, dt * par[0:1], precision=EXACT)
    last = cum[CHUNK - 1 : CHUNK]
    okay = (row >= lane) & (tok[:, 5:6] == seg_row)
    inner = jnp.where(okay, dot_nt(cb, bb), 0.0)
    enter = jnp.exp(cum) * tok[:, 3:4]
    tail = jnp.exp(jnp.minimum(last - cum, 0.0)) * tok[:, 4:5]
    return b, c, bb, cb, dt, cum, cum.T, dt.T, okay, inner, enter, tail


def ssm_fwd_kernel(
    pa, ps, tok_r, seg_r, cos_r, sin_r, taps, par, skip,
    y_o, pre_o, st_o, sq_o, q_o, kv_o, state, hist,
):
    @pl.when(pl.program_id(0) == 0)
    def _():
        state[...] = jnp.zeros_like(state)
        hist[...] = jnp.zeros_like(hist)

    lane = iota((CHUNK, CHUNK), 1)
    half = lane < PH
    tok = tok_r[...]
    xin = jnp.concatenate([pa[:, 512:896], ps[:, 128:384]], axis=1)
    ext = jnp.concatenate([hist[...], xin], axis=0)
    hist[...] = xin[CHUNK - 8 :]
    pre = taps[4:5] + xin * taps[3:4]
    for k in (1, 2, 3):
        pre = pre + ext[8 - k : 8 - k + CHUNK] * tok[:, k - 1 : k] * taps[3 - k : 4 - k]
    pre_o[...] = pre
    act = pre * jax.nn.sigmoid(pre)
    b, c, bb, cb, dt, cum, cum_t, dt_t, okay, inner, enter, tail = chunk_terms(
        act, pa[:, 896:1024], tok, seg_r[0:1], par
    )
    tail = tail * dt
    keep = enter[CHUNK - 1 : CHUNK]
    b_t = b.T.astype(BF16)
    squares = jnp.zeros((CHUNK, CHUNK), F32)
    for p in range(3):
        h0, h1 = 2 * p, 2 * p + 1
        cols = slice(128 * p, 128 * p + 128)
        xp = act[:, cols]
        xb = xp.astype(BF16)
        own = st_o.at[0]
        sp = state[:, cols]
        own[:, cols] = sp

        def weights(h):
            gap = jnp.minimum(cum[:, h : h + 1] - cum_t[h : h + 1], 0.0)
            return (inner * jnp.exp(gap) * dt_t[h : h + 1]).astype(BF16)

        y = jnp.where(half, dot_nn(weights(h0), xb), dot_nn(weights(h1), xb))
        y = y + dot_nn(cb, sp.astype(BF16)) * jnp.where(
            half, enter[:, h0 : h0 + 1], enter[:, h1 : h1 + 1]
        )
        y = y + skip[0:1, cols] * xp
        y_o[:, cols] = y
        tp = jnp.where(half, tail[:, h0 : h0 + 1], tail[:, h1 : h1 + 1])
        kp = jnp.where(half[0:1], keep[:, h0 : h0 + 1], keep[:, h1 : h1 + 1])
        state[:, cols] = kp * sp + dot_nn(b_t, (tp * xp).astype(BF16))
        z = pa[:, 128 + 128 * p : 256 + 128 * p]
        u = y * z * jax.nn.sigmoid(z)
        squares = squares + u * u
    sq_o[...] = dot_nt(jnp.ones((8, CHUNK), F32), squares, precision=EXACT)
    cos, sin = cos_r[...], sin_r[...]
    q = pa[:, 0:128]
    q_o[...] = (q * cos + partner(q, lane) * sin).astype(BF16)
    kv = ps[:, 0:128]
    kv_o[...] = jnp.where(half, kv * cos + partner(kv, lane) * sin, kv).astype(BF16)


def ssm_bwd_kernel(
    pa, ps, pre_r, y_r, st_r, dyn_r, red_r, dq_r, dkv_r, tok_r, seg_r, taps, par, skip, gain,
    da_o, ds_o, gt_o, gc_o, gh_o, dstate, nxt,
):
    @pl.when(pl.program_id(0) == 0)
    def _():
        dstate[...] = jnp.zeros_like(dstate)
        nxt[...] = jnp.zeros_like(nxt)
        gt_o[...] = jnp.zeros_like(gt_o)
        gc_o[...] = jnp.zeros_like(gc_o)
        gh_o[...] = jnp.zeros_like(gh_o)

    shape = (CHUNK, CHUNK)
    row, lane = iota(shape, 0), iota(shape, 1)
    half = lane < PH
    sub = iota((8, CHUNK), 0)
    tok = tok_r[...]
    pre = pre_r[...]
    sg = jax.nn.sigmoid(pre)
    act = pre * sg
    b, c, bb, cb, dt, cum, cum_t, dt_t, okay, inner, enter, tail = chunk_terms(
        act, pa[:, 896:1024], tok, seg_r[0:1], par
    )
    tail_dt = tail * dt
    keep = enter[CHUNK - 1 : CHUNK]
    c_t = c.T.astype(BF16)
    r2 = jnp.broadcast_to(red_r[0:1], shape).T
    coef = jnp.broadcast_to(red_r[1:2], shape).T
    db = jnp.zeros(shape, F32)
    dc = jnp.zeros(shape, F32)
    dinner = jnp.zeros(shape, F32)
    dcum = jnp.zeros(shape, F32)
    extra = jnp.zeros(shape, F32)
    col_sum = jnp.zeros((8, CHUNK), F32)
    last_row = jnp.zeros((1, CHUNK), F32)
    dx_parts = []
    for p in range(3):
        cols = slice(128 * p, 128 * p + 128)
        z = pa[:, 128 + 128 * p : 256 + 128 * p]
        y, dyn = y_r[:, cols], dyn_r[:, cols]
        zs = jax.nn.sigmoid(z)
        sz = z * zs
        u = y * sz
        dn = dyn * r2
        gc_o[0:1, cols] += jnp.sum(dn * u, axis=0, keepdims=True)
        du = gain[0:1, cols] * dn - u * coef
        da_o[:, 128 + 128 * p : 256 + 128 * p] = (
            du * y * zs * (1.0 + z * (1.0 - zs))
        ).astype(BF16)
        dy = du * sz
        dyb = dy.astype(BF16)
        xp = act[:, cols]
        xb = xp.astype(BF16)
        gc_o[1:2, cols] += jnp.sum(dy * xp, axis=0, keepdims=True)
        own = st_r.at[0]
        sp = own[:, cols]
        sb = sp.astype(BF16)
        dsp = dstate[:, cols]
        dsb = dsp.astype(BF16)
        h0, h1 = 2 * p, 2 * p + 1
        ep = jnp.where(half, enter[:, h0 : h0 + 1], enter[:, h1 : h1 + 1])
        tp = jnp.where(half, tail_dt[:, h0 : h0 + 1], tail_dt[:, h1 : h1 + 1])
        kp = jnp.where(half[0:1], keep[:, h0 : h0 + 1], keep[:, h1 : h1 + 1])
        cdb = (ep * dy).astype(BF16)
        through = dy * ep * dot_nn(cb, sb)
        bds = dot_nn(bb, dsb)
        qx = xp * bds
        kept = jnp.sum(dsp * sp, axis=0, keepdims=True) * kp
        dxi = []
        for h in (h0, h1):
            mine = half if h == h0 else ~half
            gap = jnp.minimum(cum[:, h : h + 1] - cum_t[h : h + 1], 0.0)
            decay = jnp.where(okay, jnp.exp(gap), 0.0)
            dt_row = dt_t[h : h + 1]
            dg = dot_nt(jnp.where(mine, dy, 0.0).astype(BF16), xb)
            t1 = dg * decay
            dinner = dinner + t1 * dt_row
            w0 = t1 * inner
            col_sum = col_sum + jnp.where(sub == h, jnp.sum(w0, axis=0, keepdims=True), 0.0)
            w1 = w0 * dt_row + jnp.where(mine, through, 0.0)
            dcum = dcum + jnp.where(lane == h, jnp.sum(w1, axis=1, keepdims=True), 0.0)
            e = jnp.sum(jnp.where(mine, qx, 0.0), axis=1, keepdims=True)
            extra = extra + jnp.where(lane == h, e, 0.0)
            k = jnp.sum(jnp.where(mine[0:1], kept, 0.0), axis=1, keepdims=True)
            last_row = last_row + jnp.where(lane[0:1] == h, k, 0.0)
            dxi.append(dot_tn((decay * inner * dt_row).astype(BF16), dyb))
        dx_parts.append(jnp.where(half, dxi[0], dxi[1]) + tp * bds + skip[0:1, cols] * dy)
        dc = dc + dot_nt(cdb, sb)
        db = db + dot_nt((tp * xp).astype(BF16), dsb)
        dstate[:, cols] = kp * dsp + dot_nn(c_t, cdb)
    col_sum = jnp.concatenate([col_sum, jnp.zeros((CHUNK - 8, CHUNK), F32)], axis=0).T
    moved = tail_dt * extra
    last_row = last_row + jnp.sum(moved, axis=0, keepdims=True)
    dcum = dcum - col_sum * dt - moved + jnp.where(row == CHUNK - 1, last_row, 0.0)
    dlog = dot_nn((row <= lane).astype(F32), dcum, precision=EXACT)
    ddt = col_sum + tail * extra + par[0:1] * dlog
    gh_o[0:1] += jnp.sum(dt * dlog, axis=0, keepdims=True)
    ddr = ddt * jax.nn.sigmoid(pa[:, 896:1024] + par[1:2])
    gh_o[1:2] += jnp.sum(ddr, axis=0, keepdims=True)
    da_o[:, 896:1024] = ddr.astype(BF16)
    dib = dinner.astype(BF16)
    dc = dc + dot_nn(dib, bb)
    db = db + dot_tn(dib, cb)
    dact = jnp.concatenate([*dx_parts, db, dc], axis=1)
    dpre = dact * sg * (1.0 + pre * (1.0 - sg))
    xin = jnp.concatenate([pa[:, 512:896], ps[:, 128:384]], axis=1)
    dxin = dpre * taps[3:4]
    gt_o[3:4] += jnp.sum(dpre * xin, axis=0, keepdims=True)
    gt_o[4:5] += jnp.sum(dpre, axis=0, keepdims=True)
    for k in (1, 2, 3):
        zk = dpre * tok[:, k - 1 : k]
        later = nxt.at[k - 1]
        moved_up = jnp.concatenate([zk, later[...]], axis=0)[k : k + CHUNK]
        later[...] = zk[0:8]
        dxin = dxin + moved_up * taps[3 - k : 4 - k]
        gt_o[3 - k : 4 - k] += jnp.sum(moved_up * xin, axis=0, keepdims=True)
    da_o[:, 512:896] = dxin[:, 0:384].astype(BF16)
    ds_o[:, 128:384] = dxin[:, 384:640].astype(BF16)
    da_o[:, 0:128] = dq_r[...]
    ds_o[:, 0:128] = dkv_r[...]


def ssm_forward(pa, ps, tok, seg_rows, cos, sin, taps, par, skip):
    n = pa.shape[0]
    steps = n // CHUNK

    def rows(width):
        return pl.BlockSpec((CHUNK, width), lambda i: (i, 0))

    def fixed(shape):
        return pl.BlockSpec(shape, lambda i: (0,) * len(shape))

    return pl.pallas_call(
        ssm_fwd_kernel,
        grid=(steps,),
        in_specs=[
            rows(1024), rows(384), rows(8), pl.BlockSpec((8, CHUNK), lambda i: (0, i)),
            rows(128), rows(128), fixed((8, 640)), fixed((8, 128)), fixed((8, 384)),
        ],
        out_specs=[
            rows(384), rows(640), pl.BlockSpec((1, NS, 384), lambda i: (i, 0, 0)),
            pl.BlockSpec((8, CHUNK), lambda i: (0, i)), rows(128), rows(128),
        ],
        out_shape=[
            jax.ShapeDtypeStruct((n, 384), F32),
            jax.ShapeDtypeStruct((n, 640), F32),
            jax.ShapeDtypeStruct((steps, NS, 384), F32),
            jax.ShapeDtypeStruct((8, n), F32),
            jax.ShapeDtypeStruct((n, 128), BF16),
            jax.ShapeDtypeStruct((n, 128), BF16),
        ],
        scratch_shapes=[pltpu.VMEM((NS, 384), F32), pltpu.VMEM((8, 640), F32)],
        compiler_params=pltpu.CompilerParams(
            dimension_semantics=("arbitrary",), vmem_limit_bytes=VMEM_BYTES
        ),
        cost_estimate=pl.CostEstimate(
            flops=2 * 10**9, bytes_accessed=14 * 2**20, transcendentals=3 * 10**6
        ),
        name="ssm_forward",
    )(pa, ps, tok, seg_rows, cos, sin, taps, par, skip)


def ssm_backward(pa, ps, pre, y, states, dyn, red, dq, dkv, tok, seg_rows, taps, par, skip, gain):
    n = pa.shape[0]
    steps = n // CHUNK

    def rows(width):
        return pl.BlockSpec((CHUNK, width), lambda i: (steps - 1 - i, 0))

    def lanes():
        return pl.BlockSpec((8, CHUNK), lambda i: (0, steps - 1 - i))

    def fixed(shape):
        return pl.BlockSpec(shape, lambda i: (0,) * len(shape))

    return pl.pallas_call(
        ssm_bwd_kernel,
        grid=(steps,),
        in_specs=[
            rows(1024), rows(384), rows(640), rows(384),
            pl.BlockSpec((1, NS, 384), lambda i: (steps - 1 - i, 0, 0)),
            rows(384), lanes(), rows(128), rows(128), rows(8), lanes(),
            fixed((8, 640)), fixed((8, 128)), fixed((8, 384)), fixed((8, 384)),
        ],
        out_specs=[
            rows(1024), rows(384), fixed((8, 640)), fixed((8, 384)), fixed((8, 128)),
        ],
        out_shape=[
            jax.ShapeDtypeStruct((n, 1024), BF16),
            jax.ShapeDtypeStruct((n, 384), BF16),
            jax.ShapeDtypeStruct((8, 640), F32),
            jax.ShapeDtypeStruct((8, 384), F32),
            jax.ShapeDtypeStruct((8, 128), F32),
        ],
        scratch_shapes=[pltpu.VMEM((NS, 384), F32), pltpu.VMEM((3, 8, 640), F32)],
        compiler_params=pltpu.CompilerParams(
            dimension_semantics=("arbitrary",), vmem_limit_bytes=VMEM_BYTES
        ),
        cost_estimate=pl.CostEstimate(
            flops=5 * 10**9, bytes_accessed=20 * 2**20, transcendentals=4 * 10**6
        ),
        name="ssm_backward",
    )(pa, ps, pre, y, states, dyn, red, dq, dkv, tok, seg_rows, taps, par, skip, gain)


def head_views(kv, lane):
    zero = jnp.zeros_like(kv)
    left = lane < HD
    k0 = jnp.where(left, kv, zero)
    v1 = jnp.where(left, zero, kv)
    k1 = pltpu.roll(k0.astype(F32), HD, 1).astype(BF16)
    v0 = pltpu.roll(v1.astype(F32), HD, 1).astype(BF16)
    return (k0, k1), (v0, v1)


def allowed_keys(tok_r, seg_r, start, rows, keys):
    return (
        (iota((rows, keys), 1) <= start + iota((rows, keys), 0))
        & (tok_r[start : start + rows, 5:6] == seg_r[0:1, 0:keys])
    )


def attend_fwd_kernel(q_r, kv_r, tok_r, seg_r, o_o, lse_o):
    n = q_r.shape[0]
    ks, vs = head_views(kv_r[...], iota((n, 2 * HD), 1))
    lane = iota((QBLOCK, 128), 1)
    for start in range(0, n, QBLOCK):
        keys = start + QBLOCK
        q = q_r[start:keys]
        okay = allowed_keys(tok_r, seg_r, start, QBLOCK, keys)
        out = jnp.zeros((QBLOCK, 2 * HD), F32)
        stats = []
        for h in range(2):
            s = jnp.where(okay, dot_nt(q, ks[h][0:keys]) * HD**-0.5, NEG)
            top = jnp.max(s, axis=1, keepdims=True)
            e = jnp.exp(s - top)
            total = jnp.sum(e, axis=1, keepdims=True)
            out = out + dot_nn((e * (1.0 / total)).astype(BF16), vs[h][0:keys])
            stats.append(top + jnp.log(total))
        o_o[start:keys] = out.astype(BF16)
        lse_o[start:keys] = jnp.where(lane == 0, stats[0], stats[1])


def attend_bwd_kernel(
    q_r, kv_r, do_r, lse_r, tok_r, seg_r, cos_r, sin_r, dq_o, dkv_o, dk_acc, dv_acc
):
    n = q_r.shape[0]
    ks, vs = head_views(kv_r[...], iota((n, 2 * HD), 1))
    lane = iota((QBLOCK, 128), 1)
    left = lane < HD
    dk_acc[...] = jnp.zeros_like(dk_acc)
    dv_acc[...] = jnp.zeros_like(dv_acc)
    for start in range(0, n, QBLOCK):
        keys = start + QBLOCK
        q = q_r[start:keys]
        do = do_r[start:keys]
        okay = allowed_keys(tok_r, seg_r, start, QBLOCK, keys)
        lse = lse_r[start:keys]
        zero = jnp.zeros_like(q)
        dq = jnp.zeros((QBLOCK, 2 * HD), F32)
        for h in range(2):
            mine = left if h == 0 else ~left
            s = dot_nt(q, ks[h][0:keys]) * HD**-0.5
            p = jnp.where(okay, jnp.exp(s - lse[:, h : h + 1]), 0.0)
            dp = dot_nt(do, vs[h][0:keys])
            dot_sum = jnp.sum(p * dp, axis=1, keepdims=True)
            ds = (p * (dp - dot_sum)).astype(BF16)
            dq = dq + dot_nn(ds, ks[h][0:keys])
            dk_acc[0:keys] += dot_tn(ds, jnp.where(mine, q, zero))
            dv_acc[0:keys] += dot_tn(p.astype(BF16), jnp.where(mine, do, zero))
        dq = dq * HD**-0.5
        dq_o[start:keys] = (
            dq * cos_r[start:keys] - partner(dq, lane) * sin_r[start:keys]
        ).astype(BF16)
    for start in range(0, n, QBLOCK):
        rows = slice(start, start + QBLOCK)
        dk, dv = dk_acc[rows], dv_acc[rows]
        dk = (dk + pltpu.roll(dk, HD, 1)) * HD**-0.5
        dv = dv + pltpu.roll(dv, HD, 1)
        dk = dk * cos_r[rows] - partner(dk, lane) * sin_r[rows]
        dkv_o[rows] = jnp.where(left, dk, dv).astype(BF16)


def attend_forward(q, kv, tok, seg_rows):
    n = q.shape[0]
    return pl.pallas_call(
        attend_fwd_kernel,
        out_shape=[
            jax.ShapeDtypeStruct((n, 128), BF16),
            jax.ShapeDtypeStruct((n, 128), F32),
        ],
        compiler_params=pltpu.CompilerParams(vmem_limit_bytes=VMEM_BYTES),
        cost_estimate=pl.CostEstimate(
            flops=10**9, bytes_accessed=3 * 2**20, transcendentals=2 * 10**6
        ),
        name="attend_forward",
    )(q, kv, tok, seg_rows)


def attend_backward(q, kv, do, lse, tok, seg_rows, cos, sin):
    n = q.shape[0]
    return pl.pallas_call(
        attend_bwd_kernel,
        out_shape=[
            jax.ShapeDtypeStruct((n, 128), BF16),
            jax.ShapeDtypeStruct((n, 128), BF16),
        ],
        scratch_shapes=[pltpu.VMEM((n, 128), F32), pltpu.VMEM((n, 128), F32)],
        compiler_params=pltpu.CompilerParams(vmem_limit_bytes=VMEM_BYTES),
        cost_estimate=pl.CostEstimate(
            flops=2 * 10**9, bytes_accessed=5 * 2**20, transcendentals=2 * 10**6
        ),
        name="attend_backward",
    )(q, kv, do, lse, tok, seg_rows, cos, sin)


def swap(values, axis, distance):
    size = lax.axis_size(axis)
    return lax.ppermute(values, axis, [(i, i ^ distance) for i in range(size)])


def bits_of(axis):
    size = lax.axis_size(axis)
    return [1 << b for b in range(size.bit_length() - 1)]


def sum_over(values, axes):
    for axis in axes:
        for bit in bits_of(axis):
            values = values + swap(values, axis, bit)
    return values


def rows_gather(own, rank):
    far = swap(own, "tensor", 2)
    near = swap(own, "tensor", 1)
    both = swap(far, "tensor", 1)
    q = own.shape[0]
    full = jnp.zeros((4 * q, own.shape[1]), own.dtype)
    for distance, piece in ((0, own), (1, near), (2, far), (3, both)):
        full = lax.dynamic_update_slice(full, piece, ((rank ^ distance) * q, 0))
    return full


def rows_scatter(full, rank):
    q = full.shape[0] // 4

    def part(distance):
        return lax.dynamic_slice_in_dim(full, (rank ^ distance) * q, q, 0)

    other = swap(part(3), "tensor", 1)
    near = swap(part(1), "tensor", 1)
    sent = (part(2).astype(F32) + other.astype(F32)).astype(BF16)
    far = swap(sent, "tensor", 2)
    return part(0).astype(F32) + near.astype(F32) + far.astype(F32)


def gather_everywhere(row):
    index = lax.axis_index("dp") * lax.axis_size("tensor") + lax.axis_index("tensor")
    held, order = row, [0]
    for axis, scale in (("tensor", 1), ("dp", lax.axis_size("tensor"))):
        for bit in bits_of(axis):
            held = jnp.concatenate([held, swap(held, axis, bit)], axis=0)
            order = order + [o + bit * scale for o in order]
    want = index ^ jnp.arange(len(order))
    pick = (jnp.asarray(order)[None, :] == want[:, None]).astype(F32)
    return jnp.dot(pick, held.astype(F32), precision=EXACT)


def rms_factor(v):
    return lax.rsqrt(jnp.mean(v * v, axis=-1, keepdims=True) + EPS)


def rms_back(v, factor, gain, grad):
    weighted = grad * gain
    inner = jnp.mean(weighted * v, axis=-1, keepdims=True)
    grad_gain = jnp.sum(grad * v * factor, axis=0)
    return factor * weighted - v * factor**3 * inner, grad_gain


def pad_rows(v, rows=8):
    return jnp.pad(v, ((0, rows - v.shape[0]), (0, 0)))


def body(
    inputs, cotangent, segment_ids, norm_gains, w_query, key_value_weight, w_gate_in, w_state_in,
    w_step, ssm_channel, conv_state, head_params, w_attn_out, w_ssm_out, w_gate_up, w_down,
):
    quarter, width = inputs.shape[1:]
    n = segment_ids.shape[1]
    dp_size, tp_size = lax.axis_size("dp"), lax.axis_size("tensor")
    rank = lax.axis_index("tensor")
    slot = lax.axis_index("dp") * tp_size + rank
    kv_heads = key_value_weight.shape[2] // (2 * HD)
    own_head = rank * (w_query.shape[2] // HD) // (HQ // kv_heads)
    ssm_heads = w_step.shape[2]
    channels = ssm_heads * PH
    hidden = w_gate_up.shape[3]
    depth = w_query.shape[1]

    seg = segment_ids[0]
    segf = seg.astype(F32)
    index = jnp.arange(n, dtype=jnp.int32)
    places = index - jnp.sum((seg[None, :] < seg[:, None]).astype(jnp.int32), axis=1)
    freq = ROPE_BASE ** (-jnp.arange(HD // 2, dtype=F32) / (HD // 2))
    angle = places.astype(F32)[:, None] * freq[None, :]
    cos_one, sin_one = jnp.cos(angle), jnp.sin(angle)
    cos = jnp.concatenate([cos_one] * 4, axis=1)
    sin = jnp.concatenate([-sin_one, sin_one] * 2, axis=1)
    shifted = [
        (jnp.pad(seg, (k, 0), constant_values=-1)[:n] == seg).astype(F32) for k in (1, 2, 3)
    ]
    ends = seg.reshape(-1, CHUNK)[:, -1]
    before = jnp.concatenate([jnp.full((1,), -1, jnp.int32), ends[:-1]])
    enters = (seg.reshape(-1, CHUNK) == before[:, None]).astype(F32).reshape(-1)
    leaves = (seg.reshape(-1, CHUNK) == ends[:, None]).astype(F32).reshape(-1)
    tok = jnp.stack([*shifted, enters, leaves, segf, segf, segf], axis=1)
    seg_rows = jnp.broadcast_to(segf[None, :], (8, n))

    x_full = rows_gather(inputs[0], rank)

    small = jnp.concatenate([norm_gains.reshape(-1), conv_state.reshape(-1)])[None, :]
    small_all = gather_everywhere(small)
    gain_count = norm_gains.size
    gains = (
        small_all[:, :gain_count]
        .reshape(-1, LAYERS, 2, norm_gains.shape[2])
        .transpose(1, 2, 0, 3)
        .reshape(LAYERS, 2, width)
    )
    conv_flat = (
        small_all[:, gain_count:]
        .reshape(-1, LAYERS, conv_state.shape[1])
        .transpose(1, 0, 2)
        .reshape(LAYERS, 5, 2 * NS)
    )
    shared = jnp.concatenate([key_value_weight, w_state_in], axis=2)
    near = swap(shared, "tensor", 1)
    far = swap(shared, "tensor", 2)
    both = swap(shared, "tensor", 3)
    sq = shared.shape[1]
    block = jnp.zeros((LAYERS, tp_size * sq, shared.shape[2]), BF16)
    for distance, piece in ((0, shared), (1, near), (2, far), (3, both)):
        block = lax.dynamic_update_slice(block, piece, (0, (rank ^ distance) * sq, 0))

    def gather_dp(v):
        return lax.all_gather(v, "dp", axis=0, tiled=True)

    weights = []
    for layer in range(LAYERS):
        first = jnp.concatenate(
            [
                w_query[layer],
                w_gate_in[layer].reshape(depth, 2 * channels),
                jnp.pad(w_step[layer], ((0, 0), (0, 128 - ssm_heads))),
                block[layer],
            ],
            axis=1,
        )
        second = jnp.concatenate(
            [
                w_attn_out[layer].T,
                w_ssm_out[layer].T,
                w_gate_up[layer].reshape(depth, 2 * hidden),
                w_down[layer].T,
            ],
            axis=1,
        )
        first, second = gather_dp(first), gather_dp(second)
        w_in = first[:, :1024]
        keys = lax.dynamic_slice_in_dim(first, 1024 + own_head * HD, HD, 1)
        values = lax.dynamic_slice_in_dim(first, 1024 + (kv_heads + own_head) * HD, HD, 1)
        w_sh = jnp.concatenate([keys, values, first[:, 1024 + 2 * kv_heads * HD :]], axis=1)
        weights.append(
            (w_in, w_sh, second[:, :512], second[:, 512 : 512 + 2 * hidden], second[:, 512 + 2 * hidden :])
        )

    residual = inputs[0].astype(F32)
    saved = []
    for layer in range(LAYERS):
        w_in, w_sh, w_mix, w_gu, w_dn = weights[layer]
        channel = ssm_channel[layer]
        head = head_params[layer]
        taps = jnp.concatenate([channel[:5], conv_flat[layer]], axis=1)
        taps = pad_rows(taps)
        rate = -jnp.exp(head[0])
        par = pad_rows(
            jnp.pad(jnp.stack([rate, head[1]]), ((0, 0), (0, 128 - ssm_heads)))
        )
        skip = pad_rows(jnp.repeat(head[2], PH)[None, :])
        gain_row = pad_rows(channel[5:6])
        if layer == 0:
            xf = x_full.astype(F32)
            h = (xf * rms_factor(xf) * gains[0, 0]).astype(BF16)
        else:
            h = rows_gather((residual * rms_factor(residual) * gains[layer, 0]).astype(BF16), rank)
        pa = dot_nn(h, w_in)
        ps = dot_nn(h, w_sh)
        y, pre, states, sq, q_rot, kv_rot = ssm_forward(
            pa, ps, tok, seg_rows, cos, sin, taps, par, skip
        )
        sq_own = sq[0:1]
        sq_all = (
            sq_own + swap(sq_own, "tensor", 1) + swap(sq_own, "tensor", 2) + swap(sq_own, "tensor", 3)
        )
        o, lse = attend_forward(q_rot, kv_rot, tok, seg_rows)
        factor = lax.rsqrt(sq_all[0] / (HS * PH) + EPS)
        u = y * jax.nn.silu(pa[:, 128 : 128 + channels])
        yn = (u * factor[:, None] * channel[5]).astype(BF16)
        mixed_in = jnp.concatenate([o, yn], axis=1)
        middle = residual + rows_scatter(dot_nt(mixed_in, w_mix).astype(BF16), rank)
        h2 = rows_gather((middle * rms_factor(middle) * gains[layer, 1]).astype(BF16), rank)
        gu = dot_nn(h2, w_gu)
        act = (jax.nn.silu(gu[:, :hidden]) * gu[:, hidden:]).astype(BF16)
        result = middle + rows_scatter(dot_nt(act, w_dn).astype(BF16), rank)
        saved.append(
            (residual, middle, h, pa, ps, y, pre, states, q_rot, kv_rot, lse, factor, mixed_in, h2, gu, act,
             taps, par, skip, gain_row, rate)
        )
        residual = result

    grad = cotangent[0].astype(F32)
    big, small_grads = [None] * LAYERS, [None] * LAYERS
    for layer in reversed(range(LAYERS)):
        w_in, w_sh, w_mix, w_gu, w_dn = weights[layer]
        (first_in, middle, h, pa, ps, y, pre, states, q_rot, kv_rot, lse, factor, mixed_in, h2, gu, act,
         taps, par, skip, gain_row, rate) = saved[layer]
        df = rows_gather(grad.astype(BF16), rank)
        dact = dot_nn(df, w_dn)
        g0, g1 = gu[:, :hidden], gu[:, hidden:]
        sg = jax.nn.sigmoid(g0)
        dgu = jnp.concatenate(
            [dact * g1 * sg * (1.0 + g0 * (1.0 - sg)), dact * g0 * sg], axis=1
        ).astype(BF16)
        dh2 = rows_scatter(dot_nt(dgu, w_gu).astype(BF16), rank)
        ffn_grads = jnp.concatenate([dot_tn(h2, dgu), dot_tn(df, act)], axis=1).astype(BF16)
        ffn_grads = lax.psum_scatter(ffn_grads, "dp", scatter_dimension=0, tiled=True)
        through, dgain2 = rms_back(middle, rms_factor(middle), gains[layer, 1], dh2)
        dx1 = grad + through
        dm = rows_gather(dx1.astype(BF16), rank)
        dmix = dot_nn(dm, w_mix)
        do = dmix[:, :128].astype(BF16)
        dyn = dmix[:, 128:]
        u = y * jax.nn.silu(pa[:, 128 : 128 + channels])
        cross = jnp.sum(dyn * u * gain_row[0:1], axis=1)[None, :]
        cross = cross + swap(cross, "tensor", 1) + swap(cross, "tensor", 2) + swap(cross, "tensor", 3)
        dq, dkv = attend_backward(q_rot, kv_rot, do, lse, tok, seg_rows, cos, sin)
        red = pad_rows(jnp.stack([factor, factor**3 * cross[0] / (HS * PH)]))
        da, dsh, g_taps, g_chan, g_head = ssm_backward(
            pa, ps, pre, y, states, dyn, red, dq, dkv, tok, seg_rows, taps, par, skip, gain_row
        )
        dh = rows_scatter((dot_nt(da, w_in) + dot_nt(dsh, w_sh)).astype(BF16), rank)
        g_sh = dot_tn(h, dsh)
        wide = jnp.zeros((width, 2 * kv_heads * HD), F32)
        wide = lax.dynamic_update_slice(wide, g_sh[:, :HD], (0, own_head * HD))
        wide = lax.dynamic_update_slice(wide, g_sh[:, HD : 2 * HD], (0, (kv_heads + own_head) * HD))
        mix_grads = jnp.concatenate(
            [dot_tn(h, da), dot_tn(dm, mixed_in), wide, g_sh[:, 2 * HD :]], axis=1
        ).astype(BF16)
        mix_grads = lax.psum_scatter(mix_grads, "dp", scatter_dimension=0, tiled=True)
        back, dgain1 = rms_back(first_in, rms_factor(first_in), gains[layer, 0], dh)
        grad = dx1 + back
        chan_grad = jnp.concatenate([g_taps[:5, :channels], g_chan[0:1]], axis=0)
        head_grad = jnp.stack(
            [
                g_head[0, :ssm_heads] * rate,
                g_head[1, :ssm_heads],
                jnp.sum(g_chan[1].reshape(ssm_heads, PH), axis=1),
            ]
        )
        big[layer] = (ffn_grads, mix_grads)
        small_grads[layer] = (
            jnp.concatenate([dgain1, dgain2, g_taps[:5, channels:].reshape(-1)]),
            jnp.concatenate([chan_grad.reshape(-1), head_grad.reshape(-1)]),
        )

    wide_small = jnp.concatenate([small_grads[l][0] for l in range(LAYERS)])
    local_small = jnp.concatenate([small_grads[l][1] for l in range(LAYERS)])
    total = sum_over(jnp.concatenate([wide_small, local_small])[None, :], ("dp",))[0]
    wide_small = sum_over(total[None, : wide_small.shape[0]], ("tensor",))[0]
    wide_small = wide_small.reshape(LAYERS, -1)
    local_small = total[wide_small.size :].reshape(LAYERS, -1)
    gain_share = norm_gains.shape[2]
    conv_share = conv_state.shape[1]
    grad_gains = lax.dynamic_slice_in_dim(
        wide_small[:, : 2 * width].reshape(LAYERS, 2, width), slot * gain_share, gain_share, 2
    )
    grad_conv = lax.dynamic_slice_in_dim(wide_small[:, 2 * width :], slot * conv_share, conv_share, 1)
    grad_channel = local_small[:, : 6 * channels].reshape(LAYERS, 6, channels)
    grad_head = local_small[:, 6 * channels :].reshape(LAYERS, 3, ssm_heads)

    outs = {k: [] for k in ("q", "gate", "step", "attn", "ssm", "gu", "down", "kv", "state")}
    for layer in range(LAYERS):
        ffn_grads, mix_grads = (v.astype(F32) for v in big[layer])
        outs["gu"].append(ffn_grads[:, : 2 * hidden].reshape(depth, 2, hidden))
        outs["down"].append(ffn_grads[:, 2 * hidden :].T)
        outs["q"].append(mix_grads[:, :128])
        outs["gate"].append(mix_grads[:, 128 : 128 + 2 * channels].reshape(depth, 2, channels))
        outs["step"].append(mix_grads[:, 896 : 896 + ssm_heads])
        outs["attn"].append(mix_grads[:, 1024:1152].T)
        outs["ssm"].append(mix_grads[:, 1152:1536].T)
        sh = big[layer][1][:, 1536:]
        rows = sh.shape[0] // tp_size

        def part(distance):
            return lax.dynamic_slice_in_dim(sh, (rank ^ distance) * rows, rows, 0).astype(F32)

        sh = part(0) + sum(swap(part(d), "tensor", d) for d in (1, 2, 3))
        outs["kv"].append(sh[:, : 2 * kv_heads * HD])
        outs["state"].append(sh[:, 2 * kv_heads * HD :])
    st = {k: jnp.stack(v) for k, v in outs.items()}
    return (
        residual.astype(BF16)[None], grad[None], grad_gains, st["q"], st["kv"], st["gate"], st["state"],
        st["step"], grad_channel, grad_conv, grad_head, st["attn"], st["ssm"], st["gu"], st["down"],
    )


def solution(mesh):
    split = (
        P("dp", "tensor", None),
        P("dp", "tensor", None),
        P("dp", None),
        P(None, None, ("dp", "tensor")),
        P(None, "dp", "tensor"),
        P(None, ("dp", "tensor"), None),
        P(None, "dp", None, "tensor"),
        P(None, ("dp", "tensor"), None),
        P(None, "dp", "tensor"),
        P(None, None, "tensor"),
        P(None, ("dp", "tensor")),
        P(None, None, "tensor"),
        P(None, "tensor", "dp"),
        P(None, "tensor", "dp"),
        P(None, "dp", None, "tensor"),
        P(None, "tensor", "dp"),
    )
    out_split = split[:2] + split[3:]
    return jax.shard_map(body, mesh=mesh, in_specs=split, out_specs=out_split, check_vma=False)
```

```python
import functools

import jax
import jax.numpy as jnp
from jax import lax
from jax.experimental import pallas as pl
from jax.experimental.pallas import tpu as pltpu
from jax.sharding import PartitionSpec as P

HQ = 8
HD = 64
HS = 24
PH = 64
NS = 128
LAYERS = 2
EPS = 1e-05
ROPE_BASE = 100000000000.0
R = 128
QUARTERS = 4
DISTANCE = (1, 3, 0, 2)
F32 = jnp.float32
BF16 = jnp.bfloat16
EXACT = lax.Precision.HIGHEST
NEG = -1e30
VMEM_BYTES = 28 * 1024 * 1024


def dot_nn(left, right, **kw):
    return lax.dot_general(
        left, right, (((1,), (0,)), ((), ())), preferred_element_type=F32, **kw
    )


def dot_nt(left, right, **kw):
    return lax.dot_general(
        left, right, (((1,), (1,)), ((), ())), preferred_element_type=F32, **kw
    )


def dot_tn(left, right, **kw):
    return lax.dot_general(
        left, right, (((0,), (0,)), ((), ())), preferred_element_type=F32, **kw
    )


def iota(shape, dim):
    return lax.broadcasted_iota(jnp.int32, shape, dim)


def softplus(v):
    return jnp.maximum(v, 0.0) + jnp.log1p(jnp.exp(-jnp.abs(v)))


def partner(v, lane):
    return jnp.where(lane % HD < HD // 2, pltpu.roll(v, 96, 1), pltpu.roll(v, 32, 1))


def block_of(quarter, rank):
    k = quarter ^ rank
    return 2 - 2 * (k & 1) + (k >> 1)


def sds(shape, dtype):
    return jax.ShapeDtypeStruct(shape, dtype)


def whole(shape, *at):
    at = at or (0,) * len(shape)
    return pl.BlockSpec(shape, lambda *_: at)


SCALAR = pl.BlockSpec(memory_space=pltpu.SMEM)


def call(kernel, name, in_specs, out_shapes, flops, scratch=(), deps=()):
    if deps:
        base, skipped = kernel, range(len(in_specs), len(in_specs) + len(deps))

        def kernel(*refs):
            base(*(r for i, r in enumerate(refs) if i not in skipped))

        in_specs = list(in_specs) + [pl.BlockSpec(memory_space=pl.ANY)] * len(deps)
    many = sum(s.size * s.dtype.itemsize for s in out_shapes)
    made = pl.pallas_call(
        kernel,
        grid=(1,),
        in_specs=in_specs,
        out_specs=[whole(s.shape) for s in out_shapes],
        out_shape=out_shapes,
        scratch_shapes=list(scratch),
        compiler_params=pltpu.CompilerParams(
            dimension_semantics=("arbitrary",), vmem_limit_bytes=VMEM_BYTES
        ),
        cost_estimate=pl.CostEstimate(
            flops=int(flops), bytes_accessed=2 * many, transcendentals=10**5
        ),
        name=name,
    )
    return lambda *args: made(*args, *deps)


def rms(v, gain):
    return v * lax.rsqrt(jnp.mean(v * v, axis=-1, keepdims=True) + EPS) * gain


def rms_back(v, gain, grad):
    factor = lax.rsqrt(jnp.mean(v * v, axis=-1, keepdims=True) + EPS)
    weighted = grad * gain
    inner = jnp.mean(weighted * v, axis=-1, keepdims=True)
    scaled = v * factor
    return (
        factor * weighted - scaled * (factor * factor * inner),
        jnp.sum(grad * scaled, axis=0, keepdims=True),
    )


def step_kernel(x, keep, got, far, gain, x_o, h_o):
    total = keep[...].astype(F32) + got[...].astype(F32) + far[...].astype(F32)
    new = x[...].astype(F32) + total
    x_o[...] = new.astype(x_o.dtype)
    if h_o is not None:
        h_o[...] = rms(new, gain[0:1]).astype(BF16)


def last_kernel(x, keep, got, far, x_o):
    step_kernel(x, keep, got, far, None, x_o, None)


def take_step(x, keep, got, far, gain):
    w = x.shape[1]
    specs = [whole((R, w))] * 4
    if gain is None:
        return call(last_kernel, "last_step", specs, [sds((R, w), BF16)], 10**6)(
            x, keep, got, far
        )[0]
    return call(
        step_kernel, "step", specs + [whole((8, w))], [sds((R, w), F32), sds((R, w), BF16)], 10**6
    )(x, keep, got, far, gain)


def back_step_kernel(g, v, keep, got, far, gain, g_o, low_o, gg_o):
    grad = keep[...].astype(F32) + got[...].astype(F32) + far[...].astype(F32)
    through, gg = rms_back(v[...].astype(F32), gain[0:1], grad)
    new = g[...].astype(F32) + through
    g_o[...] = new
    low_o[...] = new.astype(BF16)
    gg_o[...] = jnp.broadcast_to(gg, gg_o.shape)


def back_step(g, v, keep, got, far, gain, deps=()):
    w = v.shape[1]
    return call(
        back_step_kernel,
        "back_step",
        [whole((R, w))] * 5 + [whole((8, w))],
        [sds((R, w), F32), sds((R, w), BF16), sds((8, w), F32)],
        10**6,
        deps=deps,
    )(g, v, keep, got, far, gain)


def input_kernel(first, depth, rank, oh, p0, p1, p2, p3, gain, w_in, *refs):
    shares, outs = refs[: len(refs) - 4], refs[len(refs) - 4 :]
    h_o, pa_o, dt_o, ps_o = outs
    if len(shares) > 1:
        *shares, w_sh = shares
        sq = depth // QUARTERS
        for distance, share in enumerate(shares):
            for dp in range(share.shape[0] // depth):
                at = pl.multiple_of(dp * depth + (rank[0] ^ distance) * sq, sq)
                for c in range(QUARTERS):
                    rows = slice(dp * depth + c * sq, dp * depth + (c + 1) * sq)
                    w_sh[pl.ds(at, sq), 128 * c : 128 * c + 128] = share[rows]
    else:
        w_sh = shares[0]
    h = jnp.concatenate([p0[...], p1[...], p2[...], p3[...]], axis=0)
    if first:
        h = rms(h.astype(F32), gain[0:1]).astype(BF16)
    h_o[...] = h
    pa = dot_nn(h, w_in[...])
    pa_o[...] = pa[:, 0:896].astype(BF16)
    dt_o[...] = pa[:, 896:1024]
    ps = dot_nn(h, w_sh[...])
    k, v = ps[:, 0:128], ps[:, 128:256]
    left = iota(k.shape, 1) < HD
    is_first = oh[0] == 0
    k = jnp.where(is_first, k, pltpu.roll(k, HD, 1))
    v = jnp.where(is_first, pltpu.roll(v, HD, 1), v)
    ps_o[:, 0:128] = jnp.where(left, k, v).astype(BF16)
    ps_o[:, 128:384] = ps[:, 256:512].astype(BF16)


def project_in(first, depth, rank, oh, pieces, gain, w_in, w_sh):
    w = pieces[0].shape[1]
    n = QUARTERS * R
    shares = w_sh if isinstance(w_sh, tuple) else (w_sh,)
    outs = [sds((n, w), BF16), sds((n, 896), BF16), sds((n, 128), F32), sds((n, 384), BF16)]
    if len(shares) > 1:
        outs = [sds((w, 512), BF16)] + outs
    return call(
        functools.partial(input_kernel, first, depth),
        "project_in",
        [SCALAR, SCALAR] + [whole((R, w))] * 4 + [whole((8, w)), whole((w, 1024))]
        + [whole(v.shape) for v in shares],
        outs,
        2 * n * w * 1536,
    )(rank, oh, *pieces, gain, w_in, *shares)


def input_back_kernel(da, ds, w_in, w_sh, send, keep):
    dh = (dot_nt(da[...], w_in[...]) + dot_nt(ds[...], w_sh[...])).astype(BF16)
    send[...] = dh[0 : 2 * R]
    keep[...] = dh[2 * R :]


def project_in_back(da, ds, w_in, w_sh, deps=()):
    n, w = da.shape[0], w_in.shape[0]
    return call(
        input_back_kernel,
        "project_in_back",
        [whole((n, 1024)), whole((n, 512)), whole((w, 1024)), whole((w, 512))],
        [sds((2 * R, w), BF16)] * 2,
        2 * n * w * 1536,
        deps=deps,
    )(da, ds, w_in, w_sh)


def column(row_ref, start):
    row = row_ref[:, pl.ds(pl.multiple_of(start, R), R)]
    return jnp.broadcast_to(row, (R, R)).T


def mix_kernel(half, rank, o, y, pa, fac, gain, w_mix, m_o, send, keep):
    m_o[:, 0:128] = o[...]
    for j in range(QUARTERS):
        rows = slice(j * R, (j + 1) * R)
        f = column(fac, half * QUARTERS * R + (rank[0] ^ DISTANCE[j]) * R)
        for p in range(3):
            z = pa[rows, 128 + 128 * p : 256 + 128 * p].astype(F32)
            u = y[rows, 128 * p : 128 * p + 128].astype(F32) * (z * jax.nn.sigmoid(z))
            m_o[rows, 128 + 128 * p : 256 + 128 * p] = (
                u * f * gain[0:1, 128 * p : 128 * p + 128]
            ).astype(BF16)
    mixed = dot_nt(m_o[...], w_mix[...]).astype(BF16)
    send[...] = mixed[0 : 2 * R]
    keep[...] = mixed[2 * R :]


def mix(half, rank, o, y, pa, fac, gain, w_mix):
    n, w = y.shape[0], w_mix.shape[0]
    return call(
        functools.partial(mix_kernel, half),
        "mix",
        [
            SCALAR, whole((n, 128)), whole((n, 384)), whole((n, 512)), whole(fac.shape),
            whole((8, 384)), whole((w, 512), 0, 2),
        ],
        [sds((n, 512), BF16), sds((2 * R, w), BF16), sds((2 * R, w), BF16)],
        2 * n * w * 512,
    )(rank, o, y, pa, fac, gain, w_mix)


def mix_back_kernel(rank, p0, p1, p2, p3, y, pa, gain, w_mix, dm_o, do_o, dyn_o, cross_o):
    dm = jnp.concatenate([p0[...], p1[...], p2[...], p3[...]], axis=0)
    dm_o[...] = dm
    d = dot_nn(dm, w_mix[...])
    do_o[...] = d[:, 0:128].astype(BF16)
    dyn_o[...] = d[:, 128:512]
    ones = jnp.ones((8, R), F32)
    for j in range(QUARTERS):
        rows = slice(j * R, (j + 1) * R)
        total = jnp.zeros((R, R), F32)
        for p in range(3):
            z = pa[rows, 128 + 128 * p : 256 + 128 * p].astype(F32)
            u = y[rows, 128 * p : 128 * p + 128].astype(F32) * (z * jax.nn.sigmoid(z))
            total = total + d[rows, 128 + 128 * p : 256 + 128 * p] * u * (
                gain[0:1, 128 * p : 128 * p + 128]
            )
        at = pl.multiple_of((rank[0] ^ DISTANCE[j]) * R, R)
        cross_o[:, pl.ds(at, R)] = dot_nt(ones, total, precision=EXACT)[0:1]


def mix_back(rank, pieces, y, pa, gain, w_mix):
    n, w = y.shape[0], w_mix.shape[0]
    return call(
        mix_back_kernel,
        "mix_back",
        [SCALAR] + [whole((R, w))] * 4
        + [whole((n, 384)), whole((n, 512)), whole((8, 384)), whole((w, 512), 0, 2)],
        [sds((n, w), BF16), sds((n, 128), BF16), sds((n, 384), F32), sds((1, n), F32)],
        2 * n * w * 512,
    )(rank, *pieces, y, pa, gain, w_mix)


def ffn_kernel(p0, p1, p2, p3, w_gu, w_dn, h_o, gu_o, act_o, send, keep):
    h = jnp.concatenate([p0[...], p1[...], p2[...], p3[...]], axis=0)
    h_o[...] = h
    gu = dot_nn(h, w_gu[...])
    gu_o[...] = gu.astype(BF16)
    g0 = gu[:, 0:512]
    act = (g0 * jax.nn.sigmoid(g0) * gu[:, 512:1024]).astype(BF16)
    act_o[...] = act
    out = dot_nt(act, w_dn[...]).astype(BF16)
    send[...] = out[0 : 2 * R]
    keep[...] = out[2 * R :]


def ffn(pieces, w_second):
    n, w = QUARTERS * R, pieces[0].shape[1]
    return call(
        ffn_kernel,
        "ffn",
        [whole((R, w))] * 4 + [whole((w, 1024)), whole((w, 512), 0, 2)],
        [
            sds((n, w), BF16), sds((n, 1024), BF16), sds((n, 512), BF16),
            sds((2 * R, w), BF16), sds((2 * R, w), BF16),
        ],
        2 * n * w * 1536,
    )(*pieces, w_second, w_second)


def ffn_back_kernel(p0, p1, p2, p3, gu, w_gu, w_dn, df_o, dgu_o, send, keep):
    df = jnp.concatenate([p0[...], p1[...], p2[...], p3[...]], axis=0)
    df_o[...] = df
    da = dot_nn(df, w_dn[...])
    g0, g1 = gu[:, 0:512].astype(F32), gu[:, 512:1024].astype(F32)
    sg = jax.nn.sigmoid(g0)
    dgu_o[:, 0:512] = (da * g1 * sg * (1.0 + g0 * (1.0 - sg))).astype(BF16)
    dgu_o[:, 512:1024] = (da * g0 * sg).astype(BF16)
    out = dot_nt(dgu_o[...], w_gu[...]).astype(BF16)
    send[...] = out[0 : 2 * R]
    keep[...] = out[2 * R :]


def ffn_back(pieces, gu, w_second, deps=()):
    n, w = QUARTERS * R, pieces[0].shape[1]
    return call(
        ffn_back_kernel,
        "ffn_back",
        [whole((R, w))] * 4 + [whole((n, 1024)), whole((w, 1024)), whole((w, 512), 0, 2)],
        [sds((n, w), BF16), sds((n, 1024), BF16), sds((2 * R, w), BF16), sds((2 * R, w), BF16)],
        2 * n * w * 1536,
        deps=deps,
    )(*pieces, gu, w_second, w_second)


def weight_grad_kernel(widths, *refs):
    out = refs[-1]
    at = 0
    for i, width in enumerate(widths):
        la, lb, ra, rb = refs[4 * i : 4 * i + 4]
        g = dot_tn(la[...], ra[...]) + dot_tn(lb[...], rb[...])
        out[:, at : at + width] = g.astype(BF16)
        at += width


def weight_grads(name, groups, deps=()):
    n, w = groups[0][0][0].shape
    widths = [right[0].shape[1] for _, right in groups]
    specs, args = [], []
    for (la, lb), (ra, rb) in groups:
        specs += [whole(la.shape)] * 2 + [whole(ra.shape)] * 2
        args += [la, lb, ra, rb]
    return call(
        functools.partial(weight_grad_kernel, widths),
        name,
        specs,
        [sds((w, sum(widths)), BF16)],
        4 * n * w * sum(widths),
        deps=deps,
    )(*args)[0]


def chunk_terms(act, raw_step, tok, seg_row, par):
    row, lane = iota((R, R), 0), iota((R, R), 1)
    b, c = act[:, 384:512], act[:, 512:640]
    bb, cb = b.astype(BF16), c.astype(BF16)
    dt = softplus(raw_step + par[1:2])
    tri = (row >= lane).astype(F32)
    cum = dot_nn(tri, dt * par[0:1], precision=EXACT)
    last = cum[R - 1 : R]
    okay = (row >= lane) & (tok[:, 5:6] == seg_row)
    inner = jnp.where(okay, dot_nt(cb, bb), 0.0)
    enter = jnp.exp(cum) * tok[:, 3:4]
    tail = jnp.exp(jnp.minimum(last - cum, 0.0)) * tok[:, 4:5]
    return b, c, bb, cb, dt, cum, cum.T, dt.T, okay, inner, enter, tail


def ssm_fwd_chunk(pa, raw, ps, tok, seg_row, cos, sin, taps, par, skip, y_o, pre_o, st_o, q_o, kv_o, state, hist):
    lane = iota((R, R), 1)
    half = lane < PH
    xin = jnp.concatenate([pa[:, 512:896], ps[:, 128:384]], axis=1).astype(F32)
    ext = jnp.concatenate([hist[...], xin], axis=0)
    hist[...] = xin[R - 8 :]
    pre = taps[4:5] + xin * taps[3:4]
    for k in (1, 2, 3):
        pre = pre + ext[8 - k : 8 - k + R] * tok[:, k - 1 : k] * taps[3 - k : 4 - k]
    pre_o[...] = pre.astype(BF16)
    act = pre * jax.nn.sigmoid(pre)
    b, c, bb, cb, dt, cum, cum_t, dt_t, okay, inner, enter, tail = chunk_terms(
        act, raw[...], tok, seg_row, par
    )
    tail = tail * dt
    keep = enter[R - 1 : R]
    b_t = b.T.astype(BF16)
    squares = jnp.zeros((R, R), F32)
    for p in range(3):
        h0, h1 = 2 * p, 2 * p + 1
        cols = slice(128 * p, 128 * p + 128)
        xp = act[:, cols]
        xb = xp.astype(BF16)
        sp = state[:, cols]
        st_o[:, cols] = sp.astype(BF16)

        def weights(h):
            gap = jnp.minimum(cum[:, h : h + 1] - cum_t[h : h + 1], 0.0)
            return (inner * jnp.exp(gap) * dt_t[h : h + 1]).astype(BF16)

        y = jnp.where(half, dot_nn(weights(h0), xb), dot_nn(weights(h1), xb))
        y = y + dot_nn(cb, sp.astype(BF16)) * jnp.where(
            half, enter[:, h0 : h0 + 1], enter[:, h1 : h1 + 1]
        )
        y = y + skip[0:1, cols] * xp
        y_o[:, cols] = y.astype(BF16)
        tp = jnp.where(half, tail[:, h0 : h0 + 1], tail[:, h1 : h1 + 1])
        kp = jnp.where(half[0:1], keep[:, h0 : h0 + 1], keep[:, h1 : h1 + 1])
        state[:, cols] = kp * sp + dot_nn(b_t, (tp * xp).astype(BF16))
        z = pa[:, 128 + 128 * p : 256 + 128 * p].astype(F32)
        u = y * z * jax.nn.sigmoid(z)
        squares = squares + u * u
    q = pa[:, 0:128].astype(F32)
    q_o[...] = (q * cos + partner(q, lane) * sin).astype(BF16)
    kv = ps[:, 0:128].astype(F32)
    kv_o[...] = jnp.where(half, kv * cos + partner(kv, lane) * sin, kv).astype(BF16)
    return dot_nt(jnp.ones((8, R), F32), squares, precision=EXACT)[0:1]


def ssm_fwd_kernel(
    rank, pa0, pa1, raw0, raw1, ps0, ps1, tok_r, seg_r, cos_r, sin_r, taps, par, skip,
    y0, y1, pre0, pre1, st_o, sq_o, q_o, kv_o, state, hist,
):
    i = pl.program_id(0)

    @pl.when(i == 0)
    def _():
        state[...] = jnp.zeros_like(state)
        hist[...] = jnp.zeros_like(hist)

    halves = ((pa0, raw0, ps0, y0, pre0), (pa1, raw1, ps1, y1, pre1))
    for half, (pa, raw, ps, y_o, pre_o) in enumerate(halves):
        rows = slice(half * R, (half + 1) * R)
        at = pl.multiple_of(half * QUARTERS * R + i * R, R)
        sq_o[:, pl.ds(at, R)] = ssm_fwd_chunk(
            pa, raw, ps, tok_r[rows], seg_r[0:1, rows], cos_r[rows], sin_r[rows], taps, par, skip,
            y_o, pre_o, st_o.at[half], q_o.at[rows], kv_o.at[rows], state, hist,
        )


def wire(width, reverse=False):
    def at(i, rank):
        i = QUARTERS - 1 - i if reverse else i
        return (block_of(i, rank[0]), 0)

    return pl.BlockSpec((R, width), at)


def in_order(shape, dim=0, reverse=False):
    def at(i, rank):
        i = QUARTERS - 1 - i if reverse else i
        return tuple(i if d == dim else 0 for d in range(len(shape)))

    return pl.BlockSpec(shape, at)


def ssm_forward(rank, pa, raw, ps, tok, seg_rows, cos, sin, taps, par, skip):
    n = QUARTERS * R
    t = 2 * n
    return pl.pallas_call(
        ssm_fwd_kernel,
        grid_spec=pltpu.PrefetchScalarGridSpec(
            num_scalar_prefetch=1,
            grid=(QUARTERS,),
            in_specs=[
                wire(896), wire(896), wire(128), wire(128), wire(384), wire(384),
                in_order((2 * R, 8)), in_order((8, 2 * R), 1),
                in_order((2 * R, 128)), in_order((2 * R, 128)), whole((8, 640)), whole((8, 128)), whole((8, 384)),
            ],
            out_specs=[
                wire(384), wire(384), wire(640), wire(640), in_order((2, NS, 384)), whole((1, t)),
                in_order((2 * R, 128)), in_order((2 * R, 128)),
            ],
            scratch_shapes=[pltpu.VMEM((NS, 384), F32), pltpu.VMEM((8, 640), F32)],
        ),
        out_shape=[
            sds((n, 384), BF16), sds((n, 384), BF16), sds((n, 640), BF16), sds((n, 640), BF16),
            sds((2 * QUARTERS, NS, 384), BF16), sds((1, t), F32), sds((t, 128), BF16), sds((t, 128), BF16),
        ],
        compiler_params=pltpu.CompilerParams(
            dimension_semantics=("arbitrary",), vmem_limit_bytes=VMEM_BYTES
        ),
        cost_estimate=pl.CostEstimate(
            flops=4 * 10**9, bytes_accessed=20 * 2**20, transcendentals=3 * 10**6
        ),
        name="ssm_forward",
    )(rank, *pa, *raw, *ps, tok, seg_rows, cos, sin, taps, par, skip)


def ssm_bwd_chunk(
    pa, raw, ps, pre_r, y_r, st_r, dyn_r, r2, coef, dq, dkv, tok, seg_row, taps, par, skip, gain,
    da_o, ds_o, gt_o, gc_o, gh_o, dstate, nxt, own_first,
):
    row, lane = iota((R, R), 0), iota((R, R), 1)
    half = lane < PH
    sub = iota((8, R), 0)
    pre = pre_r[...].astype(F32)
    sg = jax.nn.sigmoid(pre)
    act = pre * sg
    b, c, bb, cb, dt, cum, cum_t, dt_t, okay, inner, enter, tail = chunk_terms(
        act, raw[...], tok, seg_row, par
    )
    tail_dt = tail * dt
    keep = enter[R - 1 : R]
    c_t = c.T.astype(BF16)
    db = jnp.zeros((R, R), F32)
    dc = jnp.zeros((R, R), F32)
    dinner = jnp.zeros((R, R), F32)
    dcum = jnp.zeros((R, R), F32)
    extra = jnp.zeros((R, R), F32)
    col_sum = jnp.zeros((8, R), F32)
    last_row = jnp.zeros((1, R), F32)
    dx_parts = []
    for p in range(3):
        cols = slice(128 * p, 128 * p + 128)
        z = pa[:, 128 + 128 * p : 256 + 128 * p].astype(F32)
        y, dyn = y_r[:, cols].astype(F32), dyn_r[:, cols]
        zs = jax.nn.sigmoid(z)
        sz = z * zs
        u = y * sz
        dn = dyn * r2
        gc_o[0:1, cols] += jnp.sum(dn * u, axis=0, keepdims=True)
        du = gain[0:1, cols] * dn - u * coef
        da_o[:, 128 + 128 * p : 256 + 128 * p] = (
            du * y * zs * (1.0 + z * (1.0 - zs))
        ).astype(BF16)
        dy = du * sz
        dyb = dy.astype(BF16)
        xp = act[:, cols]
        xb = xp.astype(BF16)
        gc_o[1:2, cols] += jnp.sum(dy * xp, axis=0, keepdims=True)
        sb = st_r[:, cols]
        sp = sb.astype(F32)
        dsp = dstate[:, cols]
        dsb = dsp.astype(BF16)
        h0, h1 = 2 * p, 2 * p + 1
        ep = jnp.where(half, enter[:, h0 : h0 + 1], enter[:, h1 : h1 + 1])
        tp = jnp.where(half, tail_dt[:, h0 : h0 + 1], tail_dt[:, h1 : h1 + 1])
        kp = jnp.where(half[0:1], keep[:, h0 : h0 + 1], keep[:, h1 : h1 + 1])
        cdb = (ep * dy).astype(BF16)
        through = dy * ep * dot_nn(cb, sb)
        bds = dot_nn(bb, dsb)
        qx = xp * bds
        kept = jnp.sum(dsp * sp, axis=0, keepdims=True) * kp
        dxi = []
        for h in (h0, h1):
            mine = half if h == h0 else ~half
            gap = jnp.minimum(cum[:, h : h + 1] - cum_t[h : h + 1], 0.0)
            decay = jnp.where(okay, jnp.exp(gap), 0.0)
            dt_row = dt_t[h : h + 1]
            dg = dot_nt(jnp.where(mine, dy, 0.0).astype(BF16), xb)
            t1 = dg * decay
            dinner = dinner + t1 * dt_row
            w0 = t1 * inner
            col_sum = col_sum + jnp.where(sub == h, jnp.sum(w0, axis=0, keepdims=True), 0.0)
            w1 = w0 * dt_row + jnp.where(mine, through, 0.0)
            dcum = dcum + jnp.where(lane == h, jnp.sum(w1, axis=1, keepdims=True), 0.0)
            e = jnp.sum(jnp.where(mine, qx, 0.0), axis=1, keepdims=True)
            extra = extra + jnp.where(lane == h, e, 0.0)
            k = jnp.sum(jnp.where(mine[0:1], kept, 0.0), axis=1, keepdims=True)
            last_row = last_row + jnp.where(lane[0:1] == h, k, 0.0)
            dxi.append(dot_tn((decay * inner * dt_row).astype(BF16), dyb))
        dx_parts.append(jnp.where(half, dxi[0], dxi[1]) + tp * bds + skip[0:1, cols] * dy)
        dc = dc + dot_nt(cdb, sb)
        db = db + dot_nt((tp * xp).astype(BF16), dsb)
        dstate[:, cols] = kp * dsp + dot_nn(c_t, cdb)
    col_sum = jnp.concatenate([col_sum, jnp.zeros((R - 8, R), F32)], axis=0).T
    moved = tail_dt * extra
    last_row = last_row + jnp.sum(moved, axis=0, keepdims=True)
    dcum = dcum - col_sum * dt - moved + jnp.where(row == R - 1, last_row, 0.0)
    dlog = dot_nn((row <= lane).astype(F32), dcum, precision=EXACT)
    ddt = col_sum + tail * extra + par[0:1] * dlog
    gh_o[0:1] += jnp.sum(dt * dlog, axis=0, keepdims=True)
    ddr = ddt * jax.nn.sigmoid(raw[...] + par[1:2])
    gh_o[1:2] += jnp.sum(ddr, axis=0, keepdims=True)
    da_o[:, 896:1024] = ddr.astype(BF16)
    dib = dinner.astype(BF16)
    dc = dc + dot_nn(dib, bb)
    db = db + dot_tn(dib, cb)
    dact = jnp.concatenate([*dx_parts, db, dc], axis=1)
    dpre = dact * sg * (1.0 + pre * (1.0 - sg))
    xin = jnp.concatenate([pa[:, 512:896], ps[:, 128:384]], axis=1).astype(F32)
    dxin = dpre * taps[3:4]
    gt_o[3:4] += jnp.sum(dpre * xin, axis=0, keepdims=True)
    gt_o[4:5] += jnp.sum(dpre, axis=0, keepdims=True)
    for k in (1, 2, 3):
        zk = dpre * tok[:, k - 1 : k]
        later = nxt.at[k - 1]
        moved_up = jnp.concatenate([zk, later[...]], axis=0)[k : k + R]
        later[...] = zk[0:8]
        dxin = dxin + moved_up * taps[3 - k : 4 - k]
        gt_o[3 - k : 4 - k] += jnp.sum(moved_up * xin, axis=0, keepdims=True)
    da_o[:, 512:896] = dxin[:, 0:384].astype(BF16)
    ds_o[:, 256:512] = dxin[:, 384:640].astype(BF16)
    da_o[:, 0:128] = dq
    other = pltpu.roll(dkv, HD, 1)
    mine = half == own_first
    ds_o[:, 0:128] = jnp.where(mine, jnp.where(half, dkv, other), 0.0).astype(BF16)
    ds_o[:, 128:256] = jnp.where(mine, jnp.where(half, other, dkv), 0.0).astype(BF16)


def ssm_bwd_kernel(
    rank, oh, pa0, pa1, raw0, raw1, ps0, ps1, pre0, pre1, y0, y1, st_r, dyn0, dyn1, fac_r, coef_r, dq_r, dkv_r,
    tok_r, seg_r, taps, par, skip, gain,
    da0, da1, ds0, ds1, gt_o, gc_o, gh_o, dstate, nxt,
):
    i = pl.program_id(0)

    @pl.when(i == 0)
    def _():
        dstate[...] = jnp.zeros_like(dstate)
        nxt[...] = jnp.zeros_like(nxt)
        gt_o[...] = jnp.zeros_like(gt_o)
        gc_o[...] = jnp.zeros_like(gc_o)
        gh_o[...] = jnp.zeros_like(gh_o)

    quarter = QUARTERS - 1 - i
    halves = (
        (pa0, raw0, ps0, pre0, y0, dyn0, da0, ds0),
        (pa1, raw1, ps1, pre1, y1, dyn1, da1, ds1),
    )
    for half in (1, 0):
        pa, raw, ps, pre, y, dyn, da, ds = halves[half]
        rows = slice(half * R, (half + 1) * R)
        start = half * QUARTERS * R + quarter * R
        ssm_bwd_chunk(
            pa, raw, ps, pre, y, st_r.at[half], dyn, column(fac_r, start), column(coef_r, start),
            dq_r[rows], dkv_r[rows].astype(F32), tok_r[rows], seg_r[0:1, rows], taps, par, skip, gain,
            da, ds, gt_o, gc_o, gh_o, dstate, nxt, oh[0] == 0,
        )


def ssm_backward(
    rank, oh, pa, raw, ps, pre, y, states, dyn, fac, coef, dq, dkv, tok, seg_rows, taps, par, skip, gain
):
    n = QUARTERS * R
    t = 2 * n
    back = {"reverse": True}
    return pl.pallas_call(
        lambda r, *refs: ssm_bwd_kernel(r, *refs),
        grid_spec=pltpu.PrefetchScalarGridSpec(
            num_scalar_prefetch=1,
            grid=(QUARTERS,),
            in_specs=[
                SCALAR, wire(896, **back), wire(896, **back), wire(128, **back), wire(128, **back),
                wire(384, **back), wire(384, **back),
                wire(640, **back), wire(640, **back), wire(384, **back), wire(384, **back),
                in_order((2, NS, 384), **back), wire(384, **back), wire(384, **back),
                whole((1, t)), whole((1, t)), in_order((2 * R, 128), **back), in_order((2 * R, 128), **back),
                in_order((2 * R, 8), **back), in_order((8, 2 * R), 1, **back),
                whole((8, 640)), whole((8, 128)), whole((8, 384)), whole((8, 384)),
            ],
            out_specs=[
                wire(1024, **back), wire(1024, **back), wire(512, **back), wire(512, **back),
                whole((8, 640)), whole((8, 384)), whole((8, 128)),
            ],
            scratch_shapes=[pltpu.VMEM((NS, 384), F32), pltpu.VMEM((3, 8, 640), F32)],
        ),
        out_shape=[
            sds((n, 1024), BF16), sds((n, 1024), BF16), sds((n, 512), BF16), sds((n, 512), BF16),
            sds((8, 640), F32), sds((8, 384), F32), sds((8, 128), F32),
        ],
        compiler_params=pltpu.CompilerParams(
            dimension_semantics=("arbitrary",), vmem_limit_bytes=VMEM_BYTES
        ),
        cost_estimate=pl.CostEstimate(
            flops=8 * 10**9, bytes_accessed=30 * 2**20, transcendentals=4 * 10**6
        ),
        name="ssm_backward",
    )(
        rank, oh, *pa, *raw, *ps, *pre, *y, states, *dyn, fac, coef, dq, dkv, tok, seg_rows, taps, par, skip, gain
    )


def head_views(kv, lane):
    zero = jnp.zeros_like(kv)
    left = lane < HD
    k0 = jnp.where(left, kv, zero)
    v1 = jnp.where(left, zero, kv)
    k1 = pltpu.roll(k0.astype(F32), HD, 1).astype(BF16)
    v0 = pltpu.roll(v1.astype(F32), HD, 1).astype(BF16)
    return (k0, k1), (v0, v1)


def allowed_keys(tok_r, seg_r, start, rows, keys):
    return (iota((rows, keys), 1) <= start + iota((rows, keys), 0)) & (
        tok_r[start : start + rows, 5:6] == seg_r[0:1, 0:keys]
    )


def attend_fwd_kernel(rank, q_r, kv_r, tok_r, seg_r, o0, o1, lse_o):
    n = q_r.shape[0]
    ks, vs = head_views(kv_r[...], iota((n, 2 * HD), 1))
    lane = iota((2 * R, 128), 1)
    for quarter in range(QUARTERS):
        start, keys = quarter * 2 * R, (quarter + 1) * 2 * R
        q = q_r[start:keys]
        okay = allowed_keys(tok_r, seg_r, start, 2 * R, keys)
        out = jnp.zeros((2 * R, 2 * HD), F32)
        stats = []
        for h in range(2):
            s = jnp.where(okay, dot_nt(q, ks[h][0:keys]) * HD**-0.5, NEG)
            top = jnp.max(s, axis=1, keepdims=True)
            e = jnp.exp(s - top)
            total = jnp.sum(e, axis=1, keepdims=True)
            out = out + dot_nn((e * (1.0 / total)).astype(BF16), vs[h][0:keys])
            stats.append(top + jnp.log(total))
        at = pl.ds(pl.multiple_of(block_of(quarter, rank[0]) * R, R), R)
        o0[at] = out[0:R].astype(BF16)
        o1[at] = out[R:].astype(BF16)
        lse_o[start:keys] = jnp.where(lane == 0, stats[0], stats[1])


def attend_bwd_kernel(
    rank, q_r, kv_r, do0, do1, lse_r, tok_r, seg_r, cos_r, sin_r, dq_o, dkv_o, dk_acc, dv_acc
):
    n = q_r.shape[0]
    ks, vs = head_views(kv_r[...], iota((n, 2 * HD), 1))
    lane = iota((2 * R, 128), 1)
    left = lane < HD
    dk_acc[...] = jnp.zeros_like(dk_acc)
    dv_acc[...] = jnp.zeros_like(dv_acc)
    for quarter in range(QUARTERS):
        start, keys = quarter * 2 * R, (quarter + 1) * 2 * R
        q = q_r[start:keys]
        at = pl.ds(pl.multiple_of(block_of(quarter, rank[0]) * R, R), R)
        do = jnp.concatenate([do0[at], do1[at]], axis=0)
        okay = allowed_keys(tok_r, seg_r, start, 2 * R, keys)
        lse = lse_r[start:keys]
        zero = jnp.zeros_like(q)
        dq = jnp.zeros((2 * R, 2 * HD), F32)
        for h in range(2):
            mine = left if h == 0 else ~left
            s = dot_nt(q, ks[h][0:keys]) * HD**-0.5
            p = jnp.where(okay, jnp.exp(s - lse[:, h : h + 1]), 0.0)
            dp = dot_nt(do, vs[h][0:keys])
            dot_sum = jnp.sum(p * dp, axis=1, keepdims=True)
            ds = (p * (dp - dot_sum)).astype(BF16)
            dq = dq + dot_nn(ds, ks[h][0:keys])
            dk_acc[0:keys] += dot_tn(ds, jnp.where(mine, q, zero))
            dv_acc[0:keys] += dot_tn(p.astype(BF16), jnp.where(mine, do, zero))
        dq = dq * HD**-0.5
        dq_o[start:keys] = (
            dq * cos_r[start:keys] - partner(dq, lane) * sin_r[start:keys]
        ).astype(BF16)
    for start in range(0, n, 2 * R):
        rows = slice(start, start + 2 * R)
        dk, dv = dk_acc[rows], dv_acc[rows]
        dk = (dk + pltpu.roll(dk, HD, 1)) * HD**-0.5
        dv = dv + pltpu.roll(dv, HD, 1)
        dk = dk * cos_r[rows] - partner(dk, lane) * sin_r[rows]
        dkv_o[rows] = jnp.where(left, dk, dv).astype(BF16)


def attend_forward(rank, q, kv, tok, seg_rows):
    t = q.shape[0]
    return call(
        attend_fwd_kernel,
        "attend_forward",
        [SCALAR, whole((t, 128)), whole((t, 128)), whole((t, 8)), whole((8, t))],
        [sds((t // 2, 128), BF16), sds((t // 2, 128), BF16), sds((t, 128), F32)],
        2 * 10**9,
    )(rank, q, kv, tok, seg_rows)


def attend_backward(rank, q, kv, do, lse, tok, seg_rows, cos, sin, deps=()):
    t = q.shape[0]
    full = whole((t, 128))
    return call(
        attend_bwd_kernel,
        "attend_backward",
        [SCALAR, full, full, whole((t // 2, 128)), whole((t // 2, 128)), full,
         whole((t, 8)), whole((8, t)), full, full],
        [sds((t, 128), BF16), sds((t, 128), BF16)],
        4 * 10**9,
        [pltpu.VMEM((t, 128), F32), pltpu.VMEM((t, 128), F32)],
        deps,
    )(rank, q, kv, *do, lse, tok, seg_rows, cos, sin)


def swap(values, axis, distance):
    size = lax.axis_size(axis)
    return lax.ppermute(values, axis, [(i, i ^ distance) for i in range(size)])


def bits_of(axis):
    size = lax.axis_size(axis)
    return [1 << b for b in range(size.bit_length() - 1)]


def sum_over(values, axes):
    for axis in axes:
        for bit in bits_of(axis):
            values = values + swap(values, axis, bit)
    return values


def sum_rows(values):
    return values + sum(swap(values, "tensor", d) for d in (1, 2, 3))


def gather_half(own):
    far = swap(own, "tensor", 2)
    near = swap(own, "tensor", 1)
    return near, swap(far, "tensor", 1), own, far


def scatter_half(send, keep):
    got = swap(send, "tensor", 1)
    far = swap((keep[R:].astype(F32) + got[R:].astype(F32)).astype(BF16), "tensor", 2)
    return keep, got, far


def gather_everywhere(own):
    held = own[:, None]
    for axis in ("dp", "tensor"):
        place = lax.axis_index(axis)
        for bit in bits_of(axis):
            upper = (place & bit) != 0
            other = swap(held, axis, bit)
            low, high = jnp.where(upper, other, held), jnp.where(upper, held, other)
            held = jnp.concatenate([low, high], axis=0 if axis == "dp" else 1)
    return held.reshape(-1, *own.shape[1:])


def gather_dp(v):
    return lax.all_gather(v, "dp", axis=0, tiled=True)


def scatter_dp(v):
    return lax.psum_scatter(v, "dp", scatter_dimension=0, tiled=True)


def pad_rows(v, rows=8):
    return jnp.pad(v, ((0, rows - v.shape[0]), (0, 0)))


def body(
    inputs, cotangent, segment_ids, norm_gains, w_query, key_value_weight, w_gate_in, w_state_in,
    w_step, ssm_channel, conv_state, head_params, w_attn_out, w_ssm_out, w_gate_up, w_down,
):
    width = inputs.shape[2]
    n = segment_ids.shape[1]
    tp_size = lax.axis_size("tensor")
    tensor = lax.axis_index("tensor")
    slot = lax.axis_index("dp") * tp_size + tensor
    kv_cols = key_value_weight.shape[2]
    kv_heads = kv_cols // (2 * HD)
    own_head = tensor * (w_query.shape[2] // HD) // (HQ // kv_heads)
    ssm_heads = w_step.shape[2]
    channels = ssm_heads * PH
    hidden = w_gate_up.shape[3]
    depth = w_query.shape[1]
    rank = tensor.reshape(1).astype(jnp.int32)
    oh = own_head.reshape(1).astype(jnp.int32)

    halves = [inputs[0, :R], inputs[0, R:]]
    x_pieces = [gather_half(v) for v in halves]

    shared = jnp.concatenate([key_value_weight, w_state_in], axis=2)
    sq, wide = shared.shape[1:]
    shares = [
        shared[layer].reshape(sq, wide // 128, 128).swapaxes(0, 1).reshape(depth, 128)
        for layer in range(LAYERS)
    ]

    def exchange(share):
        far = swap(share, "tensor", 2)
        return share, swap(share, "tensor", 1), far, swap(far, "tensor", 1)

    w_first, w_second, w_shared = [], [], []
    for layer in range(LAYERS):
        first = [
            w_query[layer],
            w_gate_in[layer].reshape(depth, 2 * channels),
            jnp.pad(w_step[layer], ((0, 0), (0, 128 - ssm_heads))),
            w_attn_out[layer].T,
            w_ssm_out[layer].T,
        ]
        second = [w_gate_up[layer].reshape(depth, 2 * hidden), w_down[layer].T]
        first = gather_dp(jnp.concatenate(first + (shares if layer == 0 else []), axis=1))
        if layer == 0:
            w_shared = [exchange(first[:, c : c + 128]) for c in range(1536, 1536 + 128 * LAYERS, 128)]
        w_first.append(first)
        w_second.append(gather_dp(jnp.concatenate(second, axis=1)))

    small = jnp.concatenate([norm_gains.reshape(-1), conv_state.reshape(-1)])[None, :]
    small_all = gather_everywhere(small).astype(F32)
    gain_count = norm_gains.size
    gains = (
        small_all[:, :gain_count]
        .reshape(-1, LAYERS, 2, norm_gains.shape[2])
        .transpose(1, 2, 0, 3)
        .reshape(LAYERS, 2, width)
    )
    conv_flat = (
        small_all[:, gain_count : gain_count + conv_state.size]
        .reshape(-1, LAYERS, conv_state.shape[1])
        .transpose(1, 0, 2)
        .reshape(LAYERS, 5, 2 * NS)
    )

    seg = segment_ids[0]
    segf = seg.astype(F32)
    index = jnp.arange(n, dtype=jnp.int32)
    places = index - jnp.sum((seg[None, :] < seg[:, None]).astype(jnp.int32), axis=1)
    freq = ROPE_BASE ** (-jnp.arange(HD // 2, dtype=F32) / (HD // 2))
    angle = places.astype(F32)[:, None] * freq[None, :]
    cos_one, sin_one = jnp.cos(angle), jnp.sin(angle)
    cos = jnp.concatenate([cos_one] * 4, axis=1)
    sin = jnp.concatenate([-sin_one, sin_one] * 2, axis=1)
    shifted = [
        (jnp.pad(seg, (k, 0), constant_values=-1)[:n] == seg).astype(F32) for k in (1, 2, 3)
    ]
    ends = seg.reshape(-1, R)[:, -1]
    before = jnp.concatenate([jnp.full((1,), -1, jnp.int32), ends[:-1]])
    enters = (seg.reshape(-1, R) == before[:, None]).astype(F32).reshape(-1)
    leaves = (seg.reshape(-1, R) == ends[:, None]).astype(F32).reshape(-1)
    tok = jnp.stack([*shifted, enters, leaves, segf, segf, segf], axis=1)
    seg_rows = jnp.broadcast_to(segf[None, :], (8, n))

    residual = halves
    pieces = x_pieces
    saved = []
    for layer in range(LAYERS):
        channel, head = ssm_channel[layer], head_params[layer]
        taps = pad_rows(jnp.concatenate([channel[:5], conv_flat[layer]], axis=1))
        rate = -jnp.exp(head[0])
        par = pad_rows(jnp.pad(jnp.stack([rate, head[1]]), ((0, 0), (0, 128 - ssm_heads))))
        skip = pad_rows(jnp.repeat(head[2], PH)[None, :])
        gain_row = pad_rows(channel[5:6])
        gain_one = pad_rows(gains[layer, 0:1])
        gain_two = pad_rows(gains[layer, 1:2])
        wf, ws, wh = w_first[layer], w_second[layer], w_shared[layer]
        ins = functools.partial(project_in, layer == 0, depth, rank, oh)
        w_all, *half_0 = ins(pieces[0], gain_one, wf, wh)
        w_shared[layer] = w_all
        h, pa, raw, ps = zip(half_0, ins(pieces[1], gain_one, wf, w_all))
        y0, y1, pre0, pre1, states, sq, q_rot, kv_rot = ssm_forward(
            rank, pa, raw, ps, tok, seg_rows, cos, sin, taps, par, skip
        )
        y, pre = (y0, y1), (pre0, pre1)
        total = sum_rows(sq)
        o0, o1, lse = attend_forward(rank, q_rot, kv_rot, tok, seg_rows)
        factor = lax.rsqrt(total / (HS * PH) + EPS)
        mixed, middle, h2, gu, act, result, pieces = [], [], [], [], [], [], []
        parts = []
        for i, o in enumerate((o0, o1)):
            m, send, keep = mix(i, rank, o, y[i], pa[i], factor, gain_row, wf)
            mixed.append(m)
            parts.append(scatter_half(send, keep))
        gathered = []
        for i in range(2):
            x1, low = take_step(residual[i], *parts[i], gain_two)
            middle.append(x1)
            gathered.append(gather_half(low))
        parts = []
        for i in range(2):
            h2_i, gu_i, act_i, send, keep = ffn(gathered[i], ws)
            h2.append(h2_i)
            gu.append(gu_i)
            act.append(act_i)
            parts.append(scatter_half(send, keep))
        for i in range(2):
            if layer + 1 < LAYERS:
                x2, low = take_step(middle[i], *parts[i], pad_rows(gains[layer + 1, 0:1]))
                result.append(x2)
                pieces.append(gather_half(low))
            else:
                result.append(take_step(middle[i], *parts[i], None))
        saved.append(
            (residual, middle, h, pa, raw, ps, y, pre, states, q_rot, kv_rot, lse, factor, mixed, h2, gu, act,
             taps, par, skip, gain_row, gain_one, gain_two, rate)
        )
        residual = result
    output = jnp.concatenate(residual, axis=0)

    grad = [cotangent[0, :R], cotangent[0, R:]]
    low = list(grad)
    big, small_grads = [None] * LAYERS, [None] * LAYERS
    for layer in reversed(range(LAYERS)):
        (first_in, middle, h, pa, raw, ps, y, pre, states, q_rot, kv_rot, lse, factor, mixed, h2, gu, act,
         taps, par, skip, gain_row, gain_one, gain_two, rate) = saved[layer]
        wf, ws, wh = w_first[layer], w_second[layer], w_shared[layer]
        gathered = [gather_half(v) for v in low]
        df, dgu, dm, do, dyn, cross, parts = [], [], [], [], [], [], []
        deps = (big[layer + 1][0],) if layer + 1 < LAYERS else ()
        for i in range(2):
            df_i, dgu_i, send, keep = ffn_back(gathered[i], gu[i], ws, deps)
            df.append(df_i)
            dgu.append(dgu_i)
            parts.append(scatter_half(send, keep))
        g1 = weight_grads("grads_one", [(h2, dgu), (df, act)])
        gathered, dx1, dgain2, dgain1 = [], [], 0.0, 0.0
        for i in range(2):
            dx, low_i, gg = back_step(grad[i], middle[i], *parts[i], gain_two, () if i else (g1,))
            dx1.append(dx)
            dgain2 = dgain2 + gg[0]
            gathered.append(gather_half(low_i))
        for i in range(2):
            dm_i, do_i, dyn_i, cross_i = mix_back(rank, gathered[i], y[i], pa[i], gain_row, wf)
            dm.append(dm_i)
            do.append(do_i)
            dyn.append(dyn_i)
            cross.append(cross_i)
        cross = sum_rows(jnp.concatenate(cross, axis=1))
        dq, dkv = attend_backward(
            rank, q_rot, kv_rot, do, lse, tok, seg_rows, cos, sin
        )
        coef = factor**3 * cross / (HS * PH)
        da0, da1, ds0, ds1, g_taps, g_chan, g_head = ssm_backward(
            rank, oh, pa, raw, ps, pre, y, states, dyn, factor, coef, dq, dkv, tok, seg_rows, taps, par, skip,
            gain_row,
        )
        groups = [(h, (da0, da1)), (h, (ds0, ds1)), (dm, mixed)]
        deps = ()
        if layer == 0:
            g2 = weight_grads("grads_two", groups, (big[layer + 1][1],))
            deps = (g2,)
        sums = [project_in_back(da, ds, wf, wh, deps) for da, ds in ((da0, ds0), (da1, ds1))]
        parts = [scatter_half(*v) for v in sums]
        deps = ()
        if layer > 0:
            g2 = weight_grads("grads_two", groups, (sums[0][0], sums[1][0]))
            deps = (g2,)
        grad, low = [], []
        for i in range(2):
            g, low_i, gg = back_step(dx1[i], first_in[i], *parts[i], gain_one, () if i else deps)
            grad.append(g)
            low.append(low_i)
            dgain1 = dgain1 + gg[0]
        chan_grad = jnp.concatenate([g_taps[:5, :channels], g_chan[0:1]], axis=0)
        head_grad = jnp.stack(
            [
                g_head[0, :ssm_heads] * rate,
                g_head[1, :ssm_heads],
                jnp.sum(g_chan[1].reshape(ssm_heads, PH), axis=1),
            ]
        )
        big[layer] = (scatter_dp(g1), scatter_dp(g2))
        small_grads[layer] = (
            jnp.concatenate([dgain1, dgain2, g_taps[:5, channels:].reshape(-1)]),
            jnp.concatenate([chan_grad.reshape(-1), head_grad.reshape(-1)]),
        )
    input_grad = jnp.concatenate(grad, axis=0)

    wide_small = jnp.concatenate([small_grads[l][0] for l in range(LAYERS)])
    local_small = jnp.concatenate([small_grads[l][1] for l in range(LAYERS)])
    total = sum_over(jnp.concatenate([wide_small, local_small])[None, :], ("dp",))[0]
    wide_small = sum_over(total[None, : wide_small.shape[0]], ("tensor",))[0]
    wide_small = wide_small.reshape(LAYERS, -1)
    local_small = total[wide_small.size :].reshape(LAYERS, -1)
    gain_share = norm_gains.shape[2]
    conv_share = conv_state.shape[1]
    grad_gains = lax.dynamic_slice_in_dim(
        wide_small[:, : 2 * width].reshape(LAYERS, 2, width), slot * gain_share, gain_share, 2
    )
    grad_conv = lax.dynamic_slice_in_dim(wide_small[:, 2 * width :], slot * conv_share, conv_share, 1)
    grad_channel = local_small[:, : 6 * channels].reshape(LAYERS, 6, channels)
    grad_head = local_small[:, 6 * channels :].reshape(LAYERS, 3, ssm_heads)

    outs = {k: [] for k in ("q", "gate", "step", "attn", "ssm", "gu", "down", "kv", "state")}
    for layer in range(LAYERS):
        g1, g2 = (v.astype(F32) for v in big[layer])
        outs["gu"].append(g1[:, : 2 * hidden].reshape(depth, 2, hidden))
        outs["down"].append(g1[:, 2 * hidden : 3 * hidden].T)
        outs["attn"].append(g2[:, 1536:1664].T)
        outs["ssm"].append(g2[:, 1664:2048].T)
        outs["q"].append(g2[:, :128])
        outs["gate"].append(g2[:, 128 : 128 + 2 * channels].reshape(depth, 2, channels))
        outs["step"].append(g2[:, 896 : 896 + ssm_heads])
        sh = big[layer][1][:, 1024:1536]
        rows = sh.shape[0] // tp_size

        def part(distance):
            return lax.dynamic_slice_in_dim(sh, (tensor ^ distance) * rows, rows, 0).astype(F32)

        sh = part(0) + sum(swap(part(d), "tensor", d) for d in (1, 2, 3))
        outs["kv"].append(sh[:, :kv_cols])
        outs["state"].append(sh[:, kv_cols:])
    st = {k: jnp.stack(v) for k, v in outs.items()}
    return (
        output[None], input_grad[None], grad_gains, st["q"], st["kv"], st["gate"], st["state"],
        st["step"], grad_channel, grad_conv, grad_head, st["attn"], st["ssm"], st["gu"], st["down"],
    )


def solution(mesh):
    split = (
        P("dp", "tensor", None),
        P("dp", "tensor", None),
        P("dp", None),
        P(None, None, ("dp", "tensor")),
        P(None, "dp", "tensor"),
        P(None, ("dp", "tensor"), None),
        P(None, "dp", None, "tensor"),
        P(None, ("dp", "tensor"), None),
        P(None, "dp", "tensor"),
        P(None, None, "tensor"),
        P(None, ("dp", "tensor")),
        P(None, None, "tensor"),
        P(None, "tensor", "dp"),
        P(None, "tensor", "dp"),
        P(None, "dp", None, "tensor"),
        P(None, "tensor", "dp"),
    )
    out_split = split[:2] + split[3:]
    return jax.shard_map(body, mesh=mesh, in_specs=split, out_specs=out_split, check_vma=False)
```

```python
import functools

import jax
import jax.numpy as jnp
from jax import lax
from jax.experimental import pallas as pl
from jax.experimental.pallas import tpu as pltpu
from jax.sharding import PartitionSpec as P

HQ = 8
HD = 64
HS = 24
PH = 64
NS = 128
LAYERS = 2
EPS = 1e-05
ROPE_BASE = 100000000000.0
R = 128
QUARTERS = 4
DISTANCE = (1, 3, 0, 2)
F32 = jnp.float32
BF16 = jnp.bfloat16
EXACT = lax.Precision.HIGHEST
NEG = -1e30
VMEM_BYTES = 16 * 1024 * 1024
GRADS_BYTES = 24 * 1024 * 1024


def dot_nn(left, right, **kw):
    return lax.dot_general(
        left, right, (((1,), (0,)), ((), ())), preferred_element_type=F32, **kw
    )


def dot_nt(left, right, **kw):
    return lax.dot_general(
        left, right, (((1,), (1,)), ((), ())), preferred_element_type=F32, **kw
    )


def dot_tn(left, right, **kw):
    return lax.dot_general(
        left, right, (((0,), (0,)), ((), ())), preferred_element_type=F32, **kw
    )


def iota(shape, dim):
    return lax.broadcasted_iota(jnp.int32, shape, dim)


def softplus(v):
    return jnp.maximum(v, 0.0) + jnp.log1p(jnp.exp(-jnp.abs(v)))


def partner(v, lane):
    return jnp.where(lane % HD < HD // 2, pltpu.roll(v, 96, 1), pltpu.roll(v, 32, 1))


def block_of(quarter, rank):
    k = quarter ^ rank
    return 2 - 2 * (k & 1) + (k >> 1)


def sds(shape, dtype):
    return jax.ShapeDtypeStruct(shape, dtype)


def whole(shape, *at):
    at = at or (0,) * len(shape)
    return pl.BlockSpec(shape, lambda *_: at, pipeline_mode=pl.Buffered(1))


def hbm(v):
    return jax.tree.map(lambda x: pltpu.with_memory_space_constraint(x, pltpu.HBM), v)


def far_out(shape, dtype):
    return pltpu.HBM(shape, dtype)


def bytes_of(made):
    size = made.dtype.itemsize
    for d in made.shape:
        size *= d
    return size


SCALAR = pl.BlockSpec(memory_space=pltpu.SMEM)


def call(kernel, name, in_specs, out_shapes, flops, scratch=(), deps=(), vmem=VMEM_BYTES):
    if deps:
        base, skipped = kernel, range(len(in_specs), len(in_specs) + len(deps))

        def kernel(*refs):
            base(*(r for i, r in enumerate(refs) if i not in skipped))

        in_specs = list(in_specs) + [pl.BlockSpec(memory_space=pl.ANY)] * len(deps)
    many = sum(bytes_of(s) for s in out_shapes)
    made = pl.pallas_call(
        kernel,
        grid=(1,),
        in_specs=in_specs,
        out_specs=[whole(s.shape) for s in out_shapes],
        out_shape=out_shapes,
        scratch_shapes=list(scratch),
        compiler_params=pltpu.CompilerParams(
            dimension_semantics=("arbitrary",), vmem_limit_bytes=vmem
        ),
        cost_estimate=pl.CostEstimate(
            flops=int(flops), bytes_accessed=2 * many, transcendentals=10**5
        ),
        name=name,
    )
    return lambda *args: made(*args, *deps)


def rms(v, gain):
    return v * lax.rsqrt(jnp.mean(v * v, axis=-1, keepdims=True) + EPS) * gain


def rms_back(v, gain, grad):
    factor = lax.rsqrt(jnp.mean(v * v, axis=-1, keepdims=True) + EPS)
    weighted = grad * gain
    inner = jnp.mean(weighted * v, axis=-1, keepdims=True)
    scaled = v * factor
    return (
        factor * weighted - scaled * (factor * factor * inner),
        jnp.sum(grad * scaled, axis=0, keepdims=True),
    )


def step_kernel(x, keep, got, far, gain, x_o, h_o):
    total = keep[...].astype(F32) + got[...].astype(F32) + far[...].astype(F32)
    new = x[...].astype(F32) + total
    x_o[...] = new.astype(x_o.dtype)
    if h_o is not None:
        h_o[...] = rms(new, gain[0:1]).astype(BF16)


def last_kernel(x, keep, got, far, x_o):
    step_kernel(x, keep, got, far, None, x_o, None)


def take_step(x, keep, got, far, gain, deps=()):
    w = x.shape[1]
    specs = [whole((R, w))] * 4
    if gain is None:
        return call(last_kernel, "last_step", specs, [sds((R, w), BF16)], 10**6, deps=deps)(
            hbm(x), *hbm((keep, got, far))
        )[0]
    return call(
        step_kernel, "step", specs + [whole((8, w))], [far_out((R, w), F32), sds((R, w), BF16)], 10**6
    )(hbm(x), *hbm((keep, got, far)), gain)


def back_step_kernel(g, v, keep, got, far, gain, g_o, low_o, gg_o):
    grad = keep[...].astype(F32) + got[...].astype(F32) + far[...].astype(F32)
    through, gg = rms_back(v[...].astype(F32), gain[0:1], grad)
    new = g[...].astype(F32) + through
    g_o[...] = new
    low_o[...] = new.astype(BF16)
    gg_o[...] = jnp.broadcast_to(gg, gg_o.shape)


def back_step(g, v, keep, got, far, gain, deps=()):
    w = v.shape[1]
    return call(
        back_step_kernel,
        "back_step",
        [whole((R, w))] * 5 + [whole((8, w))],
        [far_out((R, w), F32), sds((R, w), BF16), sds((8, w), F32)],
        10**6,
        deps=deps,
    )(hbm(g), hbm(v), *hbm((keep, got, far)), gain)


def input_kernel(first, depth, rank, oh, p0, p1, p2, p3, gain, w_in, *refs):
    shares, outs = refs[: len(refs) - 4], refs[len(refs) - 4 :]
    h_o, pa_o, dt_o, ps_o = outs
    if len(shares) > 1:
        *shares, w_sh = shares
        sq = depth // QUARTERS
        for distance, share in enumerate(shares):
            for dp in range(share.shape[0] // depth):
                at = pl.multiple_of(dp * depth + (rank[0] ^ distance) * sq, sq)
                for c in range(QUARTERS):
                    rows = slice(dp * depth + c * sq, dp * depth + (c + 1) * sq)
                    w_sh[pl.ds(at, sq), 128 * c : 128 * c + 128] = share[rows]
    else:
        w_sh = shares[0]
    h = jnp.concatenate([p0[...], p1[...], p2[...], p3[...]], axis=0)
    if first:
        h = rms(h.astype(F32), gain[0:1]).astype(BF16)
    h_o[...] = h
    pa = dot_nn(h, w_in[...])
    pa_o[...] = pa[:, 0:896].astype(BF16)
    dt_o[...] = pa[:, 896:1024]
    ps = dot_nn(h, w_sh[...])
    k, v = ps[:, 0:128], ps[:, 128:256]
    left = iota(k.shape, 1) < HD
    is_first = oh[0] == 0
    k = jnp.where(is_first, k, pltpu.roll(k, HD, 1))
    v = jnp.where(is_first, pltpu.roll(v, HD, 1), v)
    ps_o[:, 0:128] = jnp.where(left, k, v).astype(BF16)
    ps_o[:, 128:384] = ps[:, 256:512].astype(BF16)


def project_in(first, depth, rank, oh, pieces, gain, w_in, w_sh):
    w = pieces[0].shape[1]
    n = QUARTERS * R
    shares = w_sh if isinstance(w_sh, tuple) else (w_sh,)
    outs = [far_out((n, w), BF16), sds((n, 896), BF16), sds((n, 128), F32), sds((n, 384), BF16)]
    if len(shares) > 1:
        outs = [sds((w, 512), BF16)] + outs
    return call(
        functools.partial(input_kernel, first, depth),
        "project_in",
        [SCALAR, SCALAR] + [whole((R, w))] * 4 + [whole((8, w)), whole((w, 1024))]
        + [whole(v.shape) for v in shares],
        outs,
        2 * n * w * 1536,
    )(rank, oh, *hbm(pieces), gain, w_in, *shares)


def input_back_kernel(da, ds, w_in, w_sh, send, keep):
    dh = (dot_nt(da[...], w_in[...]) + dot_nt(ds[...], w_sh[...])).astype(BF16)
    send[...] = dh[0 : 2 * R]
    keep[...] = dh[2 * R :]


def project_in_back(da, ds, w_in, w_sh, deps=()):
    n, w = da.shape[0], w_in.shape[0]
    return call(
        input_back_kernel,
        "project_in_back",
        [whole((n, 1024)), whole((n, 512)), whole((w, 1024)), whole((w, 512))],
        [sds((2 * R, w), BF16)] * 2,
        2 * n * w * 1536,
        deps=deps,
    )(hbm(da), hbm(ds), w_in, w_sh)


def column(row_ref, start):
    row = row_ref[:, pl.ds(pl.multiple_of(start, R), R)]
    return jnp.broadcast_to(row, (R, R)).T


def mix_kernel(half, rank, o, y, pa, fac, gain, w_mix, m_o, send, keep):
    m_o[:, 0:128] = o[...]
    for j in range(QUARTERS):
        rows = slice(j * R, (j + 1) * R)
        f = column(fac, half * QUARTERS * R + (rank[0] ^ DISTANCE[j]) * R)
        for p in range(3):
            z = pa[rows, 128 + 128 * p : 256 + 128 * p].astype(F32)
            u = y[rows, 128 * p : 128 * p + 128].astype(F32) * (z * jax.nn.sigmoid(z))
            m_o[rows, 128 + 128 * p : 256 + 128 * p] = (
                u * f * gain[0:1, 128 * p : 128 * p + 128]
            ).astype(BF16)
    mixed = dot_nt(m_o[...], w_mix[...]).astype(BF16)
    send[...] = mixed[0 : 2 * R]
    keep[...] = mixed[2 * R :]


def mix(half, rank, o, y, pa, fac, gain, w_mix):
    n, w = y.shape[0], w_mix.shape[0]
    return call(
        functools.partial(mix_kernel, half),
        "mix",
        [
            SCALAR, whole((n, 128)), whole((n, 384)), whole((n, 512)), whole(fac.shape),
            whole((8, 384)), whole((w, 512), 0, 2),
        ],
        [far_out((n, 512), BF16), sds((2 * R, w), BF16), sds((2 * R, w), BF16)],
        2 * n * w * 512,
    )(rank, o, y, pa, fac, gain, w_mix)


def mix_back_kernel(rank, p0, p1, p2, p3, y, pa, gain, w_mix, dm_o, do_o, dyn_o, cross_o):
    dm = jnp.concatenate([p0[...], p1[...], p2[...], p3[...]], axis=0)
    dm_o[...] = dm
    d = dot_nn(dm, w_mix[...])
    do_o[...] = d[:, 0:128].astype(BF16)
    dyn_o[...] = d[:, 128:512]
    ones = jnp.ones((8, R), F32)
    for j in range(QUARTERS):
        rows = slice(j * R, (j + 1) * R)
        total = jnp.zeros((R, R), F32)
        for p in range(3):
            z = pa[rows, 128 + 128 * p : 256 + 128 * p].astype(F32)
            u = y[rows, 128 * p : 128 * p + 128].astype(F32) * (z * jax.nn.sigmoid(z))
            total = total + d[rows, 128 + 128 * p : 256 + 128 * p] * u * (
                gain[0:1, 128 * p : 128 * p + 128]
            )
        at = pl.multiple_of((rank[0] ^ DISTANCE[j]) * R, R)
        cross_o[:, pl.ds(at, R)] = dot_nt(ones, total, precision=EXACT)[0:1]


def mix_back(rank, pieces, y, pa, gain, w_mix):
    n, w = y.shape[0], w_mix.shape[0]
    return call(
        mix_back_kernel,
        "mix_back",
        [SCALAR] + [whole((R, w))] * 4
        + [whole((n, 384)), whole((n, 512)), whole((8, 384)), whole((w, 512), 0, 2)],
        [far_out((n, w), BF16), sds((n, 128), BF16), far_out((n, 384), F32), sds((1, n), F32)],
        2 * n * w * 512,
    )(rank, *hbm(pieces), hbm(y), hbm(pa), gain, w_mix)


def ffn_kernel(p0, p1, p2, p3, w_gu, w_dn, h_o, gu_o, act_o, send, keep):
    h = jnp.concatenate([p0[...], p1[...], p2[...], p3[...]], axis=0)
    h_o[...] = h
    gu = dot_nn(h, w_gu[...])
    gu_o[...] = gu.astype(BF16)
    g0 = gu[:, 0:512]
    act = (g0 * jax.nn.sigmoid(g0) * gu[:, 512:1024]).astype(BF16)
    act_o[...] = act
    out = dot_nt(act, w_dn[...]).astype(BF16)
    send[...] = out[0 : 2 * R]
    keep[...] = out[2 * R :]


def ffn(pieces, w_second):
    n, w = QUARTERS * R, pieces[0].shape[1]
    return call(
        ffn_kernel,
        "ffn",
        [whole((R, w))] * 4 + [whole((w, 1024)), whole((w, 512), 0, 2)],
        [
            far_out((n, w), BF16), far_out((n, 1024), BF16), far_out((n, 512), BF16),
            sds((2 * R, w), BF16), sds((2 * R, w), BF16),
        ],
        2 * n * w * 1536,
    )(*hbm(pieces), w_second, w_second)


def ffn_back_kernel(p0, p1, p2, p3, gu, w_gu, w_dn, df_o, dgu_o, send, keep):
    df = jnp.concatenate([p0[...], p1[...], p2[...], p3[...]], axis=0)
    df_o[...] = df
    da = dot_nn(df, w_dn[...])
    g0, g1 = gu[:, 0:512].astype(F32), gu[:, 512:1024].astype(F32)
    sg = jax.nn.sigmoid(g0)
    dgu_o[:, 0:512] = (da * g1 * sg * (1.0 + g0 * (1.0 - sg))).astype(BF16)
    dgu_o[:, 512:1024] = (da * g0 * sg).astype(BF16)
    out = dot_nt(dgu_o[...], w_gu[...]).astype(BF16)
    send[...] = out[0 : 2 * R]
    keep[...] = out[2 * R :]


def ffn_back(pieces, gu, w_second, deps=()):
    n, w = QUARTERS * R, pieces[0].shape[1]
    return call(
        ffn_back_kernel,
        "ffn_back",
        [whole((R, w))] * 4 + [whole((n, 1024)), whole((w, 1024)), whole((w, 512), 0, 2)],
        [far_out((n, w), BF16), far_out((n, 1024), BF16), sds((2 * R, w), BF16), sds((2 * R, w), BF16)],
        2 * n * w * 1536,
        deps=deps,
    )(*hbm(pieces), hbm(gu), w_second, w_second)


def weight_grad_kernel(widths, share, depth, sel, *refs):
    out = refs[-1]
    at = 0
    for i, width in enumerate(widths):
        la, lb, ra, rb = refs[4 * i : 4 * i + 4]
        total = 0.0
        for left, right in ((la, ra), (lb, rb)):
            if share is None:
                rows = left[...]
            else:
                rows = left[:, pl.ds(pl.multiple_of(sel[0] * share, share), share)]
            total = total + dot_tn(rows, right[...])
        out[:, at : at + width] = total.astype(BF16)
        at += width
    if depth is None:
        return
    kept, got, far = refs[4 * len(widths) : 4 * len(widths) + 3]
    sq = depth // QUARTERS
    for d in range(out.shape[0] // depth):
        start = pl.multiple_of((pl.program_id(0) * (out.shape[0] // depth) + d) * sq, sq)
        rows = pl.ds(start, sq)
        total = kept[rows].astype(F32) + got[rows].astype(F32) + far[rows].astype(F32)
        for c in range(QUARTERS):
            out[d * depth + c * sq : d * depth + (c + 1) * sq, at:] = total[
                :, 128 * c : 128 * c + 128
            ].astype(BF16)


def weight_grads(name, groups, deps=(), share=None, sel=None, shared=None, depth=None):
    n, w = groups[0][0][0].shape
    widths = [right[0].shape[1] for _, right in groups]
    step = 512 if share is None else 2 * share
    rows = step if share is None else share
    specs, args = [], []
    for (la, lb), (ra, rb) in groups:
        specs += [pl.BlockSpec((n, step), lambda i: (0, i))] * 2 + [whole(ra.shape)] * 2
        args += [la, lb, ra, rb]
    args = list(hbm(args))
    total = sum(widths)
    if shared is not None:
        total += 128
        some = shared[2].shape
        specs += [whole(some)] * 3
        args += list(shared)
    taken = len(args)

    def kernel(sel_ref, *refs):
        weight_grad_kernel(widths, share, depth, sel_ref, *refs[:taken], refs[-1])

    return pl.pallas_call(
        kernel,
        grid=(w // step,),
        in_specs=[SCALAR] + specs + [pl.BlockSpec(memory_space=pl.ANY)] * len(deps),
        out_specs=pl.BlockSpec((rows, total), lambda i: (i, 0)),
        out_shape=far_out((w // step * rows, total), BF16),
        compiler_params=pltpu.CompilerParams(
            dimension_semantics=("arbitrary",), vmem_limit_bytes=GRADS_BYTES
        ),
        cost_estimate=pl.CostEstimate(
            flops=4 * n * w * total, bytes_accessed=2**20 * 12, transcendentals=0
        ),
        name=name,
    )(jnp.zeros((1,), jnp.int32) if sel is None else sel, *args, *deps)


def shared_grad_kernel(depth, rank, ha, hb, da, db, send, keep, made):
    made[...] = (dot_tn(ha[...], da[...]) + dot_tn(hb[...], db[...])).astype(BF16)
    sq, count = depth // QUARTERS, made.shape[0] // depth
    for j, distance in enumerate(DISTANCE):
        to = send if j < 2 else keep
        for d in range(count):
            at = pl.multiple_of(d * depth + (rank[0] ^ distance) * sq, sq)
            start = ((j % 2) * count + d) * sq
            to[start : start + sq] = made[pl.ds(at, sq)]


def shared_grads(depth, rank, h, ds):
    n, w = h[0].shape
    cols = ds[0].shape[1]
    send, keep = call(
        functools.partial(shared_grad_kernel, depth),
        "shared_grads",
        [SCALAR] + [whole((n, w))] * 2 + [whole((n, cols))] * 2,
        [sds((w // 2, cols), BF16)] * 2,
        4 * n * w * cols,
        [pltpu.VMEM((w, cols), BF16)],
    )(rank, *hbm(tuple(h)), *hbm(tuple(ds)))
    got = swap(send, "tensor", 1)
    half = w // 4
    far = swap((keep[half:].astype(F32) + got[half:].astype(F32)).astype(BF16), "tensor", 2)
    return keep, got, far


def gate(v, *deps):
    return pl.pallas_call(
        lambda *refs: None,
        in_specs=[pl.BlockSpec(memory_space=pl.ANY)] * (1 + len(deps)),
        out_specs=pl.BlockSpec(memory_space=pl.ANY),
        out_shape=far_out(v.shape, v.dtype),
        input_output_aliases={0: 0},
        name="gate",
    )(hbm(v), *deps)


def finish_kernel(a0, a1, b0, b1, gu, down, q, gate, step, attn, ssm, kv, state):
    sq = kv.shape[1]
    for layer, (a, b) in enumerate(((a0, b0), (a1, b1))):
        gu[layer] = a[:, 0:1024].astype(F32)
        down[layer] = a[:, 1024:1536].astype(F32).T
        q[layer] = b[:, 0:128].astype(F32)
        gate[layer] = b[:, 128:896].astype(F32)
        step[layer] = b[:, 896:1024].astype(F32)
        attn[layer] = b[:, 1024:1152].astype(F32).T
        ssm[layer] = b[:, 1152:1536].astype(F32).T
        share = b[:, 1536:1664].astype(F32)
        for c in range(QUARTERS):
            to = kv if c < 2 else state
            to[layer, :, 128 * (c % 2) : 128 * (c % 2) + 128] = share[c * sq : (c + 1) * sq]


def finish(firsts, seconds):
    d = firsts[0].shape[0]
    return call(
        finish_kernel,
        "finish",
        [whole((d, 1536))] * 2 + [whole((d, 1664))] * 2,
        [
            sds((2, d, 1024), F32), sds((2, 512, d), F32), sds((2, d, 128), F32), sds((2, d, 768), F32),
            sds((2, d, 128), F32), sds((2, 128, d), F32), sds((2, 384, d), F32),
            sds((2, d // QUARTERS, 256), F32), sds((2, d // QUARTERS, 256), F32),
        ],
        10**6,
    )(*firsts, *seconds)


def chunk_terms(act, raw_step, tok, seg_row, par):
    row, lane = iota((R, R), 0), iota((R, R), 1)
    b, c = act[:, 384:512], act[:, 512:640]
    bb, cb = b.astype(BF16), c.astype(BF16)
    dt = softplus(raw_step + par[1:2])
    tri = (row >= lane).astype(F32)
    cum = dot_nn(tri, dt * par[0:1], precision=EXACT)
    last = cum[R - 1 : R]
    okay = (row >= lane) & (tok[:, 5:6] == seg_row)
    inner = jnp.where(okay, dot_nt(cb, bb), 0.0)
    enter = jnp.exp(cum) * tok[:, 3:4]
    tail = jnp.exp(jnp.minimum(last - cum, 0.0)) * tok[:, 4:5]
    return b, c, bb, cb, dt, cum, cum.T, dt.T, okay, inner, enter, tail


def ssm_fwd_chunk(pa, raw, ps, tok, seg_row, cos, sin, taps, par, skip, y_o, pre_o, st_o, q_o, kv_o, state, hist):
    lane = iota((R, R), 1)
    half = lane < PH
    xin = jnp.concatenate([pa[:, 512:896], ps[:, 128:384]], axis=1).astype(F32)
    ext = jnp.concatenate([hist[...], xin], axis=0)
    hist[...] = xin[R - 8 :]
    pre = taps[4:5] + xin * taps[3:4]
    for k in (1, 2, 3):
        pre = pre + ext[8 - k : 8 - k + R] * tok[:, k - 1 : k] * taps[3 - k : 4 - k]
    pre_o[...] = pre.astype(BF16)
    act = pre * jax.nn.sigmoid(pre)
    b, c, bb, cb, dt, cum, cum_t, dt_t, okay, inner, enter, tail = chunk_terms(
        act, raw[...], tok, seg_row, par
    )
    tail = tail * dt
    keep = enter[R - 1 : R]
    b_t = b.T.astype(BF16)
    squares = jnp.zeros((R, R), F32)
    for p in range(3):
        h0, h1 = 2 * p, 2 * p + 1
        cols = slice(128 * p, 128 * p + 128)
        xp = act[:, cols]
        xb = xp.astype(BF16)
        sp = state[:, cols]
        st_o[:, cols] = sp.astype(BF16)

        def weights(h):
            gap = jnp.minimum(cum[:, h : h + 1] - cum_t[h : h + 1], 0.0)
            return (inner * jnp.exp(gap) * dt_t[h : h + 1]).astype(BF16)

        y = jnp.where(half, dot_nn(weights(h0), xb), dot_nn(weights(h1), xb))
        y = y + dot_nn(cb, sp.astype(BF16)) * jnp.where(
            half, enter[:, h0 : h0 + 1], enter[:, h1 : h1 + 1]
        )
        y = y + skip[0:1, cols] * xp
        y_o[:, cols] = y.astype(BF16)
        tp = jnp.where(half, tail[:, h0 : h0 + 1], tail[:, h1 : h1 + 1])
        kp = jnp.where(half[0:1], keep[:, h0 : h0 + 1], keep[:, h1 : h1 + 1])
        state[:, cols] = kp * sp + dot_nn(b_t, (tp * xp).astype(BF16))
        z = pa[:, 128 + 128 * p : 256 + 128 * p].astype(F32)
        u = y * z * jax.nn.sigmoid(z)
        squares = squares + u * u
    q = pa[:, 0:128].astype(F32)
    q_o[...] = (q * cos + partner(q, lane) * sin).astype(BF16)
    kv = ps[:, 0:128].astype(F32)
    kv_o[...] = jnp.where(half, kv * cos + partner(kv, lane) * sin, kv).astype(BF16)
    return dot_nt(jnp.ones((8, R), F32), squares, precision=EXACT)[0:1]


def ssm_fwd_kernel(
    rank, pa0, pa1, raw0, raw1, ps0, ps1, tok_r, seg_r, cos_r, sin_r, taps, par, skip,
    y0, y1, pre0, pre1, st_o, sq_o, q_o, kv_o, state, hist,
):
    i = pl.program_id(0)

    @pl.when(i == 0)
    def _():
        state[...] = jnp.zeros_like(state)
        hist[...] = jnp.zeros_like(hist)

    halves = ((pa0, raw0, ps0, y0, pre0), (pa1, raw1, ps1, y1, pre1))
    for half, (pa, raw, ps, y_o, pre_o) in enumerate(halves):
        rows = slice(half * R, (half + 1) * R)
        at = pl.multiple_of(half * QUARTERS * R + i * R, R)
        sq_o[:, pl.ds(at, R)] = ssm_fwd_chunk(
            pa, raw, ps, tok_r[rows], seg_r[0:1, rows], cos_r[rows], sin_r[rows], taps, par, skip,
            y_o, pre_o, st_o.at[half], q_o.at[rows], kv_o.at[rows], state, hist,
        )


def wire(width, reverse=False):
    def at(i, rank):
        i = QUARTERS - 1 - i if reverse else i
        return (block_of(i, rank[0]), 0)

    return pl.BlockSpec((R, width), at)


def in_order(shape, dim=0, reverse=False):
    def at(i, rank):
        i = QUARTERS - 1 - i if reverse else i
        return tuple(i if d == dim else 0 for d in range(len(shape)))

    return pl.BlockSpec(shape, at)


def ssm_forward(rank, pa, raw, ps, tok, seg_rows, cos, sin, taps, par, skip):
    n = QUARTERS * R
    t = 2 * n
    return pl.pallas_call(
        ssm_fwd_kernel,
        grid_spec=pltpu.PrefetchScalarGridSpec(
            num_scalar_prefetch=1,
            grid=(QUARTERS,),
            in_specs=[
                wire(896), wire(896), wire(128), wire(128), wire(384), wire(384),
                in_order((2 * R, 8)), in_order((8, 2 * R), 1),
                in_order((2 * R, 128)), in_order((2 * R, 128)), whole((8, 640)), whole((8, 128)), whole((8, 384)),
            ],
            out_specs=[
                wire(384), wire(384), wire(640), wire(640), in_order((2, NS, 384)), whole((1, t)),
                in_order((2 * R, 128)), in_order((2 * R, 128)),
            ],
            scratch_shapes=[pltpu.VMEM((NS, 384), F32), pltpu.VMEM((8, 640), F32)],
        ),
        out_shape=[
            sds((n, 384), BF16), sds((n, 384), BF16), far_out((n, 640), BF16), far_out((n, 640), BF16),
            far_out((2 * QUARTERS, NS, 384), BF16), sds((1, t), F32), sds((t, 128), BF16), sds((t, 128), BF16),
        ],
        compiler_params=pltpu.CompilerParams(
            dimension_semantics=("arbitrary",), vmem_limit_bytes=VMEM_BYTES
        ),
        cost_estimate=pl.CostEstimate(
            flops=4 * 10**9, bytes_accessed=20 * 2**20, transcendentals=3 * 10**6
        ),
        name="ssm_forward",
    )(rank, *pa, *raw, *ps, tok, seg_rows, cos, sin, taps, par, skip)


def ssm_bwd_chunk(
    pa, raw, ps, pre_r, y_r, st_r, dyn_r, r2, coef, dq, dkv, tok, seg_row, taps, par, skip, gain,
    da_o, ds_o, gt_o, gc_o, gh_o, dstate, nxt, own_first,
):
    row, lane = iota((R, R), 0), iota((R, R), 1)
    half = lane < PH
    sub = iota((8, R), 0)
    pre = pre_r[...].astype(F32)
    sg = jax.nn.sigmoid(pre)
    act = pre * sg
    b, c, bb, cb, dt, cum, cum_t, dt_t, okay, inner, enter, tail = chunk_terms(
        act, raw[...], tok, seg_row, par
    )
    tail_dt = tail * dt
    keep = enter[R - 1 : R]
    c_t = c.T.astype(BF16)
    db = jnp.zeros((R, R), F32)
    dc = jnp.zeros((R, R), F32)
    dinner = jnp.zeros((R, R), F32)
    dcum = jnp.zeros((R, R), F32)
    extra = jnp.zeros((R, R), F32)
    col_sum = jnp.zeros((8, R), F32)
    last_row = jnp.zeros((1, R), F32)
    dx_parts = []
    for p in range(3):
        cols = slice(128 * p, 128 * p + 128)
        z = pa[:, 128 + 128 * p : 256 + 128 * p].astype(F32)
        y, dyn = y_r[:, cols].astype(F32), dyn_r[:, cols]
        zs = jax.nn.sigmoid(z)
        sz = z * zs
        u = y * sz
        dn = dyn * r2
        gc_o[0:1, cols] += jnp.sum(dn * u, axis=0, keepdims=True)
        du = gain[0:1, cols] * dn - u * coef
        da_o[:, 128 + 128 * p : 256 + 128 * p] = (
            du * y * zs * (1.0 + z * (1.0 - zs))
        ).astype(BF16)
        dy = du * sz
        dyb = dy.astype(BF16)
        xp = act[:, cols]
        xb = xp.astype(BF16)
        gc_o[1:2, cols] += jnp.sum(dy * xp, axis=0, keepdims=True)
        sb = st_r[:, cols]
        sp = sb.astype(F32)
        dsp = dstate[:, cols]
        dsb = dsp.astype(BF16)
        h0, h1 = 2 * p, 2 * p + 1
        ep = jnp.where(half, enter[:, h0 : h0 + 1], enter[:, h1 : h1 + 1])
        tp = jnp.where(half, tail_dt[:, h0 : h0 + 1], tail_dt[:, h1 : h1 + 1])
        kp = jnp.where(half[0:1], keep[:, h0 : h0 + 1], keep[:, h1 : h1 + 1])
        cdb = (ep * dy).astype(BF16)
        through = dy * ep * dot_nn(cb, sb)
        bds = dot_nn(bb, dsb)
        qx = xp * bds
        kept = jnp.sum(dsp * sp, axis=0, keepdims=True) * kp
        dxi = []
        for h in (h0, h1):
            mine = half if h == h0 else ~half
            gap = jnp.minimum(cum[:, h : h + 1] - cum_t[h : h + 1], 0.0)
            decay = jnp.where(okay, jnp.exp(gap), 0.0)
            dt_row = dt_t[h : h + 1]
            dg = dot_nt(jnp.where(mine, dy, 0.0).astype(BF16), xb)
            t1 = dg * decay
            dinner = dinner + t1 * dt_row
            w0 = t1 * inner
            col_sum = col_sum + jnp.where(sub == h, jnp.sum(w0, axis=0, keepdims=True), 0.0)
            w1 = w0 * dt_row + jnp.where(mine, through, 0.0)
            dcum = dcum + jnp.where(lane == h, jnp.sum(w1, axis=1, keepdims=True), 0.0)
            e = jnp.sum(jnp.where(mine, qx, 0.0), axis=1, keepdims=True)
            extra = extra + jnp.where(lane == h, e, 0.0)
            k = jnp.sum(jnp.where(mine[0:1], kept, 0.0), axis=1, keepdims=True)
            last_row = last_row + jnp.where(lane[0:1] == h, k, 0.0)
            dxi.append(dot_tn((decay * inner * dt_row).astype(BF16), dyb))
        dx_parts.append(jnp.where(half, dxi[0], dxi[1]) + tp * bds + skip[0:1, cols] * dy)
        dc = dc + dot_nt(cdb, sb)
        db = db + dot_nt((tp * xp).astype(BF16), dsb)
        dstate[:, cols] = kp * dsp + dot_nn(c_t, cdb)
    col_sum = jnp.concatenate([col_sum, jnp.zeros((R - 8, R), F32)], axis=0).T
    moved = tail_dt * extra
    last_row = last_row + jnp.sum(moved, axis=0, keepdims=True)
    dcum = dcum - col_sum * dt - moved + jnp.where(row == R - 1, last_row, 0.0)
    dlog = dot_nn((row <= lane).astype(F32), dcum, precision=EXACT)
    ddt = col_sum + tail * extra + par[0:1] * dlog
    gh_o[0:1] += jnp.sum(dt * dlog, axis=0, keepdims=True)
    ddr = ddt * jax.nn.sigmoid(raw[...] + par[1:2])
    gh_o[1:2] += jnp.sum(ddr, axis=0, keepdims=True)
    da_o[:, 896:1024] = ddr.astype(BF16)
    dib = dinner.astype(BF16)
    dc = dc + dot_nn(dib, bb)
    db = db + dot_tn(dib, cb)
    dact = jnp.concatenate([*dx_parts, db, dc], axis=1)
    dpre = dact * sg * (1.0 + pre * (1.0 - sg))
    xin = jnp.concatenate([pa[:, 512:896], ps[:, 128:384]], axis=1).astype(F32)
    dxin = dpre * taps[3:4]
    gt_o[3:4] += jnp.sum(dpre * xin, axis=0, keepdims=True)
    gt_o[4:5] += jnp.sum(dpre, axis=0, keepdims=True)
    for k in (1, 2, 3):
        zk = dpre * tok[:, k - 1 : k]
        later = nxt.at[k - 1]
        moved_up = jnp.concatenate([zk, later[...]], axis=0)[k : k + R]
        later[...] = zk[0:8]
        dxin = dxin + moved_up * taps[3 - k : 4 - k]
        gt_o[3 - k : 4 - k] += jnp.sum(moved_up * xin, axis=0, keepdims=True)
    da_o[:, 512:896] = dxin[:, 0:384].astype(BF16)
    ds_o[:, 256:512] = dxin[:, 384:640].astype(BF16)
    da_o[:, 0:128] = dq
    other = pltpu.roll(dkv, HD, 1)
    mine = half == own_first
    ds_o[:, 0:128] = jnp.where(mine, jnp.where(half, dkv, other), 0.0).astype(BF16)
    ds_o[:, 128:256] = jnp.where(mine, jnp.where(half, other, dkv), 0.0).astype(BF16)


def ssm_bwd_kernel(
    rank, oh, pa0, pa1, raw0, raw1, ps0, ps1, pre0, pre1, y0, y1, st_r, dyn0, dyn1, fac_r, coef_r, dq_r, dkv_r,
    tok_r, seg_r, taps, par, skip, gain,
    da0, da1, ds0, ds1, gt_o, gc_o, gh_o, dstate, nxt,
):
    i = pl.program_id(0)

    @pl.when(i == 0)
    def _():
        dstate[...] = jnp.zeros_like(dstate)
        nxt[...] = jnp.zeros_like(nxt)
        gt_o[...] = jnp.zeros_like(gt_o)
        gc_o[...] = jnp.zeros_like(gc_o)
        gh_o[...] = jnp.zeros_like(gh_o)

    quarter = QUARTERS - 1 - i
    halves = (
        (pa0, raw0, ps0, pre0, y0, dyn0, da0, ds0),
        (pa1, raw1, ps1, pre1, y1, dyn1, da1, ds1),
    )
    for half in (1, 0):
        pa, raw, ps, pre, y, dyn, da, ds = halves[half]
        rows = slice(half * R, (half + 1) * R)
        start = half * QUARTERS * R + quarter * R
        ssm_bwd_chunk(
            pa, raw, ps, pre, y, st_r.at[half], dyn, column(fac_r, start), column(coef_r, start),
            dq_r[rows], dkv_r[rows].astype(F32), tok_r[rows], seg_r[0:1, rows], taps, par, skip, gain,
            da, ds, gt_o, gc_o, gh_o, dstate, nxt, oh[0] == 0,
        )


def ssm_backward(
    rank, oh, pa, raw, ps, pre, y, states, dyn, fac, coef, dq, dkv, tok, seg_rows, taps, par, skip, gain
):
    n = QUARTERS * R
    t = 2 * n
    back = {"reverse": True}
    return pl.pallas_call(
        lambda r, *refs: ssm_bwd_kernel(r, *refs),
        grid_spec=pltpu.PrefetchScalarGridSpec(
            num_scalar_prefetch=1,
            grid=(QUARTERS,),
            in_specs=[
                SCALAR, wire(896, **back), wire(896, **back), wire(128, **back), wire(128, **back),
                wire(384, **back), wire(384, **back),
                wire(640, **back), wire(640, **back), wire(384, **back), wire(384, **back),
                in_order((2, NS, 384), **back), wire(384, **back), wire(384, **back),
                whole((1, t)), whole((1, t)), in_order((2 * R, 128), **back), in_order((2 * R, 128), **back),
                in_order((2 * R, 8), **back), in_order((8, 2 * R), 1, **back),
                whole((8, 640)), whole((8, 128)), whole((8, 384)), whole((8, 384)),
            ],
            out_specs=[
                wire(1024, **back), wire(1024, **back), wire(512, **back), wire(512, **back),
                whole((8, 640)), whole((8, 384)), whole((8, 128)),
            ],
            scratch_shapes=[pltpu.VMEM((NS, 384), F32), pltpu.VMEM((3, 8, 640), F32)],
        ),
        out_shape=[
            far_out((n, 1024), BF16), far_out((n, 1024), BF16), far_out((n, 512), BF16), far_out((n, 512), BF16),
            sds((8, 640), F32), sds((8, 384), F32), sds((8, 128), F32),
        ],
        compiler_params=pltpu.CompilerParams(
            dimension_semantics=("arbitrary",), vmem_limit_bytes=VMEM_BYTES
        ),
        cost_estimate=pl.CostEstimate(
            flops=8 * 10**9, bytes_accessed=30 * 2**20, transcendentals=4 * 10**6
        ),
        name="ssm_backward",
    )(
        rank, oh, *hbm(pa), *hbm(raw), *hbm(ps), *hbm(pre), *hbm(y), hbm(states), *hbm(dyn), fac, coef, dq, dkv, tok, seg_rows, taps, par, skip, gain
    )


def head_views(kv, lane):
    zero = jnp.zeros_like(kv)
    left = lane < HD
    k0 = jnp.where(left, kv, zero)
    v1 = jnp.where(left, zero, kv)
    k1 = pltpu.roll(k0.astype(F32), HD, 1).astype(BF16)
    v0 = pltpu.roll(v1.astype(F32), HD, 1).astype(BF16)
    return (k0, k1), (v0, v1)


def allowed_keys(tok_r, seg_r, start, rows, keys):
    return (iota((rows, keys), 1) <= start + iota((rows, keys), 0)) & (
        tok_r[start : start + rows, 5:6] == seg_r[0:1, 0:keys]
    )


def attend_fwd_kernel(rank, q_r, kv_r, tok_r, seg_r, o0, o1, lse_o):
    n = q_r.shape[0]
    ks, vs = head_views(kv_r[...], iota((n, 2 * HD), 1))
    lane = iota((2 * R, 128), 1)
    for quarter in range(QUARTERS):
        start, keys = quarter * 2 * R, (quarter + 1) * 2 * R
        q = q_r[start:keys]
        okay = allowed_keys(tok_r, seg_r, start, 2 * R, keys)
        out = jnp.zeros((2 * R, 2 * HD), F32)
        stats = []
        for h in range(2):
            s = jnp.where(okay, dot_nt(q, ks[h][0:keys]) * HD**-0.5, NEG)
            top = jnp.max(s, axis=1, keepdims=True)
            e = jnp.exp(s - top)
            total = jnp.sum(e, axis=1, keepdims=True)
            out = out + dot_nn((e * (1.0 / total)).astype(BF16), vs[h][0:keys])
            stats.append(top + jnp.log(total))
        at = pl.ds(pl.multiple_of(block_of(quarter, rank[0]) * R, R), R)
        o0[at] = out[0:R].astype(BF16)
        o1[at] = out[R:].astype(BF16)
        lse_o[start:keys] = jnp.where(lane == 0, stats[0], stats[1])


def attend_bwd_kernel(
    rank, q_r, kv_r, do0, do1, lse_r, tok_r, seg_r, cos_r, sin_r, dq_o, dkv_o, dk_acc, dv_acc
):
    n = q_r.shape[0]
    ks, vs = head_views(kv_r[...], iota((n, 2 * HD), 1))
    lane = iota((2 * R, 128), 1)
    left = lane < HD
    dk_acc[...] = jnp.zeros_like(dk_acc)
    dv_acc[...] = jnp.zeros_like(dv_acc)
    for quarter in range(QUARTERS):
        start, keys = quarter * 2 * R, (quarter + 1) * 2 * R
        q = q_r[start:keys]
        at = pl.ds(pl.multiple_of(block_of(quarter, rank[0]) * R, R), R)
        do = jnp.concatenate([do0[at], do1[at]], axis=0)
        okay = allowed_keys(tok_r, seg_r, start, 2 * R, keys)
        lse = lse_r[start:keys]
        zero = jnp.zeros_like(q)
        dq = jnp.zeros((2 * R, 2 * HD), F32)
        for h in range(2):
            mine = left if h == 0 else ~left
            s = dot_nt(q, ks[h][0:keys]) * HD**-0.5
            p = jnp.where(okay, jnp.exp(s - lse[:, h : h + 1]), 0.0)
            dp = dot_nt(do, vs[h][0:keys])
            dot_sum = jnp.sum(p * dp, axis=1, keepdims=True)
            ds = (p * (dp - dot_sum)).astype(BF16)
            dq = dq + dot_nn(ds, ks[h][0:keys])
            dk_acc[0:keys] += dot_tn(ds, jnp.where(mine, q, zero))
            dv_acc[0:keys] += dot_tn(p.astype(BF16), jnp.where(mine, do, zero))
        dq = dq * HD**-0.5
        dq_o[start:keys] = (
            dq * cos_r[start:keys] - partner(dq, lane) * sin_r[start:keys]
        ).astype(BF16)
    for start in range(0, n, 2 * R):
        rows = slice(start, start + 2 * R)
        dk, dv = dk_acc[rows], dv_acc[rows]
        dk = (dk + pltpu.roll(dk, HD, 1)) * HD**-0.5
        dv = dv + pltpu.roll(dv, HD, 1)
        dk = dk * cos_r[rows] - partner(dk, lane) * sin_r[rows]
        dkv_o[rows] = jnp.where(left, dk, dv).astype(BF16)


def attend_forward(rank, q, kv, tok, seg_rows):
    t = q.shape[0]
    return call(
        attend_fwd_kernel,
        "attend_forward",
        [SCALAR, whole((t, 128)), whole((t, 128)), whole((t, 8)), whole((8, t))],
        [sds((t // 2, 128), BF16), sds((t // 2, 128), BF16), far_out((t, 128), F32)],
        2 * 10**9,
    )(rank, q, kv, tok, seg_rows)


def attend_backward(rank, q, kv, do, lse, tok, seg_rows, cos, sin, deps=()):
    t = q.shape[0]
    full = whole((t, 128))
    return call(
        attend_bwd_kernel,
        "attend_backward",
        [SCALAR, full, full, whole((t // 2, 128)), whole((t // 2, 128)), full,
         whole((t, 8)), whole((8, t)), full, full],
        [sds((t, 128), BF16), sds((t, 128), BF16)],
        4 * 10**9,
        [pltpu.VMEM((t, 128), F32), pltpu.VMEM((t, 128), F32)],
        deps,
    )(rank, hbm(q), hbm(kv), *do, hbm(lse), tok, seg_rows, cos, sin)


def swap(values, axis, distance):
    size = lax.axis_size(axis)
    return lax.ppermute(values, axis, [(i, i ^ distance) for i in range(size)])


def bits_of(axis):
    size = lax.axis_size(axis)
    return [1 << b for b in range(size.bit_length() - 1)]


def sum_over(values, axes):
    for axis in axes:
        for bit in bits_of(axis):
            values = values + swap(values, axis, bit)
    return values


def sum_rows(values):
    return values + sum(swap(values, "tensor", d) for d in (1, 2, 3))


def gather_half(own):
    far = swap(own, "tensor", 2)
    near = swap(own, "tensor", 1)
    return near, swap(far, "tensor", 1), own, far


def scatter_half(send, keep, on_the_way):
    got = swap(send, "tensor", 1)
    given = (keep[R:].astype(F32) + got[R:].astype(F32)).astype(BF16)
    on_the_way.append(given)
    return keep, got, swap(given, "tensor", 2)


def gather_everywhere(own):
    held = own[:, None]
    for axis in ("dp", "tensor"):
        place = lax.axis_index(axis)
        for bit in bits_of(axis):
            upper = (place & bit) != 0
            other = swap(held, axis, bit)
            low, high = jnp.where(upper, other, held), jnp.where(upper, held, other)
            held = jnp.concatenate([low, high], axis=0 if axis == "dp" else 1)
    return held.reshape(-1, *own.shape[1:])


def gather_dp(v):
    return lax.all_gather(v, "dp", axis=0, tiled=True)


def scatter_dp(v):
    return lax.psum_scatter(v, "dp", scatter_dimension=0, tiled=True)


def pairs_of_dp(share):
    size = lax.axis_size("dp")
    return share % 128 == 0 and size % 2 == 0 and size >= 4


def merge_kernel(a, b, o):
    o[...] = (a[...].astype(F32) + b[...].astype(F32)).astype(BF16)


def merge(a, b, deps):
    return call(merge_kernel, "merge", [whole(a.shape)] * 2, [far_out(a.shape, BF16)], 10**6, deps=deps)(
        hbm(a), hbm(b)
    )[0]


def scatter_lines(v):
    size = lax.axis_size("dp")
    lines = [[i for i in range(size) if i % 2 == s] for s in range(2)]
    return lax.psum_scatter(v, "dp", scatter_dimension=0, tiled=True, axis_index_groups=lines)


def pad_rows(v, rows=8):
    return jnp.pad(v, ((0, rows - v.shape[0]), (0, 0)))


def body(
    inputs, cotangent, segment_ids, norm_gains, w_query, key_value_weight, w_gate_in, w_state_in,
    w_step, ssm_channel, conv_state, head_params, w_attn_out, w_ssm_out, w_gate_up, w_down,
):
    width = inputs.shape[2]
    n = segment_ids.shape[1]
    tp_size = lax.axis_size("tensor")
    tensor = lax.axis_index("tensor")
    slot = lax.axis_index("dp") * tp_size + tensor
    kv_cols = key_value_weight.shape[2]
    kv_heads = kv_cols // (2 * HD)
    own_head = tensor * (w_query.shape[2] // HD) // (HQ // kv_heads)
    ssm_heads = w_step.shape[2]
    channels = ssm_heads * PH
    hidden = w_gate_up.shape[3]
    depth = w_query.shape[1]
    rank = tensor.reshape(1).astype(jnp.int32)
    oh = own_head.reshape(1).astype(jnp.int32)

    halves = [inputs[0, :R], inputs[0, R:]]
    x_pieces = [gather_half(v) for v in halves]

    shared = jnp.concatenate([key_value_weight, w_state_in], axis=2)
    sq, wide = shared.shape[1:]
    shares = [
        shared[layer].reshape(sq, wide // 128, 128).swapaxes(0, 1).reshape(depth, 128)
        for layer in range(LAYERS)
    ]

    def exchange(share):
        far = swap(share, "tensor", 2)
        return share, swap(share, "tensor", 1), far, swap(far, "tensor", 1)

    w_first, w_second, w_shared = [], [], []
    for layer in range(LAYERS):
        first = [
            w_query[layer],
            w_gate_in[layer].reshape(depth, 2 * channels),
            jnp.pad(w_step[layer], ((0, 0), (0, 128 - ssm_heads))),
            w_attn_out[layer].T,
            w_ssm_out[layer].T,
        ]
        second = [w_gate_up[layer].reshape(depth, 2 * hidden), w_down[layer].T]
        first = gather_dp(jnp.concatenate(first + (shares if layer == 0 else []), axis=1))
        if layer == 0:
            w_shared = [exchange(first[:, c : c + 128]) for c in range(1536, 1536 + 128 * LAYERS, 128)]
        w_first.append(first)
        w_second.append(gather_dp(jnp.concatenate(second, axis=1)))

    small = jnp.concatenate([norm_gains.reshape(-1), conv_state.reshape(-1)])[None, :]
    small_all = gather_everywhere(small).astype(F32)
    gain_count = norm_gains.size
    gains = (
        small_all[:, :gain_count]
        .reshape(-1, LAYERS, 2, norm_gains.shape[2])
        .transpose(1, 2, 0, 3)
        .reshape(LAYERS, 2, width)
    )
    conv_flat = (
        small_all[:, gain_count : gain_count + conv_state.size]
        .reshape(-1, LAYERS, conv_state.shape[1])
        .transpose(1, 0, 2)
        .reshape(LAYERS, 5, 2 * NS)
    )

    seg = segment_ids[0]
    segf = seg.astype(F32)
    index = jnp.arange(n, dtype=jnp.int32)
    places = index - jnp.sum((seg[None, :] < seg[:, None]).astype(jnp.int32), axis=1)
    freq = ROPE_BASE ** (-jnp.arange(HD // 2, dtype=F32) / (HD // 2))
    angle = places.astype(F32)[:, None] * freq[None, :]
    cos_one, sin_one = jnp.cos(angle), jnp.sin(angle)
    cos = jnp.concatenate([cos_one] * 4, axis=1)
    sin = jnp.concatenate([-sin_one, sin_one] * 2, axis=1)
    shifted = [
        (jnp.pad(seg, (k, 0), constant_values=-1)[:n] == seg).astype(F32) for k in (1, 2, 3)
    ]
    ends = seg.reshape(-1, R)[:, -1]
    before = jnp.concatenate([jnp.full((1,), -1, jnp.int32), ends[:-1]])
    enters = (seg.reshape(-1, R) == before[:, None]).astype(F32).reshape(-1)
    leaves = (seg.reshape(-1, R) == ends[:, None]).astype(F32).reshape(-1)
    tok = jnp.stack([*shifted, enters, leaves, segf, segf, segf], axis=1)
    seg_rows = jnp.broadcast_to(segf[None, :], (8, n))

    residual, last_parts, sent_on = halves, [], []
    pieces = x_pieces
    saved = []
    for layer in range(LAYERS):
        channel, head = ssm_channel[layer], head_params[layer]
        taps = pad_rows(jnp.concatenate([channel[:5], conv_flat[layer]], axis=1))
        rate = -jnp.exp(head[0])
        par = pad_rows(jnp.pad(jnp.stack([rate, head[1]]), ((0, 0), (0, 128 - ssm_heads))))
        skip = pad_rows(jnp.repeat(head[2], PH)[None, :])
        gain_row = pad_rows(channel[5:6])
        gain_one = pad_rows(gains[layer, 0:1])
        gain_two = pad_rows(gains[layer, 1:2])
        wf, ws, wh = w_first[layer], w_second[layer], w_shared[layer]
        ins = functools.partial(project_in, layer == 0, depth, rank, oh)
        w_all, *half_0 = ins(pieces[0], gain_one, wf, wh)
        w_shared[layer] = w_all
        h, pa, raw, ps = zip(half_0, ins(pieces[1], gain_one, wf, w_all))
        y0, y1, pre0, pre1, states, sq, q_rot, kv_rot = ssm_forward(
            rank, pa, raw, ps, tok, seg_rows, cos, sin, taps, par, skip
        )
        y, pre = (y0, y1), (pre0, pre1)
        total = sum_rows(sq)
        o0, o1, lse = attend_forward(rank, q_rot, kv_rot, tok, seg_rows)
        factor = lax.rsqrt(total / (HS * PH) + EPS)
        mixed, middle, h2, gu, act, result, pieces = [], [], [], [], [], [], []
        parts = []
        for i, o in enumerate((o0, o1)):
            m, send, keep = mix(i, rank, o, y[i], pa[i], factor, gain_row, wf)
            mixed.append(m)
            parts.append(scatter_half(send, keep, sent_on))
        gathered = []
        for i in range(2):
            x1, low = take_step(residual[i], *parts[i], gain_two)
            middle.append(x1)
            gathered.append(gather_half(low))
        parts = []
        for i in range(2):
            h2_i, gu_i, act_i, send, keep = ffn(gathered[i], ws)
            h2.append(h2_i)
            gu.append(gu_i)
            act.append(act_i)
            parts.append(scatter_half(send, keep, sent_on))
        for i in range(2):
            if layer + 1 < LAYERS:
                x2, low = take_step(middle[i], *parts[i], pad_rows(gains[layer + 1, 0:1]))
                result.append(x2)
                pieces.append(gather_half(low))
            else:
                last_parts.append((middle[i], *parts[i], None))
        saved.append(
            (residual, middle, h, pa, raw, ps, y, pre, states, q_rot, kv_rot, lse, factor, mixed, h2, gu, act,
             taps, par, skip, gain_row, gain_one, gain_two, rate)
        )
        residual = result

    grad = [cotangent[0, :R], cotangent[0, R:]]
    low = list(grad)
    big, small_grads = [None] * LAYERS, [None] * LAYERS
    for layer in reversed(range(LAYERS)):
        (first_in, middle, h, pa, raw, ps, y, pre, states, q_rot, kv_rot, lse, factor, mixed, h2, gu, act,
         taps, par, skip, gain_row, gain_one, gain_two, rate) = saved[layer]
        wf, ws, wh = w_first[layer], w_second[layer], w_shared[layer]
        gathered = [gather_half(v) for v in low]
        df, dgu, dm, do, dyn, cross, parts = [], [], [], [], [], [], []
        deps = (big[layer + 1][0],) if layer + 1 < LAYERS else ()
        for i in range(2):
            df_i, dgu_i, send, keep = ffn_back(gathered[i], gu[i], ws, deps)
            df.append(df_i)
            dgu.append(dgu_i)
            parts.append(scatter_half(send, keep, sent_on))
        groups = [(h2, dgu), (df, act)]
        paired = layer == 0 and pairs_of_dp(depth)
        if paired:
            side = (lax.axis_index("dp") % 2).reshape(1).astype(jnp.int32)
            given = weight_grads("grads_one_sent", groups, sent_on[-2:], depth, 1 - side)
            kept = weight_grads("grads_one_kept", groups, (given,), depth, side)
            sent = swap(given, "dp", 1)
            early = [(given,), (kept,)]
        else:
            g1 = weight_grads("grads_one", groups, sent_on[-2:])
            early = [(g1,), ()]
        gathered, dx1, dgain2, dgain1 = [], [], 0.0, 0.0
        for i in range(2):
            dx, low_i, gg = back_step(grad[i], middle[i], *parts[i], gain_two, early[i])
            dx1.append(dx)
            dgain2 = dgain2 + gg[0]
            gathered.append(gather_half(low_i))
        for i in range(2):
            dm_i, do_i, dyn_i, cross_i = mix_back(rank, gathered[i], y[i], pa[i], gain_row, wf)
            dm.append(dm_i)
            do.append(do_i)
            dyn.append(dyn_i)
            cross.append(cross_i)
        cross = sum_rows(jnp.concatenate(cross, axis=1))
        dq, dkv = attend_backward(
            rank, q_rot, kv_rot, do, lse, tok, seg_rows, cos, sin
        )
        coef = factor**3 * cross / (HS * PH)
        da0, da1, ds0, ds1, g_taps, g_chan, g_head = ssm_backward(
            rank, oh, pa, raw, ps, pre, y, states, dyn, factor, coef, dq, dkv, tok, seg_rows, taps, par, skip,
            gain_row,
        )
        groups = [(h, (da0, da1)), (dm, mixed)]
        shared_sum = shared_grads(depth, rank, h, (ds0, ds1))
        grads_two = functools.partial(
            weight_grads, "grads_two", groups, shared=shared_sum, depth=depth
        )
        if layer == 0:
            g2 = grads_two((big[layer + 1][1],))
            if paired:
                g1 = scatter_lines(merge(kept, sent, tuple(do)))
                g2 = gate(g2, g1)
        sums = [project_in_back(da, ds, wf, wh) for da, ds in ((da0, ds0), (da1, ds1))]
        parts = [scatter_half(*v, sent_on) for v in sums]
        deps = ()
        if layer > 0:
            g2 = grads_two(sent_on[-2:])
            deps = (g2,)
        grad, low = [], []
        for i in range(2):
            g, low_i, gg = back_step(dx1[i], first_in[i], *parts[i], gain_one, () if i else deps)
            grad.append(g)
            low.append(low_i)
            dgain1 = dgain1 + gg[0]
        chan_grad = jnp.concatenate([g_taps[:5, :channels], g_chan[0:1]], axis=0)
        head_grad = jnp.stack(
            [
                g_head[0, :ssm_heads] * rate,
                g_head[1, :ssm_heads],
                jnp.sum(g_chan[1].reshape(ssm_heads, PH), axis=1),
            ]
        )
        big[layer] = (g1 if paired else scatter_dp(g1), scatter_dp(g2))
        small_grads[layer] = (
            jnp.concatenate([dgain1, dgain2, g_taps[:5, channels:].reshape(-1)]),
            jnp.concatenate([chan_grad.reshape(-1), head_grad.reshape(-1)]),
        )
    input_grad = jnp.concatenate(grad, axis=0)
    output = jnp.concatenate([take_step(*v, (da0,)) for v in last_parts], axis=0)

    wide_small = jnp.concatenate([small_grads[l][0] for l in range(LAYERS)])
    local_small = jnp.concatenate([small_grads[l][1] for l in range(LAYERS)])
    total = sum_over(jnp.concatenate([wide_small, local_small])[None, :], ("dp",))[0]
    wide_small = sum_over(total[None, : wide_small.shape[0]], ("tensor",))[0]
    wide_small = wide_small.reshape(LAYERS, -1)
    local_small = total[wide_small.size :].reshape(LAYERS, -1)
    gain_share = norm_gains.shape[2]
    conv_share = conv_state.shape[1]
    grad_gains = lax.dynamic_slice_in_dim(
        wide_small[:, : 2 * width].reshape(LAYERS, 2, width), slot * gain_share, gain_share, 2
    )
    grad_conv = lax.dynamic_slice_in_dim(wide_small[:, 2 * width :], slot * conv_share, conv_share, 1)
    grad_channel = local_small[:, : 6 * channels].reshape(LAYERS, 6, channels)
    grad_head = local_small[:, 6 * channels :].reshape(LAYERS, 3, ssm_heads)

    gu, down, q, gate_in, step, attn, ssm, kv, state = finish(*zip(*big))
    return (
        output[None], input_grad[None], grad_gains, q, kv, gate_in.reshape(LAYERS, depth, 2, channels),
        state, step[:, :, :ssm_heads], grad_channel, grad_conv, grad_head, attn, ssm,
        gu.reshape(LAYERS, depth, 2, hidden), down,
    )


def solution(mesh):
    split = (
        P("dp", "tensor", None),
        P("dp", "tensor", None),
        P("dp", None),
        P(None, None, ("dp", "tensor")),
        P(None, "dp", "tensor"),
        P(None, ("dp", "tensor"), None),
        P(None, "dp", None, "tensor"),
        P(None, ("dp", "tensor"), None),
        P(None, "dp", "tensor"),
        P(None, None, "tensor"),
        P(None, ("dp", "tensor")),
        P(None, None, "tensor"),
        P(None, "tensor", "dp"),
        P(None, "tensor", "dp"),
        P(None, "dp", None, "tensor"),
        P(None, "tensor", "dp"),
    )
    out_split = split[:2] + split[3:]
    return jax.shard_map(body, mesh=mesh, in_specs=split, out_specs=out_split, check_vma=False)
```

```python
import functools

import jax
import jax.numpy as jnp
from jax import lax
from jax.experimental import pallas as pl
from jax.experimental.pallas import tpu as pltpu
from jax.sharding import PartitionSpec as P

HQ = 8
HD = 64
HS = 24
PH = 64
NS = 128
LAYERS = 2
EPS = 1e-05
ROPE_BASE = 100000000000.0
R = 128
QUARTERS = 4
DISTANCE = (1, 3, 0, 2)
F32 = jnp.float32
BF16 = jnp.bfloat16
EXACT = lax.Precision.HIGHEST
NEG = -1e30
VMEM_BYTES = 16 * 1024 * 1024
GRADS_BYTES = 24 * 1024 * 1024


def dot_nn(left, right, **kw):
    return lax.dot_general(
        left, right, (((1,), (0,)), ((), ())), preferred_element_type=F32, **kw
    )


def dot_nt(left, right, **kw):
    return lax.dot_general(
        left, right, (((1,), (1,)), ((), ())), preferred_element_type=F32, **kw
    )


def dot_tn(left, right, **kw):
    return lax.dot_general(
        left, right, (((0,), (0,)), ((), ())), preferred_element_type=F32, **kw
    )


def iota(shape, dim):
    return lax.broadcasted_iota(jnp.int32, shape, dim)


def softplus(v):
    return jnp.maximum(v, 0.0) + jnp.log1p(jnp.exp(-jnp.abs(v)))


def partner(v, lane):
    return jnp.where(lane % HD < HD // 2, pltpu.roll(v, 96, 1), pltpu.roll(v, 32, 1))


def block_of(quarter, rank):
    k = quarter ^ rank
    return 2 - 2 * (k & 1) + (k >> 1)


def sds(shape, dtype):
    return jax.ShapeDtypeStruct(shape, dtype)


def whole(shape, *at):
    at = at or (0,) * len(shape)
    return pl.BlockSpec(shape, lambda *_: at, pipeline_mode=pl.Buffered(1))


def hbm(v):
    return jax.tree.map(lambda x: pltpu.with_memory_space_constraint(x, pltpu.HBM), v)


def far_out(shape, dtype):
    return pltpu.HBM(shape, dtype)


def bytes_of(made):
    size = made.dtype.itemsize
    for d in made.shape:
        size *= d
    return size


SCALAR = pl.BlockSpec(memory_space=pltpu.SMEM)


def call(kernel, name, in_specs, out_shapes, flops, scratch=(), deps=(), vmem=VMEM_BYTES):
    if deps:
        base, skipped = kernel, range(len(in_specs), len(in_specs) + len(deps))

        def kernel(*refs):
            base(*(r for i, r in enumerate(refs) if i not in skipped))

        in_specs = list(in_specs) + [pl.BlockSpec(memory_space=pl.ANY)] * len(deps)
    many = sum(bytes_of(s) for s in out_shapes)
    made = pl.pallas_call(
        kernel,
        grid=(1,),
        in_specs=in_specs,
        out_specs=[whole(s.shape) for s in out_shapes],
        out_shape=out_shapes,
        scratch_shapes=list(scratch),
        compiler_params=pltpu.CompilerParams(
            dimension_semantics=("arbitrary",), vmem_limit_bytes=vmem
        ),
        cost_estimate=pl.CostEstimate(
            flops=int(flops), bytes_accessed=2 * many, transcendentals=10**5
        ),
        name=name,
    )
    return lambda *args: made(*args, *deps)


def rms(v, gain):
    return v * lax.rsqrt(jnp.mean(v * v, axis=-1, keepdims=True) + EPS) * gain


def rms_back(v, gain, grad):
    factor = lax.rsqrt(jnp.mean(v * v, axis=-1, keepdims=True) + EPS)
    weighted = grad * gain
    inner = jnp.mean(weighted * v, axis=-1, keepdims=True)
    scaled = v * factor
    return (
        factor * weighted - scaled * (factor * factor * inner),
        jnp.sum(grad * scaled, axis=0, keepdims=True),
    )


def step_kernel(x, keep, got, far, gain, x_o, h_o):
    total = keep[...].astype(F32) + got[...].astype(F32) + far[...].astype(F32)
    new = x[...].astype(F32) + total
    x_o[...] = new.astype(x_o.dtype)
    if h_o is not None:
        h_o[...] = rms(new, gain[0:1]).astype(BF16)


def last_kernel(x, keep, got, far, x_o):
    step_kernel(x, keep, got, far, None, x_o, None)


def take_step(x, keep, got, far, gain, deps=()):
    w = x.shape[1]
    specs = [whole((R, w))] * 4
    if gain is None:
        return call(last_kernel, "last_step", specs, [sds((R, w), BF16)], 10**6, deps=deps)(
            hbm(x), *hbm((keep, got, far))
        )[0]
    return call(
        step_kernel, "step", specs + [whole((8, w))], [far_out((R, w), F32), sds((R, w), BF16)], 10**6
    )(hbm(x), *hbm((keep, got, far)), gain)


def back_step_kernel(g, v, keep, got, far, gain, g_o, low_o, gg_o):
    grad = keep[...].astype(F32) + got[...].astype(F32) + far[...].astype(F32)
    through, gg = rms_back(v[...].astype(F32), gain[0:1], grad)
    new = g[...].astype(F32) + through
    g_o[...] = new
    low_o[...] = new.astype(BF16)
    gg_o[...] = jnp.broadcast_to(gg, gg_o.shape)


def back_step(g, v, keep, got, far, gain, deps=()):
    w = v.shape[1]
    return call(
        back_step_kernel,
        "back_step",
        [whole((R, w))] * 5 + [whole((8, w))],
        [far_out((R, w), F32), sds((R, w), BF16), sds((8, w), F32)],
        10**6,
        deps=deps,
    )(hbm(g), hbm(v), *hbm((keep, got, far)), gain)


def input_kernel(first, depth, rank, oh, p0, p1, p2, p3, gain, w_in, *refs):
    shares, outs = refs[: len(refs) - 4], refs[len(refs) - 4 :]
    h_o, pa_o, dt_o, ps_o = outs
    if len(shares) > 1:
        *shares, w_sh = shares
        sq = depth // QUARTERS
        for distance, share in enumerate(shares):
            for dp in range(share.shape[0] // depth):
                at = pl.multiple_of(dp * depth + (rank[0] ^ distance) * sq, sq)
                for c in range(QUARTERS):
                    rows = slice(dp * depth + c * sq, dp * depth + (c + 1) * sq)
                    w_sh[pl.ds(at, sq), 128 * c : 128 * c + 128] = share[rows]
    else:
        w_sh = shares[0]
    h = jnp.concatenate([p0[...], p1[...], p2[...], p3[...]], axis=0)
    if first:
        h = rms(h.astype(F32), gain[0:1]).astype(BF16)
    h_o[...] = h
    pa = dot_nn(h, w_in[...])
    pa_o[...] = pa[:, 0:896].astype(BF16)
    dt_o[...] = pa[:, 896:1024]
    ps = dot_nn(h, w_sh[...])
    k, v = ps[:, 0:128], ps[:, 128:256]
    left = iota(k.shape, 1) < HD
    is_first = oh[0] == 0
    k = jnp.where(is_first, k, pltpu.roll(k, HD, 1))
    v = jnp.where(is_first, pltpu.roll(v, HD, 1), v)
    ps_o[:, 0:128] = jnp.where(left, k, v).astype(BF16)
    ps_o[:, 128:384] = ps[:, 256:512].astype(BF16)


def project_in(first, depth, rank, oh, pieces, gain, w_in, w_sh):
    w = pieces[0].shape[1]
    n = QUARTERS * R
    shares = w_sh if isinstance(w_sh, tuple) else (w_sh,)
    outs = [far_out((n, w), BF16), sds((n, 896), BF16), sds((n, 128), F32), sds((n, 384), BF16)]
    if len(shares) > 1:
        outs = [sds((w, 512), BF16)] + outs
    return call(
        functools.partial(input_kernel, first, depth),
        "project_in",
        [SCALAR, SCALAR] + [whole((R, w))] * 4 + [whole((8, w)), whole((w, 1024))]
        + [whole(v.shape) for v in shares],
        outs,
        2 * n * w * 1536,
    )(rank, oh, *hbm(pieces), gain, w_in, *shares)


def input_back_kernel(da, ds, w_in, w_sh, send, keep):
    dh = (dot_nt(da[...], w_in[...]) + dot_nt(ds[...], w_sh[...])).astype(BF16)
    send[...] = dh[0 : 2 * R]
    keep[...] = dh[2 * R :]


def project_in_back(da, ds, w_in, w_sh, deps=()):
    n, w = da.shape[0], w_in.shape[0]
    return call(
        input_back_kernel,
        "project_in_back",
        [whole((n, 1024)), whole((n, 512)), whole((w, 1024)), whole((w, 512))],
        [sds((2 * R, w), BF16)] * 2,
        2 * n * w * 1536,
        deps=deps,
    )(hbm(da), hbm(ds), w_in, w_sh)


def column(row_ref, start):
    row = row_ref[:, pl.ds(pl.multiple_of(start, R), R)]
    return jnp.broadcast_to(row, (R, R)).T


def mix_kernel(half, rank, o, y, pa, fac, gain, w_mix, m_o, send, keep):
    m_o[:, 0:128] = o[...]
    for j in range(QUARTERS):
        rows = slice(j * R, (j + 1) * R)
        f = column(fac, half * QUARTERS * R + (rank[0] ^ DISTANCE[j]) * R)
        for p in range(3):
            z = pa[rows, 128 + 128 * p : 256 + 128 * p].astype(F32)
            u = y[rows, 128 * p : 128 * p + 128].astype(F32) * (z * jax.nn.sigmoid(z))
            m_o[rows, 128 + 128 * p : 256 + 128 * p] = (
                u * f * gain[0:1, 128 * p : 128 * p + 128]
            ).astype(BF16)
    mixed = dot_nt(m_o[...], w_mix[...]).astype(BF16)
    send[...] = mixed[0 : 2 * R]
    keep[...] = mixed[2 * R :]


def mix(half, rank, o, y, pa, fac, gain, w_mix):
    n, w = y.shape[0], w_mix.shape[0]
    return call(
        functools.partial(mix_kernel, half),
        "mix",
        [
            SCALAR, whole((n, 128)), whole((n, 384)), whole((n, 512)), whole(fac.shape),
            whole((8, 384)), whole((w, 512), 0, 2),
        ],
        [far_out((n, 512), BF16), sds((2 * R, w), BF16), sds((2 * R, w), BF16)],
        2 * n * w * 512,
    )(rank, o, y, pa, fac, gain, w_mix)


def mix_back_kernel(rank, p0, p1, p2, p3, y, pa, gain, w_mix, dm_o, do_o, dyn_o, cross_o):
    dm = jnp.concatenate([p0[...], p1[...], p2[...], p3[...]], axis=0)
    dm_o[...] = dm
    d = dot_nn(dm, w_mix[...])
    do_o[...] = d[:, 0:128].astype(BF16)
    dyn_o[...] = d[:, 128:512]
    ones = jnp.ones((8, R), F32)
    for j in range(QUARTERS):
        rows = slice(j * R, (j + 1) * R)
        total = jnp.zeros((R, R), F32)
        for p in range(3):
            z = pa[rows, 128 + 128 * p : 256 + 128 * p].astype(F32)
            u = y[rows, 128 * p : 128 * p + 128].astype(F32) * (z * jax.nn.sigmoid(z))
            total = total + d[rows, 128 + 128 * p : 256 + 128 * p] * u * (
                gain[0:1, 128 * p : 128 * p + 128]
            )
        at = pl.multiple_of((rank[0] ^ DISTANCE[j]) * R, R)
        cross_o[:, pl.ds(at, R)] = dot_nt(ones, total, precision=EXACT)[0:1]


def mix_back(rank, pieces, y, pa, gain, w_mix):
    n, w = y.shape[0], w_mix.shape[0]
    return call(
        mix_back_kernel,
        "mix_back",
        [SCALAR] + [whole((R, w))] * 4
        + [whole((n, 384)), whole((n, 512)), whole((8, 384)), whole((w, 512), 0, 2)],
        [far_out((n, w), BF16), sds((n, 128), BF16), far_out((n, 384), F32), sds((1, n), F32)],
        2 * n * w * 512,
    )(rank, *hbm(pieces), hbm(y), hbm(pa), gain, w_mix)


def ffn_kernel(p0, p1, p2, p3, w_gu, w_dn, h_o, gu_o, act_o, send, keep):
    h = jnp.concatenate([p0[...], p1[...], p2[...], p3[...]], axis=0)
    h_o[...] = h
    gu = dot_nn(h, w_gu[...])
    gu_o[...] = gu.astype(BF16)
    g0 = gu[:, 0:512]
    act = (g0 * jax.nn.sigmoid(g0) * gu[:, 512:1024]).astype(BF16)
    act_o[...] = act
    out = dot_nt(act, w_dn[...]).astype(BF16)
    send[...] = out[0 : 2 * R]
    keep[...] = out[2 * R :]


def ffn(pieces, w_second):
    n, w = QUARTERS * R, pieces[0].shape[1]
    return call(
        ffn_kernel,
        "ffn",
        [whole((R, w))] * 4 + [whole((w, 1024)), whole((w, 512), 0, 2)],
        [
            far_out((n, w), BF16), far_out((n, 1024), BF16), far_out((n, 512), BF16),
            sds((2 * R, w), BF16), sds((2 * R, w), BF16),
        ],
        2 * n * w * 1536,
    )(*hbm(pieces), w_second, w_second)


def ffn_back_kernel(p0, p1, p2, p3, gu, w_gu, w_dn, df_o, dgu_o, send, keep):
    df = jnp.concatenate([p0[...], p1[...], p2[...], p3[...]], axis=0)
    df_o[...] = df
    da = dot_nn(df, w_dn[...])
    g0, g1 = gu[:, 0:512].astype(F32), gu[:, 512:1024].astype(F32)
    sg = jax.nn.sigmoid(g0)
    dgu_o[:, 0:512] = (da * g1 * sg * (1.0 + g0 * (1.0 - sg))).astype(BF16)
    dgu_o[:, 512:1024] = (da * g0 * sg).astype(BF16)
    out = dot_nt(dgu_o[...], w_gu[...]).astype(BF16)
    send[...] = out[0 : 2 * R]
    keep[...] = out[2 * R :]


def ffn_back(pieces, gu, w_second, deps=()):
    n, w = QUARTERS * R, pieces[0].shape[1]
    return call(
        ffn_back_kernel,
        "ffn_back",
        [whole((R, w))] * 4 + [whole((n, 1024)), whole((w, 1024)), whole((w, 512), 0, 2)],
        [far_out((n, w), BF16), far_out((n, 1024), BF16), sds((2 * R, w), BF16), sds((2 * R, w), BF16)],
        2 * n * w * 1536,
        deps=deps,
    )(*hbm(pieces), hbm(gu), w_second, w_second)


def weight_grad_kernel(widths, share, sel, *refs):
    out = refs[-1]
    at = 0
    for i, width in enumerate(widths):
        la, lb, ra, rb = refs[4 * i : 4 * i + 4]
        total = 0.0
        for left, right in ((la, ra), (lb, rb)):
            if share is None:
                rows = left[...]
            else:
                rows = left[:, pl.ds(pl.multiple_of(sel[0] * share, share), share)]
            total = total + dot_tn(rows, right[...])
        out[:, at : at + width] = total.astype(BF16)
        at += width


def insert_kernel(depth, base, kept, got, far, *refs):
    out = refs[-1]
    sq = depth // QUARTERS
    count = out.shape[0] // depth
    for d in range(count):
        rows = pl.ds(pl.multiple_of((pl.program_id(0) * count + d) * sq, sq), sq)
        total = kept[rows].astype(F32) + got[rows].astype(F32) + far[rows].astype(F32)
        for c in range(QUARTERS):
            out[d * depth + c * sq : d * depth + (c + 1) * sq] = total[
                :, 128 * c : 128 * c + 128
            ].astype(BF16)


def insert_shared(made, shared, depth, deps=()):
    w, total = made.shape
    keep_in_place = pl.BlockSpec(memory_space=pl.ANY)
    return pl.pallas_call(
        functools.partial(insert_kernel, depth),
        grid=(w // 512,),
        in_specs=[keep_in_place] + [whole(shared[2].shape)] * 3 + [keep_in_place] * len(deps),
        out_specs=pl.BlockSpec((512, 128), lambda i: (i, total // 128 - 1)),
        out_shape=far_out((w, total), BF16),
        input_output_aliases={0: 0},
        compiler_params=pltpu.CompilerParams(
            dimension_semantics=("arbitrary",), vmem_limit_bytes=VMEM_BYTES
        ),
        name="insert_shared",
    )(hbm(made), *shared, *deps)


def weight_grads(name, groups, deps=(), share=None, sel=None, room=0):
    n, w = groups[0][0][0].shape
    widths = [right[0].shape[1] for _, right in groups]
    step = 512 if share is None else 2 * share
    rows = step if share is None else share
    specs, args = [], []
    for (la, lb), (ra, rb) in groups:
        specs += [pl.BlockSpec((n, step), lambda i: (0, i))] * 2 + [whole(ra.shape)] * 2
        args += [la, lb, ra, rb]
    args = list(hbm(args))
    total = sum(widths) + room
    taken = len(args)

    def kernel(sel_ref, *refs):
        weight_grad_kernel(widths, share, sel_ref, *refs[:taken], refs[-1])

    return pl.pallas_call(
        kernel,
        grid=(w // step,),
        in_specs=[SCALAR] + specs + [pl.BlockSpec(memory_space=pl.ANY)] * len(deps),
        out_specs=pl.BlockSpec((rows, total), lambda i: (i, 0)),
        out_shape=far_out((w // step * rows, total), BF16),
        compiler_params=pltpu.CompilerParams(
            dimension_semantics=("arbitrary",), vmem_limit_bytes=GRADS_BYTES
        ),
        cost_estimate=pl.CostEstimate(
            flops=4 * n * w * total, bytes_accessed=2**20 * 12, transcendentals=0
        ),
        name=name,
    )(jnp.zeros((1,), jnp.int32) if sel is None else sel, *args, *deps)


def shared_grad_kernel(depth, rank, ha, hb, da, db, send, keep, made):
    made[...] = (dot_tn(ha[...], da[...]) + dot_tn(hb[...], db[...])).astype(BF16)
    sq, count = depth // QUARTERS, made.shape[0] // depth
    for j, distance in enumerate(DISTANCE):
        to = send if j < 2 else keep
        for d in range(count):
            at = pl.multiple_of(d * depth + (rank[0] ^ distance) * sq, sq)
            start = ((j % 2) * count + d) * sq
            to[start : start + sq] = made[pl.ds(at, sq)]


def shared_grads(depth, rank, h, ds):
    n, w = h[0].shape
    cols = ds[0].shape[1]
    send, keep = call(
        functools.partial(shared_grad_kernel, depth),
        "shared_grads",
        [SCALAR] + [whole((n, w))] * 2 + [whole((n, cols))] * 2,
        [sds((w // 2, cols), BF16)] * 2,
        4 * n * w * cols,
        [pltpu.VMEM((w, cols), BF16)],
    )(rank, *hbm(tuple(h)), *hbm(tuple(ds)))
    got = swap(send, "tensor", 1)
    half = w // 4
    far = swap((keep[half:].astype(F32) + got[half:].astype(F32)).astype(BF16), "tensor", 2)
    return keep, got, far


def finish_kernel(a0, a1, b0, b1, gu, down, q, gate, step, attn, ssm, kv, state):
    sq = kv.shape[1]
    for layer, (a, b) in enumerate(((a0, b0), (a1, b1))):
        gu[layer] = a[:, 0:1024].astype(F32)
        down[layer] = a[:, 1024:1536].astype(F32).T
        q[layer] = b[:, 0:128].astype(F32)
        gate[layer] = b[:, 128:896].astype(F32)
        step[layer] = b[:, 896:1024].astype(F32)
        attn[layer] = b[:, 1024:1152].astype(F32).T
        ssm[layer] = b[:, 1152:1536].astype(F32).T
        share = b[:, 1536:1664].astype(F32)
        for c in range(QUARTERS):
            to = kv if c < 2 else state
            to[layer, :, 128 * (c % 2) : 128 * (c % 2) + 128] = share[c * sq : (c + 1) * sq]


def finish(firsts, seconds):
    d = firsts[0].shape[0]
    return call(
        finish_kernel,
        "finish",
        [whole((d, 1536))] * 2 + [whole((d, 1664))] * 2,
        [
            sds((2, d, 1024), F32), sds((2, 512, d), F32), sds((2, d, 128), F32), sds((2, d, 768), F32),
            sds((2, d, 128), F32), sds((2, 128, d), F32), sds((2, 384, d), F32),
            sds((2, d // QUARTERS, 256), F32), sds((2, d // QUARTERS, 256), F32),
        ],
        10**6,
    )(*firsts, *seconds)


def chunk_terms(act, raw_step, tok, seg_row, par):
    row, lane = iota((R, R), 0), iota((R, R), 1)
    b, c = act[:, 384:512], act[:, 512:640]
    bb, cb = b.astype(BF16), c.astype(BF16)
    dt = softplus(raw_step + par[1:2])
    tri = (row >= lane).astype(F32)
    cum = dot_nn(tri, dt * par[0:1], precision=EXACT)
    last = cum[R - 1 : R]
    okay = (row >= lane) & (tok[:, 5:6] == seg_row)
    inner = jnp.where(okay, dot_nt(cb, bb), 0.0)
    enter = jnp.exp(cum) * tok[:, 3:4]
    tail = jnp.exp(jnp.minimum(last - cum, 0.0)) * tok[:, 4:5]
    return b, c, bb, cb, dt, cum, cum.T, dt.T, okay, inner, enter, tail


def ssm_fwd_chunk(pa, raw, ps, tok, seg_row, cos, sin, taps, par, skip, y_o, pre_o, st_o, q_o, kv_o, state, hist):
    lane = iota((R, R), 1)
    half = lane < PH
    xin = jnp.concatenate([pa[:, 512:896], ps[:, 128:384]], axis=1).astype(F32)
    ext = jnp.concatenate([hist[...], xin], axis=0)
    hist[...] = xin[R - 8 :]
    pre = taps[4:5] + xin * taps[3:4]
    for k in (1, 2, 3):
        pre = pre + ext[8 - k : 8 - k + R] * tok[:, k - 1 : k] * taps[3 - k : 4 - k]
    pre_o[...] = pre.astype(BF16)
    act = pre * jax.nn.sigmoid(pre)
    b, c, bb, cb, dt, cum, cum_t, dt_t, okay, inner, enter, tail = chunk_terms(
        act, raw[...], tok, seg_row, par
    )
    tail = tail * dt
    keep = enter[R - 1 : R]
    b_t = b.T.astype(BF16)
    squares = jnp.zeros((R, R), F32)
    for p in range(3):
        h0, h1 = 2 * p, 2 * p + 1
        cols = slice(128 * p, 128 * p + 128)
        xp = act[:, cols]
        xb = xp.astype(BF16)
        sp = state[:, cols]
        st_o[:, cols] = sp.astype(BF16)

        def weights(h):
            gap = jnp.minimum(cum[:, h : h + 1] - cum_t[h : h + 1], 0.0)
            return (inner * jnp.exp(gap) * dt_t[h : h + 1]).astype(BF16)

        y = jnp.where(half, dot_nn(weights(h0), xb), dot_nn(weights(h1), xb))
        y = y + dot_nn(cb, sp.astype(BF16)) * jnp.where(
            half, enter[:, h0 : h0 + 1], enter[:, h1 : h1 + 1]
        )
        y = y + skip[0:1, cols] * xp
        y_o[:, cols] = y.astype(BF16)
        tp = jnp.where(half, tail[:, h0 : h0 + 1], tail[:, h1 : h1 + 1])
        kp = jnp.where(half[0:1], keep[:, h0 : h0 + 1], keep[:, h1 : h1 + 1])
        state[:, cols] = kp * sp + dot_nn(b_t, (tp * xp).astype(BF16))
        z = pa[:, 128 + 128 * p : 256 + 128 * p].astype(F32)
        u = y * z * jax.nn.sigmoid(z)
        squares = squares + u * u
    q = pa[:, 0:128].astype(F32)
    q_o[...] = (q * cos + partner(q, lane) * sin).astype(BF16)
    kv = ps[:, 0:128].astype(F32)
    kv_o[...] = jnp.where(half, kv * cos + partner(kv, lane) * sin, kv).astype(BF16)
    return dot_nt(jnp.ones((8, R), F32), squares, precision=EXACT)[0:1]


def ssm_fwd_kernel(
    rank, pa0, pa1, raw0, raw1, ps0, ps1, tok_r, seg_r, cos_r, sin_r, taps, par, skip,
    y0, y1, pre0, pre1, st_o, sq_o, q_o, kv_o, state, hist,
):
    i = pl.program_id(0)

    @pl.when(i == 0)
    def _():
        state[...] = jnp.zeros_like(state)
        hist[...] = jnp.zeros_like(hist)

    halves = ((pa0, raw0, ps0, y0, pre0), (pa1, raw1, ps1, y1, pre1))
    for half, (pa, raw, ps, y_o, pre_o) in enumerate(halves):
        rows = slice(half * R, (half + 1) * R)
        at = pl.multiple_of(half * QUARTERS * R + i * R, R)
        sq_o[:, pl.ds(at, R)] = ssm_fwd_chunk(
            pa, raw, ps, tok_r[rows], seg_r[0:1, rows], cos_r[rows], sin_r[rows], taps, par, skip,
            y_o, pre_o, st_o.at[half], q_o.at[rows], kv_o.at[rows], state, hist,
        )


def wire(width, reverse=False):
    def at(i, rank):
        i = QUARTERS - 1 - i if reverse else i
        return (block_of(i, rank[0]), 0)

    return pl.BlockSpec((R, width), at)


def in_order(shape, dim=0, reverse=False):
    def at(i, rank):
        i = QUARTERS - 1 - i if reverse else i
        return tuple(i if d == dim else 0 for d in range(len(shape)))

    return pl.BlockSpec(shape, at)


def ssm_forward(rank, pa, raw, ps, tok, seg_rows, cos, sin, taps, par, skip):
    n = QUARTERS * R
    t = 2 * n
    return pl.pallas_call(
        ssm_fwd_kernel,
        grid_spec=pltpu.PrefetchScalarGridSpec(
            num_scalar_prefetch=1,
            grid=(QUARTERS,),
            in_specs=[
                wire(896), wire(896), wire(128), wire(128), wire(384), wire(384),
                in_order((2 * R, 8)), in_order((8, 2 * R), 1),
                in_order((2 * R, 128)), in_order((2 * R, 128)), whole((8, 640)), whole((8, 128)), whole((8, 384)),
            ],
            out_specs=[
                wire(384), wire(384), wire(640), wire(640), in_order((2, NS, 384)), whole((1, t)),
                in_order((2 * R, 128)), in_order((2 * R, 128)),
            ],
            scratch_shapes=[pltpu.VMEM((NS, 384), F32), pltpu.VMEM((8, 640), F32)],
        ),
        out_shape=[
            sds((n, 384), BF16), sds((n, 384), BF16), far_out((n, 640), BF16), far_out((n, 640), BF16),
            far_out((2 * QUARTERS, NS, 384), BF16), sds((1, t), F32), sds((t, 128), BF16), sds((t, 128), BF16),
        ],
        compiler_params=pltpu.CompilerParams(
            dimension_semantics=("arbitrary",), vmem_limit_bytes=VMEM_BYTES
        ),
        cost_estimate=pl.CostEstimate(
            flops=4 * 10**9, bytes_accessed=20 * 2**20, transcendentals=3 * 10**6
        ),
        name="ssm_forward",
    )(rank, *pa, *raw, *ps, tok, seg_rows, cos, sin, taps, par, skip)


def ssm_bwd_chunk(
    pa, raw, ps, pre_r, y_r, st_r, dyn_r, r2, coef, dq, dkv, tok, seg_row, taps, par, skip, gain,
    da_o, ds_o, gt_o, gc_o, gh_o, dstate, nxt, own_first,
):
    row, lane = iota((R, R), 0), iota((R, R), 1)
    half = lane < PH
    sub = iota((8, R), 0)
    pre = pre_r[...].astype(F32)
    sg = jax.nn.sigmoid(pre)
    act = pre * sg
    b, c, bb, cb, dt, cum, cum_t, dt_t, okay, inner, enter, tail = chunk_terms(
        act, raw[...], tok, seg_row, par
    )
    tail_dt = tail * dt
    keep = enter[R - 1 : R]
    c_t = c.T.astype(BF16)
    db = jnp.zeros((R, R), F32)
    dc = jnp.zeros((R, R), F32)
    dinner = jnp.zeros((R, R), F32)
    dcum = jnp.zeros((R, R), F32)
    extra = jnp.zeros((R, R), F32)
    col_sum = jnp.zeros((8, R), F32)
    last_row = jnp.zeros((1, R), F32)
    dx_parts = []
    for p in range(3):
        cols = slice(128 * p, 128 * p + 128)
        z = pa[:, 128 + 128 * p : 256 + 128 * p].astype(F32)
        y, dyn = y_r[:, cols].astype(F32), dyn_r[:, cols]
        zs = jax.nn.sigmoid(z)
        sz = z * zs
        u = y * sz
        dn = dyn * r2
        gc_o[0:1, cols] += jnp.sum(dn * u, axis=0, keepdims=True)
        du = gain[0:1, cols] * dn - u * coef
        da_o[:, 128 + 128 * p : 256 + 128 * p] = (
            du * y * zs * (1.0 + z * (1.0 - zs))
        ).astype(BF16)
        dy = du * sz
        dyb = dy.astype(BF16)
        xp = act[:, cols]
        xb = xp.astype(BF16)
        gc_o[1:2, cols] += jnp.sum(dy * xp, axis=0, keepdims=True)
        sb = st_r[:, cols]
        sp = sb.astype(F32)
        dsp = dstate[:, cols]
        dsb = dsp.astype(BF16)
        h0, h1 = 2 * p, 2 * p + 1
        ep = jnp.where(half, enter[:, h0 : h0 + 1], enter[:, h1 : h1 + 1])
        tp = jnp.where(half, tail_dt[:, h0 : h0 + 1], tail_dt[:, h1 : h1 + 1])
        kp = jnp.where(half[0:1], keep[:, h0 : h0 + 1], keep[:, h1 : h1 + 1])
        cdb = (ep * dy).astype(BF16)
        through = dy * ep * dot_nn(cb, sb)
        bds = dot_nn(bb, dsb)
        qx = xp * bds
        kept = jnp.sum(dsp * sp, axis=0, keepdims=True) * kp
        dxi = []
        for h in (h0, h1):
            mine = half if h == h0 else ~half
            gap = jnp.minimum(cum[:, h : h + 1] - cum_t[h : h + 1], 0.0)
            decay = jnp.where(okay, jnp.exp(gap), 0.0)
            dt_row = dt_t[h : h + 1]
            dg = dot_nt(jnp.where(mine, dy, 0.0).astype(BF16), xb)
            t1 = dg * decay
            dinner = dinner + t1 * dt_row
            w0 = t1 * inner
            col_sum = col_sum + jnp.where(sub == h, jnp.sum(w0, axis=0, keepdims=True), 0.0)
            w1 = w0 * dt_row + jnp.where(mine, through, 0.0)
            dcum = dcum + jnp.where(lane == h, jnp.sum(w1, axis=1, keepdims=True), 0.0)
            e = jnp.sum(jnp.where(mine, qx, 0.0), axis=1, keepdims=True)
            extra = extra + jnp.where(lane == h, e, 0.0)
            k = jnp.sum(jnp.where(mine[0:1], kept, 0.0), axis=1, keepdims=True)
            last_row = last_row + jnp.where(lane[0:1] == h, k, 0.0)
            dxi.append(dot_tn((decay * inner * dt_row).astype(BF16), dyb))
        dx_parts.append(jnp.where(half, dxi[0], dxi[1]) + tp * bds + skip[0:1, cols] * dy)
        dc = dc + dot_nt(cdb, sb)
        db = db + dot_nt((tp * xp).astype(BF16), dsb)
        dstate[:, cols] = kp * dsp + dot_nn(c_t, cdb)
    col_sum = jnp.concatenate([col_sum, jnp.zeros((R - 8, R), F32)], axis=0).T
    moved = tail_dt * extra
    last_row = last_row + jnp.sum(moved, axis=0, keepdims=True)
    dcum = dcum - col_sum * dt - moved + jnp.where(row == R - 1, last_row, 0.0)
    dlog = dot_nn((row <= lane).astype(F32), dcum, precision=EXACT)
    ddt = col_sum + tail * extra + par[0:1] * dlog
    gh_o[0:1] += jnp.sum(dt * dlog, axis=0, keepdims=True)
    ddr = ddt * jax.nn.sigmoid(raw[...] + par[1:2])
    gh_o[1:2] += jnp.sum(ddr, axis=0, keepdims=True)
    da_o[:, 896:1024] = ddr.astype(BF16)
    dib = dinner.astype(BF16)
    dc = dc + dot_nn(dib, bb)
    db = db + dot_tn(dib, cb)
    dact = jnp.concatenate([*dx_parts, db, dc], axis=1)
    dpre = dact * sg * (1.0 + pre * (1.0 - sg))
    xin = jnp.concatenate([pa[:, 512:896], ps[:, 128:384]], axis=1).astype(F32)
    dxin = dpre * taps[3:4]
    gt_o[3:4] += jnp.sum(dpre * xin, axis=0, keepdims=True)
    gt_o[4:5] += jnp.sum(dpre, axis=0, keepdims=True)
    for k in (1, 2, 3):
        zk = dpre * tok[:, k - 1 : k]
        later = nxt.at[k - 1]
        moved_up = jnp.concatenate([zk, later[...]], axis=0)[k : k + R]
        later[...] = zk[0:8]
        dxin = dxin + moved_up * taps[3 - k : 4 - k]
        gt_o[3 - k : 4 - k] += jnp.sum(moved_up * xin, axis=0, keepdims=True)
    da_o[:, 512:896] = dxin[:, 0:384].astype(BF16)
    ds_o[:, 256:512] = dxin[:, 384:640].astype(BF16)
    da_o[:, 0:128] = dq
    other = pltpu.roll(dkv, HD, 1)
    mine = half == own_first
    ds_o[:, 0:128] = jnp.where(mine, jnp.where(half, dkv, other), 0.0).astype(BF16)
    ds_o[:, 128:256] = jnp.where(mine, jnp.where(half, other, dkv), 0.0).astype(BF16)


def ssm_bwd_kernel(
    rank, oh, pa0, pa1, raw0, raw1, ps0, ps1, pre0, pre1, y0, y1, st_r, dyn0, dyn1, fac_r, coef_r, dq_r, dkv_r,
    tok_r, seg_r, taps, par, skip, gain,
    da0, da1, ds0, ds1, gt_o, gc_o, gh_o, dstate, nxt,
):
    i = pl.program_id(0)

    @pl.when(i == 0)
    def _():
        dstate[...] = jnp.zeros_like(dstate)
        nxt[...] = jnp.zeros_like(nxt)
        gt_o[...] = jnp.zeros_like(gt_o)
        gc_o[...] = jnp.zeros_like(gc_o)
        gh_o[...] = jnp.zeros_like(gh_o)

    quarter = QUARTERS - 1 - i
    halves = (
        (pa0, raw0, ps0, pre0, y0, dyn0, da0, ds0),
        (pa1, raw1, ps1, pre1, y1, dyn1, da1, ds1),
    )
    for half in (1, 0):
        pa, raw, ps, pre, y, dyn, da, ds = halves[half]
        rows = slice(half * R, (half + 1) * R)
        start = half * QUARTERS * R + quarter * R
        ssm_bwd_chunk(
            pa, raw, ps, pre, y, st_r.at[half], dyn, column(fac_r, start), column(coef_r, start),
            dq_r[rows], dkv_r[rows].astype(F32), tok_r[rows], seg_r[0:1, rows], taps, par, skip, gain,
            da, ds, gt_o, gc_o, gh_o, dstate, nxt, oh[0] == 0,
        )


def ssm_backward(
    rank, oh, pa, raw, ps, pre, y, states, dyn, fac, coef, dq, dkv, tok, seg_rows, taps, par, skip, gain
):
    n = QUARTERS * R
    t = 2 * n
    back = {"reverse": True}
    return pl.pallas_call(
        lambda r, *refs: ssm_bwd_kernel(r, *refs),
        grid_spec=pltpu.PrefetchScalarGridSpec(
            num_scalar_prefetch=1,
            grid=(QUARTERS,),
            in_specs=[
                SCALAR, wire(896, **back), wire(896, **back), wire(128, **back), wire(128, **back),
                wire(384, **back), wire(384, **back),
                wire(640, **back), wire(640, **back), wire(384, **back), wire(384, **back),
                in_order((2, NS, 384), **back), wire(384, **back), wire(384, **back),
                whole((1, t)), whole((1, t)), in_order((2 * R, 128), **back), in_order((2 * R, 128), **back),
                in_order((2 * R, 8), **back), in_order((8, 2 * R), 1, **back),
                whole((8, 640)), whole((8, 128)), whole((8, 384)), whole((8, 384)),
            ],
            out_specs=[
                wire(1024, **back), wire(1024, **back), wire(512, **back), wire(512, **back),
                whole((8, 640)), whole((8, 384)), whole((8, 128)),
            ],
            scratch_shapes=[pltpu.VMEM((NS, 384), F32), pltpu.VMEM((3, 8, 640), F32)],
        ),
        out_shape=[
            far_out((n, 1024), BF16), far_out((n, 1024), BF16), far_out((n, 512), BF16), far_out((n, 512), BF16),
            sds((8, 640), F32), sds((8, 384), F32), sds((8, 128), F32),
        ],
        compiler_params=pltpu.CompilerParams(
            dimension_semantics=("arbitrary",), vmem_limit_bytes=VMEM_BYTES
        ),
        cost_estimate=pl.CostEstimate(
            flops=8 * 10**9, bytes_accessed=30 * 2**20, transcendentals=4 * 10**6
        ),
        name="ssm_backward",
    )(
        rank, oh, *hbm(pa), *hbm(raw), *hbm(ps), *hbm(pre), *hbm(y), hbm(states), *hbm(dyn), fac, coef, dq, dkv, tok, seg_rows, taps, par, skip, gain
    )


def head_views(kv, lane):
    zero = jnp.zeros_like(kv)
    left = lane < HD
    k0 = jnp.where(left, kv, zero)
    v1 = jnp.where(left, zero, kv)
    k1 = pltpu.roll(k0.astype(F32), HD, 1).astype(BF16)
    v0 = pltpu.roll(v1.astype(F32), HD, 1).astype(BF16)
    return (k0, k1), (v0, v1)


def allowed_keys(tok_r, seg_r, start, rows, keys):
    return (iota((rows, keys), 1) <= start + iota((rows, keys), 0)) & (
        tok_r[start : start + rows, 5:6] == seg_r[0:1, 0:keys]
    )


def attend_fwd_kernel(rank, q_r, kv_r, tok_r, seg_r, o0, o1, lse_o):
    n = q_r.shape[0]
    ks, vs = head_views(kv_r[...], iota((n, 2 * HD), 1))
    lane = iota((2 * R, 128), 1)
    for quarter in range(QUARTERS):
        start, keys = quarter * 2 * R, (quarter + 1) * 2 * R
        q = q_r[start:keys]
        okay = allowed_keys(tok_r, seg_r, start, 2 * R, keys)
        out = jnp.zeros((2 * R, 2 * HD), F32)
        stats = []
        for h in range(2):
            s = jnp.where(okay, dot_nt(q, ks[h][0:keys]) * HD**-0.5, NEG)
            top = jnp.max(s, axis=1, keepdims=True)
            e = jnp.exp(s - top)
            total = jnp.sum(e, axis=1, keepdims=True)
            out = out + dot_nn((e * (1.0 / total)).astype(BF16), vs[h][0:keys])
            stats.append(top + jnp.log(total))
        at = pl.ds(pl.multiple_of(block_of(quarter, rank[0]) * R, R), R)
        o0[at] = out[0:R].astype(BF16)
        o1[at] = out[R:].astype(BF16)
        lse_o[start:keys] = jnp.where(lane == 0, stats[0], stats[1])


def attend_bwd_kernel(
    rank, q_r, kv_r, do0, do1, lse_r, tok_r, seg_r, cos_r, sin_r, dq_o, dkv_o, dk_acc, dv_acc
):
    n = q_r.shape[0]
    ks, vs = head_views(kv_r[...], iota((n, 2 * HD), 1))
    lane = iota((2 * R, 128), 1)
    left = lane < HD
    dk_acc[...] = jnp.zeros_like(dk_acc)
    dv_acc[...] = jnp.zeros_like(dv_acc)
    for quarter in range(QUARTERS):
        start, keys = quarter * 2 * R, (quarter + 1) * 2 * R
        q = q_r[start:keys]
        at = pl.ds(pl.multiple_of(block_of(quarter, rank[0]) * R, R), R)
        do = jnp.concatenate([do0[at], do1[at]], axis=0)
        okay = allowed_keys(tok_r, seg_r, start, 2 * R, keys)
        lse = lse_r[start:keys]
        zero = jnp.zeros_like(q)
        dq = jnp.zeros((2 * R, 2 * HD), F32)
        for h in range(2):
            mine = left if h == 0 else ~left
            s = dot_nt(q, ks[h][0:keys]) * HD**-0.5
            p = jnp.where(okay, jnp.exp(s - lse[:, h : h + 1]), 0.0)
            dp = dot_nt(do, vs[h][0:keys])
            dot_sum = jnp.sum(p * dp, axis=1, keepdims=True)
            ds = (p * (dp - dot_sum)).astype(BF16)
            dq = dq + dot_nn(ds, ks[h][0:keys])
            dk_acc[0:keys] += dot_tn(ds, jnp.where(mine, q, zero))
            dv_acc[0:keys] += dot_tn(p.astype(BF16), jnp.where(mine, do, zero))
        dq = dq * HD**-0.5
        dq_o[start:keys] = (
            dq * cos_r[start:keys] - partner(dq, lane) * sin_r[start:keys]
        ).astype(BF16)
    for start in range(0, n, 2 * R):
        rows = slice(start, start + 2 * R)
        dk, dv = dk_acc[rows], dv_acc[rows]
        dk = (dk + pltpu.roll(dk, HD, 1)) * HD**-0.5
        dv = dv + pltpu.roll(dv, HD, 1)
        dk = dk * cos_r[rows] - partner(dk, lane) * sin_r[rows]
        dkv_o[rows] = jnp.where(left, dk, dv).astype(BF16)


def attend_forward(rank, q, kv, tok, seg_rows):
    t = q.shape[0]
    return call(
        attend_fwd_kernel,
        "attend_forward",
        [SCALAR, whole((t, 128)), whole((t, 128)), whole((t, 8)), whole((8, t))],
        [sds((t // 2, 128), BF16), sds((t // 2, 128), BF16), far_out((t, 128), F32)],
        2 * 10**9,
    )(rank, q, kv, tok, seg_rows)


def attend_backward(rank, q, kv, do, lse, tok, seg_rows, cos, sin, deps=()):
    t = q.shape[0]
    full = whole((t, 128))
    return call(
        attend_bwd_kernel,
        "attend_backward",
        [SCALAR, full, full, whole((t // 2, 128)), whole((t // 2, 128)), full,
         whole((t, 8)), whole((8, t)), full, full],
        [sds((t, 128), BF16), sds((t, 128), BF16)],
        4 * 10**9,
        [pltpu.VMEM((t, 128), F32), pltpu.VMEM((t, 128), F32)],
        deps,
    )(rank, hbm(q), hbm(kv), *do, hbm(lse), tok, seg_rows, cos, sin)


def swap(values, axis, distance):
    size = lax.axis_size(axis)
    return lax.ppermute(values, axis, [(i, i ^ distance) for i in range(size)])


def bits_of(axis):
    size = lax.axis_size(axis)
    return [1 << b for b in range(size.bit_length() - 1)]


def sum_over(values, axes):
    for axis in axes:
        for bit in bits_of(axis):
            values = values + swap(values, axis, bit)
    return values


def sum_rows(values):
    return values + sum(swap(values, "tensor", d) for d in (1, 2, 3))


def gather_half(own):
    far = swap(own, "tensor", 2)
    near = swap(own, "tensor", 1)
    return near, swap(far, "tensor", 1), own, far


def scatter_half(send, keep, on_the_way):
    got = swap(send, "tensor", 1)
    given = (keep[R:].astype(F32) + got[R:].astype(F32)).astype(BF16)
    on_the_way.append(given)
    return keep, got, swap(given, "tensor", 2)


def gather_everywhere(own):
    held = own[:, None]
    for axis in ("dp", "tensor"):
        place = lax.axis_index(axis)
        for bit in bits_of(axis):
            upper = (place & bit) != 0
            other = swap(held, axis, bit)
            low, high = jnp.where(upper, other, held), jnp.where(upper, held, other)
            held = jnp.concatenate([low, high], axis=0 if axis == "dp" else 1)
    return held.reshape(-1, *own.shape[1:])


def gather_dp(v):
    return lax.all_gather(v, "dp", axis=0, tiled=True)


def scatter_dp(v):
    return lax.psum_scatter(v, "dp", scatter_dimension=0, tiled=True)


def pairs_of_dp(share):
    size = lax.axis_size("dp")
    return share % 128 == 0 and size % 2 == 0 and size >= 4


def merge_kernel(a, b, o):
    o[...] = (a[...].astype(F32) + b[...].astype(F32)).astype(BF16)


def merge(a, b, deps):
    return call(merge_kernel, "merge", [whole(a.shape)] * 2, [far_out(a.shape, BF16)], 10**6, deps=deps)(
        hbm(a), hbm(b)
    )[0]


def scatter_lines(v):
    size = lax.axis_size("dp")
    lines = [[i for i in range(size) if i % 2 == s] for s in range(2)]
    return lax.psum_scatter(v, "dp", scatter_dimension=0, tiled=True, axis_index_groups=lines)


def pad_rows(v, rows=8):
    return jnp.pad(v, ((0, rows - v.shape[0]), (0, 0)))


def body(
    inputs, cotangent, segment_ids, norm_gains, w_query, key_value_weight, w_gate_in, w_state_in,
    w_step, ssm_channel, conv_state, head_params, w_attn_out, w_ssm_out, w_gate_up, w_down,
):
    width = inputs.shape[2]
    n = segment_ids.shape[1]
    tp_size = lax.axis_size("tensor")
    tensor = lax.axis_index("tensor")
    slot = lax.axis_index("dp") * tp_size + tensor
    kv_cols = key_value_weight.shape[2]
    kv_heads = kv_cols // (2 * HD)
    own_head = tensor * (w_query.shape[2] // HD) // (HQ // kv_heads)
    ssm_heads = w_step.shape[2]
    channels = ssm_heads * PH
    hidden = w_gate_up.shape[3]
    depth = w_query.shape[1]
    rank = tensor.reshape(1).astype(jnp.int32)
    oh = own_head.reshape(1).astype(jnp.int32)

    halves = [inputs[0, :R], inputs[0, R:]]
    x_pieces = [gather_half(v) for v in halves]

    shared = jnp.concatenate([key_value_weight, w_state_in], axis=2)
    sq, wide = shared.shape[1:]
    shares = [
        shared[layer].reshape(sq, wide // 128, 128).swapaxes(0, 1).reshape(depth, 128)
        for layer in range(LAYERS)
    ]

    def exchange(share):
        far = swap(share, "tensor", 2)
        return share, swap(share, "tensor", 1), far, swap(far, "tensor", 1)

    w_first, w_second, w_shared = [], [], []
    for layer in range(LAYERS):
        first = [
            w_query[layer],
            w_gate_in[layer].reshape(depth, 2 * channels),
            jnp.pad(w_step[layer], ((0, 0), (0, 128 - ssm_heads))),
            w_attn_out[layer].T,
            w_ssm_out[layer].T,
        ]
        second = [w_gate_up[layer].reshape(depth, 2 * hidden), w_down[layer].T]
        first = gather_dp(jnp.concatenate(first + (shares if layer == 0 else []), axis=1))
        if layer == 0:
            w_shared = [exchange(first[:, c : c + 128]) for c in range(1536, 1536 + 128 * LAYERS, 128)]
        w_first.append(first)
        w_second.append(gather_dp(jnp.concatenate(second, axis=1)))

    small = jnp.concatenate([norm_gains.reshape(-1), conv_state.reshape(-1)])[None, :]
    small_all = gather_everywhere(small).astype(F32)
    gain_count = norm_gains.size
    gains = (
        small_all[:, :gain_count]
        .reshape(-1, LAYERS, 2, norm_gains.shape[2])
        .transpose(1, 2, 0, 3)
        .reshape(LAYERS, 2, width)
    )
    conv_flat = (
        small_all[:, gain_count : gain_count + conv_state.size]
        .reshape(-1, LAYERS, conv_state.shape[1])
        .transpose(1, 0, 2)
        .reshape(LAYERS, 5, 2 * NS)
    )

    seg = segment_ids[0]
    segf = seg.astype(F32)
    index = jnp.arange(n, dtype=jnp.int32)
    places = index - jnp.sum((seg[None, :] < seg[:, None]).astype(jnp.int32), axis=1)
    freq = ROPE_BASE ** (-jnp.arange(HD // 2, dtype=F32) / (HD // 2))
    angle = places.astype(F32)[:, None] * freq[None, :]
    cos_one, sin_one = jnp.cos(angle), jnp.sin(angle)
    cos = jnp.concatenate([cos_one] * 4, axis=1)
    sin = jnp.concatenate([-sin_one, sin_one] * 2, axis=1)
    shifted = [
        (jnp.pad(seg, (k, 0), constant_values=-1)[:n] == seg).astype(F32) for k in (1, 2, 3)
    ]
    ends = seg.reshape(-1, R)[:, -1]
    before = jnp.concatenate([jnp.full((1,), -1, jnp.int32), ends[:-1]])
    enters = (seg.reshape(-1, R) == before[:, None]).astype(F32).reshape(-1)
    leaves = (seg.reshape(-1, R) == ends[:, None]).astype(F32).reshape(-1)
    tok = jnp.stack([*shifted, enters, leaves, segf, segf, segf], axis=1)
    seg_rows = jnp.broadcast_to(segf[None, :], (8, n))

    residual, last_parts, sent_on = halves, [], []
    pieces = x_pieces
    saved = []
    for layer in range(LAYERS):
        channel, head = ssm_channel[layer], head_params[layer]
        taps = pad_rows(jnp.concatenate([channel[:5], conv_flat[layer]], axis=1))
        rate = -jnp.exp(head[0])
        par = pad_rows(jnp.pad(jnp.stack([rate, head[1]]), ((0, 0), (0, 128 - ssm_heads))))
        skip = pad_rows(jnp.repeat(head[2], PH)[None, :])
        gain_row = pad_rows(channel[5:6])
        gain_one = pad_rows(gains[layer, 0:1])
        gain_two = pad_rows(gains[layer, 1:2])
        wf, ws, wh = w_first[layer], w_second[layer], w_shared[layer]
        ins = functools.partial(project_in, layer == 0, depth, rank, oh)
        w_all, *half_0 = ins(pieces[0], gain_one, wf, wh)
        w_shared[layer] = w_all
        h, pa, raw, ps = zip(half_0, ins(pieces[1], gain_one, wf, w_all))
        y0, y1, pre0, pre1, states, sq, q_rot, kv_rot = ssm_forward(
            rank, pa, raw, ps, tok, seg_rows, cos, sin, taps, par, skip
        )
        y, pre = (y0, y1), (pre0, pre1)
        total = sum_rows(sq)
        o0, o1, lse = attend_forward(rank, q_rot, kv_rot, tok, seg_rows)
        factor = lax.rsqrt(total / (HS * PH) + EPS)
        mixed, middle, h2, gu, act, result, pieces = [], [], [], [], [], [], []
        parts = []
        for i, o in enumerate((o0, o1)):
            m, send, keep = mix(i, rank, o, y[i], pa[i], factor, gain_row, wf)
            mixed.append(m)
            parts.append(scatter_half(send, keep, sent_on))
        gathered = []
        for i in range(2):
            x1, low = take_step(residual[i], *parts[i], gain_two)
            middle.append(x1)
            gathered.append(gather_half(low))
        parts = []
        for i in range(2):
            h2_i, gu_i, act_i, send, keep = ffn(gathered[i], ws)
            h2.append(h2_i)
            gu.append(gu_i)
            act.append(act_i)
            parts.append(scatter_half(send, keep, sent_on))
        for i in range(2):
            if layer + 1 < LAYERS:
                x2, low = take_step(middle[i], *parts[i], pad_rows(gains[layer + 1, 0:1]))
                result.append(x2)
                pieces.append(gather_half(low))
            else:
                last_parts.append((middle[i], *parts[i], None))
        saved.append(
            (residual, middle, h, pa, raw, ps, y, pre, states, q_rot, kv_rot, lse, factor, mixed, h2, gu, act,
             taps, par, skip, gain_row, gain_one, gain_two, rate)
        )
        residual = result

    grad = [cotangent[0, :R], cotangent[0, R:]]
    low = list(grad)
    big, small_grads = [None] * LAYERS, [None] * LAYERS
    for layer in reversed(range(LAYERS)):
        (first_in, middle, h, pa, raw, ps, y, pre, states, q_rot, kv_rot, lse, factor, mixed, h2, gu, act,
         taps, par, skip, gain_row, gain_one, gain_two, rate) = saved[layer]
        wf, ws, wh = w_first[layer], w_second[layer], w_shared[layer]
        gathered = [gather_half(v) for v in low]
        df, dgu, dm, do, dyn, cross, parts = [], [], [], [], [], [], []
        deps = (big[layer + 1][0],) if layer + 1 < LAYERS else ()
        for i in range(2):
            df_i, dgu_i, send, keep = ffn_back(gathered[i], gu[i], ws, deps)
            df.append(df_i)
            dgu.append(dgu_i)
            parts.append(scatter_half(send, keep, sent_on))
        groups = [(h2, dgu), (df, act)]
        paired = layer == 0 and pairs_of_dp(depth)
        if paired:
            side = (lax.axis_index("dp") % 2).reshape(1).astype(jnp.int32)
            given = weight_grads("grads_one_sent", groups, sent_on[-2:], depth, 1 - side)
            kept = weight_grads("grads_one_kept", groups, (given,), depth, side)
            sent = swap(given, "dp", 1)
            early = [(given,), (kept,)]
        else:
            g1 = weight_grads("grads_one", groups, sent_on[-2:])
            early = [(g1,), ()]
        gathered, dx1, dgain2, dgain1 = [], [], 0.0, 0.0
        for i in range(2):
            dx, low_i, gg = back_step(grad[i], middle[i], *parts[i], gain_two, early[i])
            dx1.append(dx)
            dgain2 = dgain2 + gg[0]
            gathered.append(gather_half(low_i))
        for i in range(2):
            dm_i, do_i, dyn_i, cross_i = mix_back(rank, gathered[i], y[i], pa[i], gain_row, wf)
            dm.append(dm_i)
            do.append(do_i)
            dyn.append(dyn_i)
            cross.append(cross_i)
        cross = sum_rows(jnp.concatenate(cross, axis=1))
        dq, dkv = attend_backward(
            rank, q_rot, kv_rot, do, lse, tok, seg_rows, cos, sin
        )
        coef = factor**3 * cross / (HS * PH)
        da0, da1, ds0, ds1, g_taps, g_chan, g_head = ssm_backward(
            rank, oh, pa, raw, ps, pre, y, states, dyn, factor, coef, dq, dkv, tok, seg_rows, taps, par, skip,
            gain_row,
        )
        groups = [(h, (da0, da1)), (dm, mixed)]
        shared_sum = shared_grads(depth, rank, h, (ds0, ds1))
        before = ()
        if layer == 0:
            g2 = weight_grads("grads_two", groups, (big[layer + 1][1],), room=128)
            if paired:
                g1 = scatter_lines(merge(kept, sent, tuple(do)))
                before = (g1,)
            g2 = insert_shared(g2, shared_sum, depth, before)
        sums = [project_in_back(da, ds, wf, wh) for da, ds in ((da0, ds0), (da1, ds1))]
        parts = [scatter_half(*v, sent_on) for v in sums]
        deps = ()
        if layer > 0:
            g2 = weight_grads("grads_two", groups, sent_on[-2:], room=128)
            g2 = insert_shared(g2, shared_sum, depth)
            deps = (g2,)
        grad, low = [], []
        for i in range(2):
            g, low_i, gg = back_step(dx1[i], first_in[i], *parts[i], gain_one, () if i else deps)
            grad.append(g)
            low.append(low_i)
            dgain1 = dgain1 + gg[0]
        chan_grad = jnp.concatenate([g_taps[:5, :channels], g_chan[0:1]], axis=0)
        head_grad = jnp.stack(
            [
                g_head[0, :ssm_heads] * rate,
                g_head[1, :ssm_heads],
                jnp.sum(g_chan[1].reshape(ssm_heads, PH), axis=1),
            ]
        )
        big[layer] = (g1 if paired else scatter_dp(g1), scatter_dp(g2))
        small_grads[layer] = (
            jnp.concatenate([dgain1, dgain2, g_taps[:5, channels:].reshape(-1)]),
            jnp.concatenate([chan_grad.reshape(-1), head_grad.reshape(-1)]),
        )
    input_grad = jnp.concatenate(grad, axis=0)
    output = jnp.concatenate([take_step(*v, (da0,)) for v in last_parts], axis=0)

    wide_small = jnp.concatenate([small_grads[l][0] for l in range(LAYERS)])
    local_small = jnp.concatenate([small_grads[l][1] for l in range(LAYERS)])
    total = sum_over(jnp.concatenate([wide_small, local_small])[None, :], ("dp",))[0]
    wide_small = sum_over(total[None, : wide_small.shape[0]], ("tensor",))[0]
    wide_small = wide_small.reshape(LAYERS, -1)
    local_small = total[wide_small.size :].reshape(LAYERS, -1)
    gain_share = norm_gains.shape[2]
    conv_share = conv_state.shape[1]
    grad_gains = lax.dynamic_slice_in_dim(
        wide_small[:, : 2 * width].reshape(LAYERS, 2, width), slot * gain_share, gain_share, 2
    )
    grad_conv = lax.dynamic_slice_in_dim(wide_small[:, 2 * width :], slot * conv_share, conv_share, 1)
    grad_channel = local_small[:, : 6 * channels].reshape(LAYERS, 6, channels)
    grad_head = local_small[:, 6 * channels :].reshape(LAYERS, 3, ssm_heads)

    gu, down, q, gate_in, step, attn, ssm, kv, state = finish(*zip(*big))
    return (
        output[None], input_grad[None], grad_gains, q, kv, gate_in.reshape(LAYERS, depth, 2, channels),
        state, step[:, :, :ssm_heads], grad_channel, grad_conv, grad_head, attn, ssm,
        gu.reshape(LAYERS, depth, 2, hidden), down,
    )


def solution(mesh):
    split = (
        P("dp", "tensor", None),
        P("dp", "tensor", None),
        P("dp", None),
        P(None, None, ("dp", "tensor")),
        P(None, "dp", "tensor"),
        P(None, ("dp", "tensor"), None),
        P(None, "dp", None, "tensor"),
        P(None, ("dp", "tensor"), None),
        P(None, "dp", "tensor"),
        P(None, None, "tensor"),
        P(None, ("dp", "tensor")),
        P(None, None, "tensor"),
        P(None, "tensor", "dp"),
        P(None, "tensor", "dp"),
        P(None, "dp", None, "tensor"),
        P(None, "tensor", "dp"),
    )
    out_split = split[:2] + split[3:]
    return jax.shard_map(body, mesh=mesh, in_specs=split, out_specs=out_split, check_vma=False)
```

```python
import functools

import jax
import jax.numpy as jnp
from jax import lax
from jax.experimental import pallas as pl
from jax.experimental.pallas import tpu as pltpu
from jax.sharding import PartitionSpec as P

HQ = 8
HD = 64
HS = 24
PH = 64
NS = 128
LAYERS = 2
EPS = 1e-05
ROPE_BASE = 100000000000.0
R = 128
QUARTERS = 4
DISTANCE = (1, 3, 0, 2)
F32 = jnp.float32
BF16 = jnp.bfloat16
EXACT = lax.Precision.HIGHEST
NEG = -1e30
VMEM_BYTES = 16 * 1024 * 1024
GRADS_BYTES = 24 * 1024 * 1024


def dot_nn(left, right, **kw):
    return lax.dot_general(
        left, right, (((1,), (0,)), ((), ())), preferred_element_type=F32, **kw
    )


def dot_nt(left, right, **kw):
    return lax.dot_general(
        left, right, (((1,), (1,)), ((), ())), preferred_element_type=F32, **kw
    )


def dot_tn(left, right, **kw):
    return lax.dot_general(
        left, right, (((0,), (0,)), ((), ())), preferred_element_type=F32, **kw
    )


def iota(shape, dim):
    return lax.broadcasted_iota(jnp.int32, shape, dim)


def softplus(v):
    return jnp.maximum(v, 0.0) + jnp.log1p(jnp.exp(-jnp.abs(v)))


def partner(v, lane):
    return jnp.where(lane % HD < HD // 2, pltpu.roll(v, 96, 1), pltpu.roll(v, 32, 1))


def block_of(quarter, rank):
    k = quarter ^ rank
    return 2 - 2 * (k & 1) + (k >> 1)


def sds(shape, dtype):
    return jax.ShapeDtypeStruct(shape, dtype)


def whole(shape, *at):
    at = at or (0,) * len(shape)
    return pl.BlockSpec(shape, lambda *_: at, pipeline_mode=pl.Buffered(1))


def hbm(v):
    return jax.tree.map(lambda x: pltpu.with_memory_space_constraint(x, pltpu.HBM), v)


def far_out(shape, dtype):
    return pltpu.HBM(shape, dtype)


def bytes_of(made):
    size = made.dtype.itemsize
    for d in made.shape:
        size *= d
    return size


SCALAR = pl.BlockSpec(memory_space=pltpu.SMEM)


def call(kernel, name, in_specs, out_shapes, flops, scratch=(), deps=(), vmem=VMEM_BYTES):
    if deps:
        base, skipped = kernel, range(len(in_specs), len(in_specs) + len(deps))

        def kernel(*refs):
            base(*(r for i, r in enumerate(refs) if i not in skipped))

        in_specs = list(in_specs) + [pl.BlockSpec(memory_space=pl.ANY)] * len(deps)
    many = sum(bytes_of(s) for s in out_shapes)
    made = pl.pallas_call(
        kernel,
        grid=(1,),
        in_specs=in_specs,
        out_specs=[whole(s.shape) for s in out_shapes],
        out_shape=out_shapes,
        scratch_shapes=list(scratch),
        compiler_params=pltpu.CompilerParams(
            dimension_semantics=("arbitrary",), vmem_limit_bytes=vmem
        ),
        cost_estimate=pl.CostEstimate(
            flops=int(flops), bytes_accessed=2 * many, transcendentals=10**5
        ),
        name=name,
    )
    return lambda *args: made(*args, *deps)


def rms(v, gain):
    return v * lax.rsqrt(jnp.mean(v * v, axis=-1, keepdims=True) + EPS) * gain


def rms_back(v, gain, grad):
    factor = lax.rsqrt(jnp.mean(v * v, axis=-1, keepdims=True) + EPS)
    weighted = grad * gain
    inner = jnp.mean(weighted * v, axis=-1, keepdims=True)
    scaled = v * factor
    return (
        factor * weighted - scaled * (factor * factor * inner),
        jnp.sum(grad * scaled, axis=0, keepdims=True),
    )


def step_kernel(x, keep, got, far, gain, x_o, h_o):
    total = keep[...].astype(F32) + got[...].astype(F32) + far[...].astype(F32)
    new = x[...].astype(F32) + total
    x_o[...] = new.astype(x_o.dtype)
    if h_o is not None:
        h_o[...] = rms(new, gain[0:1]).astype(BF16)


def last_kernel(x, keep, got, far, x_o):
    step_kernel(x, keep, got, far, None, x_o, None)


def take_step(x, keep, got, far, gain, deps=()):
    w = x.shape[1]
    specs = [whole((R, w))] * 4
    if gain is None:
        return call(last_kernel, "last_step", specs, [sds((R, w), BF16)], 10**6, deps=deps)(
            hbm(x), *hbm((keep, got, far))
        )[0]
    return call(
        step_kernel, "step", specs + [whole((8, w))], [far_out((R, w), F32), sds((R, w), BF16)], 10**6
    )(hbm(x), *hbm((keep, got, far)), gain)


def back_step_kernel(g, v, keep, got, far, gain, g_o, low_o, gg_o):
    grad = keep[...].astype(F32) + got[...].astype(F32) + far[...].astype(F32)
    through, gg = rms_back(v[...].astype(F32), gain[0:1], grad)
    new = g[...].astype(F32) + through
    g_o[...] = new
    low_o[...] = new.astype(BF16)
    gg_o[...] = jnp.broadcast_to(gg, gg_o.shape)


def back_step(g, v, keep, got, far, gain, deps=()):
    w = v.shape[1]
    return call(
        back_step_kernel,
        "back_step",
        [whole((R, w))] * 5 + [whole((8, w))],
        [far_out((R, w), F32), sds((R, w), BF16), sds((8, w), F32)],
        10**6,
        deps=deps,
    )(hbm(g), hbm(v), *hbm((keep, got, far)), gain)


def input_kernel(first, depth, rank, oh, p0, p1, p2, p3, gain, w_in, *refs):
    shares, outs = refs[: len(refs) - 4], refs[len(refs) - 4 :]
    h_o, pa_o, dt_o, ps_o = outs
    if len(shares) > 1:
        *shares, w_sh = shares
        sq = depth // QUARTERS
        for distance, share in enumerate(shares):
            for dp in range(share.shape[0] // depth):
                at = pl.multiple_of(dp * depth + (rank[0] ^ distance) * sq, sq)
                for c in range(QUARTERS):
                    rows = slice(dp * depth + c * sq, dp * depth + (c + 1) * sq)
                    w_sh[pl.ds(at, sq), 128 * c : 128 * c + 128] = share[rows]
    else:
        w_sh = shares[0]
    h = jnp.concatenate([p0[...], p1[...], p2[...], p3[...]], axis=0)
    if first:
        h = rms(h.astype(F32), gain[0:1]).astype(BF16)
    h_o[...] = h
    pa = dot_nn(h, w_in[...])
    pa_o[...] = pa[:, 0:896].astype(BF16)
    dt_o[...] = pa[:, 896:1024]
    ps = dot_nn(h, w_sh[...])
    k, v = ps[:, 0:128], ps[:, 128:256]
    left = iota(k.shape, 1) < HD
    is_first = oh[0] == 0
    k = jnp.where(is_first, k, pltpu.roll(k, HD, 1))
    v = jnp.where(is_first, pltpu.roll(v, HD, 1), v)
    ps_o[:, 0:128] = jnp.where(left, k, v).astype(BF16)
    ps_o[:, 128:384] = ps[:, 256:512].astype(BF16)


def project_in(first, depth, rank, oh, pieces, gain, w_in, w_sh):
    w = pieces[0].shape[1]
    n = QUARTERS * R
    shares = w_sh if isinstance(w_sh, tuple) else (w_sh,)
    outs = [far_out((n, w), BF16), sds((n, 896), BF16), sds((n, 128), F32), sds((n, 384), BF16)]
    if len(shares) > 1:
        outs = [sds((w, 512), BF16)] + outs
    return call(
        functools.partial(input_kernel, first, depth),
        "project_in",
        [SCALAR, SCALAR] + [whole((R, w))] * 4 + [whole((8, w)), whole((w, 1024))]
        + [whole(v.shape) for v in shares],
        outs,
        2 * n * w * 1536,
    )(rank, oh, *hbm(pieces), gain, w_in, *shares)


def input_back_kernel(da, ds, w_in, w_sh, send, keep):
    dh = (dot_nt(da[...], w_in[...]) + dot_nt(ds[...], w_sh[...])).astype(BF16)
    send[...] = dh[0 : 2 * R]
    keep[...] = dh[2 * R :]


def project_in_back(da, ds, w_in, w_sh, deps=()):
    n, w = da.shape[0], w_in.shape[0]
    return call(
        input_back_kernel,
        "project_in_back",
        [whole((n, 1024)), whole((n, 512)), whole((w, 1024)), whole((w, 512))],
        [sds((2 * R, w), BF16)] * 2,
        2 * n * w * 1536,
        deps=deps,
    )(hbm(da), hbm(ds), w_in, w_sh)


def column(row_ref, start):
    row = row_ref[:, pl.ds(pl.multiple_of(start, R), R)]
    return jnp.broadcast_to(row, (R, R)).T


def mix_kernel(half, rank, o, y, pa, fac, gain, w_mix, m_o, send, keep):
    m_o[:, 0:128] = o[...]
    for j in range(QUARTERS):
        rows = slice(j * R, (j + 1) * R)
        f = column(fac, half * QUARTERS * R + (rank[0] ^ DISTANCE[j]) * R)
        for p in range(3):
            z = pa[rows, 128 + 128 * p : 256 + 128 * p].astype(F32)
            u = y[rows, 128 * p : 128 * p + 128].astype(F32) * (z * jax.nn.sigmoid(z))
            m_o[rows, 128 + 128 * p : 256 + 128 * p] = (
                u * f * gain[0:1, 128 * p : 128 * p + 128]
            ).astype(BF16)
    mixed = dot_nt(m_o[...], w_mix[...]).astype(BF16)
    send[...] = mixed[0 : 2 * R]
    keep[...] = mixed[2 * R :]


def mix(half, rank, o, y, pa, fac, gain, w_mix):
    n, w = y.shape[0], w_mix.shape[0]
    return call(
        functools.partial(mix_kernel, half),
        "mix",
        [
            SCALAR, whole((n, 128)), whole((n, 384)), whole((n, 512)), whole(fac.shape),
            whole((8, 384)), whole((w, 512), 0, 2),
        ],
        [far_out((n, 512), BF16), sds((2 * R, w), BF16), sds((2 * R, w), BF16)],
        2 * n * w * 512,
    )(rank, o, y, pa, fac, gain, w_mix)


def mix_back_kernel(rank, p0, p1, p2, p3, y, pa, gain, w_mix, dm_o, do_o, dyn_o, cross_o):
    dm = jnp.concatenate([p0[...], p1[...], p2[...], p3[...]], axis=0)
    dm_o[...] = dm
    d = dot_nn(dm, w_mix[...])
    do_o[...] = d[:, 0:128].astype(BF16)
    dyn_o[...] = d[:, 128:512]
    ones = jnp.ones((8, R), F32)
    for j in range(QUARTERS):
        rows = slice(j * R, (j + 1) * R)
        total = jnp.zeros((R, R), F32)
        for p in range(3):
            z = pa[rows, 128 + 128 * p : 256 + 128 * p].astype(F32)
            u = y[rows, 128 * p : 128 * p + 128].astype(F32) * (z * jax.nn.sigmoid(z))
            total = total + d[rows, 128 + 128 * p : 256 + 128 * p] * u * (
                gain[0:1, 128 * p : 128 * p + 128]
            )
        at = pl.multiple_of((rank[0] ^ DISTANCE[j]) * R, R)
        cross_o[:, pl.ds(at, R)] = dot_nt(ones, total, precision=EXACT)[0:1]


def mix_back(rank, pieces, y, pa, gain, w_mix):
    n, w = y.shape[0], w_mix.shape[0]
    return call(
        mix_back_kernel,
        "mix_back",
        [SCALAR] + [whole((R, w))] * 4
        + [whole((n, 384)), whole((n, 512)), whole((8, 384)), whole((w, 512), 0, 2)],
        [far_out((n, w), BF16), sds((n, 128), BF16), far_out((n, 384), F32), sds((1, n), F32)],
        2 * n * w * 512,
    )(rank, *hbm(pieces), hbm(y), hbm(pa), gain, w_mix)


def ffn_kernel(p0, p1, p2, p3, w_gu, w_dn, h_o, gu_o, act_o, send, keep):
    h = jnp.concatenate([p0[...], p1[...], p2[...], p3[...]], axis=0)
    h_o[...] = h
    gu = dot_nn(h, w_gu[...])
    gu_o[...] = gu.astype(BF16)
    g0 = gu[:, 0:512]
    act = (g0 * jax.nn.sigmoid(g0) * gu[:, 512:1024]).astype(BF16)
    act_o[...] = act
    out = dot_nt(act, w_dn[...]).astype(BF16)
    send[...] = out[0 : 2 * R]
    keep[...] = out[2 * R :]


def ffn(pieces, w_second):
    n, w = QUARTERS * R, pieces[0].shape[1]
    return call(
        ffn_kernel,
        "ffn",
        [whole((R, w))] * 4 + [whole((w, 1024)), whole((w, 512), 0, 2)],
        [
            far_out((n, w), BF16), far_out((n, 1024), BF16), far_out((n, 512), BF16),
            sds((2 * R, w), BF16), sds((2 * R, w), BF16),
        ],
        2 * n * w * 1536,
    )(*hbm(pieces), w_second, w_second)


def ffn_back_kernel(p0, p1, p2, p3, gu, w_gu, w_dn, df_o, dgu_o, send, keep):
    df = jnp.concatenate([p0[...], p1[...], p2[...], p3[...]], axis=0)
    df_o[...] = df
    da = dot_nn(df, w_dn[...])
    g0, g1 = gu[:, 0:512].astype(F32), gu[:, 512:1024].astype(F32)
    sg = jax.nn.sigmoid(g0)
    dgu_o[:, 0:512] = (da * g1 * sg * (1.0 + g0 * (1.0 - sg))).astype(BF16)
    dgu_o[:, 512:1024] = (da * g0 * sg).astype(BF16)
    out = dot_nt(dgu_o[...], w_gu[...]).astype(BF16)
    send[...] = out[0 : 2 * R]
    keep[...] = out[2 * R :]


def ffn_back(pieces, gu, w_second, deps=()):
    n, w = QUARTERS * R, pieces[0].shape[1]
    return call(
        ffn_back_kernel,
        "ffn_back",
        [whole((R, w))] * 4 + [whole((n, 1024)), whole((w, 1024)), whole((w, 512), 0, 2)],
        [far_out((n, w), BF16), far_out((n, 1024), BF16), sds((2 * R, w), BF16), sds((2 * R, w), BF16)],
        2 * n * w * 1536,
        deps=deps,
    )(*hbm(pieces), hbm(gu), w_second, w_second)


def weight_grad_kernel(widths, share, sel, *refs):
    out = refs[-1]
    at = 0
    for i, width in enumerate(widths):
        la, lb, ra, rb = refs[4 * i : 4 * i + 4]
        total = 0.0
        for left, right in ((la, ra), (lb, rb)):
            if share is None:
                rows = left[...]
            else:
                rows = left[:, pl.ds(pl.multiple_of(sel[0] * share, share), share)]
            total = total + dot_tn(rows, right[...])
        out[:, at : at + width] = total.astype(BF16)
        at += width


def insert_kernel(depth, base, kept, got, far, *refs):
    out = refs[-1]
    sq = depth // QUARTERS
    count = out.shape[0] // depth
    for d in range(count):
        rows = pl.ds(pl.multiple_of((pl.program_id(0) * count + d) * sq, sq), sq)
        total = kept[rows].astype(F32) + got[rows].astype(F32) + far[rows].astype(F32)
        for c in range(QUARTERS):
            out[d * depth + c * sq : d * depth + (c + 1) * sq] = total[
                :, 128 * c : 128 * c + 128
            ].astype(BF16)


def insert_shared(made, shared, depth, deps=()):
    w, total = made.shape
    keep_in_place = pl.BlockSpec(memory_space=pl.ANY)
    return pl.pallas_call(
        functools.partial(insert_kernel, depth),
        grid=(w // 512,),
        in_specs=[keep_in_place] + [whole(shared[2].shape)] * 3 + [keep_in_place] * len(deps),
        out_specs=pl.BlockSpec((512, 128), lambda i: (i, total // 128 - 1)),
        out_shape=far_out((w, total), BF16),
        input_output_aliases={0: 0},
        compiler_params=pltpu.CompilerParams(
            dimension_semantics=("arbitrary",), vmem_limit_bytes=VMEM_BYTES
        ),
        name="insert_shared",
    )(hbm(made), *shared, *deps)


def weight_grads(name, groups, deps=(), share=None, sel=None, room=0):
    n, w = groups[0][0][0].shape
    widths = [right[0].shape[1] for _, right in groups]
    step = 512 if share is None else 2 * share
    rows = step if share is None else share
    specs, args = [], []
    for (la, lb), (ra, rb) in groups:
        specs += [pl.BlockSpec((n, step), lambda i: (0, i))] * 2 + [whole(ra.shape)] * 2
        args += [la, lb, ra, rb]
    args = list(hbm(args))
    total = sum(widths) + room
    taken = len(args)

    def kernel(sel_ref, *refs):
        weight_grad_kernel(widths, share, sel_ref, *refs[:taken], refs[-1])

    return pl.pallas_call(
        kernel,
        grid=(w // step,),
        in_specs=[SCALAR] + specs + [pl.BlockSpec(memory_space=pl.ANY)] * len(deps),
        out_specs=pl.BlockSpec((rows, total), lambda i: (i, 0)),
        out_shape=far_out((w // step * rows, total), BF16),
        compiler_params=pltpu.CompilerParams(
            dimension_semantics=("arbitrary",), vmem_limit_bytes=GRADS_BYTES
        ),
        cost_estimate=pl.CostEstimate(
            flops=4 * n * w * total, bytes_accessed=2**20 * 12, transcendentals=0
        ),
        name=name,
    )(jnp.zeros((1,), jnp.int32) if sel is None else sel, *args, *deps)


def shared_grad_kernel(depth, rank, ha, hb, da, db, send, keep, made):
    made[...] = (dot_tn(ha[...], da[...]) + dot_tn(hb[...], db[...])).astype(BF16)
    sq, count = depth // QUARTERS, made.shape[0] // depth
    for j, distance in enumerate(DISTANCE):
        to = send if j < 2 else keep
        for d in range(count):
            at = pl.multiple_of(d * depth + (rank[0] ^ distance) * sq, sq)
            start = ((j % 2) * count + d) * sq
            to[start : start + sq] = made[pl.ds(at, sq)]


def shared_grads(depth, rank, h, ds):
    n, w = h[0].shape
    cols = ds[0].shape[1]
    send, keep = call(
        functools.partial(shared_grad_kernel, depth),
        "shared_grads",
        [SCALAR] + [whole((n, w))] * 2 + [whole((n, cols))] * 2,
        [sds((w // 2, cols), BF16)] * 2,
        4 * n * w * cols,
        [pltpu.VMEM((w, cols), BF16)],
    )(rank, *hbm(tuple(h)), *hbm(tuple(ds)))
    got = swap(send, "tensor", 1)
    half = w // 4
    far = swap((keep[half:].astype(F32) + got[half:].astype(F32)).astype(BF16), "tensor", 2)
    return keep, got, far


def finish_kernel(a0, a1, b0, b1, gu, down, q, gate, step, attn, ssm, kv, state):
    sq = kv.shape[1]
    for layer, (a, b) in enumerate(((a0, b0), (a1, b1))):
        gu[layer] = a[:, 0:1024].astype(F32)
        down[layer] = a[:, 1024:1536].astype(F32).T
        q[layer] = b[:, 0:128].astype(F32)
        gate[layer] = b[:, 128:896].astype(F32)
        step[layer] = b[:, 896:1024].astype(F32)
        attn[layer] = b[:, 1024:1152].astype(F32).T
        ssm[layer] = b[:, 1152:1536].astype(F32).T
        share = b[:, 1536:1664].astype(F32)
        for c in range(QUARTERS):
            to = kv if c < 2 else state
            to[layer, :, 128 * (c % 2) : 128 * (c % 2) + 128] = share[c * sq : (c + 1) * sq]


def finish(firsts, seconds):
    d = firsts[0].shape[0]
    return call(
        finish_kernel,
        "finish",
        [whole((d, 1536))] * 2 + [whole((d, 1664))] * 2,
        [
            sds((2, d, 1024), F32), sds((2, 512, d), F32), sds((2, d, 128), F32), sds((2, d, 768), F32),
            sds((2, d, 128), F32), sds((2, 128, d), F32), sds((2, 384, d), F32),
            sds((2, d // QUARTERS, 256), F32), sds((2, d // QUARTERS, 256), F32),
        ],
        10**6,
    )(*firsts, *seconds)


def chunk_terms(act, raw_step, tok, seg_row, par):
    row, lane = iota((R, R), 0), iota((R, R), 1)
    b, c = act[:, 384:512], act[:, 512:640]
    bb, cb = b.astype(BF16), c.astype(BF16)
    dt = softplus(raw_step + par[1:2])
    tri = (row >= lane).astype(F32)
    cum = dot_nn(tri, dt * par[0:1], precision=EXACT)
    last = cum[R - 1 : R]
    okay = (row >= lane) & (tok[:, 5:6] == seg_row)
    inner = jnp.where(okay, dot_nt(cb, bb), 0.0)
    enter = jnp.exp(cum) * tok[:, 3:4]
    tail = jnp.exp(jnp.minimum(last - cum, 0.0)) * tok[:, 4:5]
    return b, c, bb, cb, dt, cum, cum.T, dt.T, okay, inner, enter, tail


def ssm_fwd_chunk(pa, raw, ps, tok, seg_row, cos, sin, taps, par, skip, y_o, pre_o, st_o, q_o, kv_o, state, hist):
    lane = iota((R, R), 1)
    half = lane < PH
    xin = jnp.concatenate([pa[:, 512:896], ps[:, 128:384]], axis=1).astype(F32)
    ext = jnp.concatenate([hist[...], xin], axis=0)
    hist[...] = xin[R - 8 :]
    pre = taps[4:5] + xin * taps[3:4]
    for k in (1, 2, 3):
        pre = pre + ext[8 - k : 8 - k + R] * tok[:, k - 1 : k] * taps[3 - k : 4 - k]
    pre_o[...] = pre.astype(BF16)
    act = pre * jax.nn.sigmoid(pre)
    b, c, bb, cb, dt, cum, cum_t, dt_t, okay, inner, enter, tail = chunk_terms(
        act, raw[...], tok, seg_row, par
    )
    tail = tail * dt
    keep = enter[R - 1 : R]
    b_t = b.T.astype(BF16)
    squares = jnp.zeros((R, R), F32)
    for p in range(3):
        h0, h1 = 2 * p, 2 * p + 1
        cols = slice(128 * p, 128 * p + 128)
        xp = act[:, cols]
        xb = xp.astype(BF16)
        sp = state[:, cols]
        st_o[:, cols] = sp.astype(BF16)

        def weights(h):
            gap = jnp.minimum(cum[:, h : h + 1] - cum_t[h : h + 1], 0.0)
            return (inner * jnp.exp(gap) * dt_t[h : h + 1]).astype(BF16)

        y = jnp.where(half, dot_nn(weights(h0), xb), dot_nn(weights(h1), xb))
        y = y + dot_nn(cb, sp.astype(BF16)) * jnp.where(
            half, enter[:, h0 : h0 + 1], enter[:, h1 : h1 + 1]
        )
        y = y + skip[0:1, cols] * xp
        y_o[:, cols] = y.astype(BF16)
        tp = jnp.where(half, tail[:, h0 : h0 + 1], tail[:, h1 : h1 + 1])
        kp = jnp.where(half[0:1], keep[:, h0 : h0 + 1], keep[:, h1 : h1 + 1])
        state[:, cols] = kp * sp + dot_nn(b_t, (tp * xp).astype(BF16))
        z = pa[:, 128 + 128 * p : 256 + 128 * p].astype(F32)
        u = y * z * jax.nn.sigmoid(z)
        squares = squares + u * u
    q = pa[:, 0:128].astype(F32)
    q_o[...] = (q * cos + partner(q, lane) * sin).astype(BF16)
    kv = ps[:, 0:128].astype(F32)
    kv_o[...] = jnp.where(half, kv * cos + partner(kv, lane) * sin, kv).astype(BF16)
    return dot_nt(jnp.ones((8, R), F32), squares, precision=EXACT)[0:1]


def ssm_fwd_kernel(
    rank, pa0, pa1, raw0, raw1, ps0, ps1, tok_r, seg_r, cos_r, sin_r, taps, par, skip,
    y0, y1, pre0, pre1, st_o, sq_o, q_o, kv_o, state, hist,
):
    i = pl.program_id(0)

    @pl.when(i == 0)
    def _():
        state[...] = jnp.zeros_like(state)
        hist[...] = jnp.zeros_like(hist)

    halves = ((pa0, raw0, ps0, y0, pre0), (pa1, raw1, ps1, y1, pre1))
    for half, (pa, raw, ps, y_o, pre_o) in enumerate(halves):
        rows = slice(half * R, (half + 1) * R)
        at = pl.multiple_of(half * QUARTERS * R + i * R, R)
        sq_o[:, pl.ds(at, R)] = ssm_fwd_chunk(
            pa, raw, ps, tok_r[rows], seg_r[0:1, rows], cos_r[rows], sin_r[rows], taps, par, skip,
            y_o, pre_o, st_o.at[half], q_o.at[rows], kv_o.at[rows], state, hist,
        )


def wire(width, reverse=False):
    def at(i, rank):
        i = QUARTERS - 1 - i if reverse else i
        return (block_of(i, rank[0]), 0)

    return pl.BlockSpec((R, width), at)


def in_order(shape, dim=0, reverse=False):
    def at(i, rank):
        i = QUARTERS - 1 - i if reverse else i
        return tuple(i if d == dim else 0 for d in range(len(shape)))

    return pl.BlockSpec(shape, at)


def ssm_forward(rank, pa, raw, ps, tok, seg_rows, cos, sin, taps, par, skip):
    n = QUARTERS * R
    t = 2 * n
    return pl.pallas_call(
        ssm_fwd_kernel,
        grid_spec=pltpu.PrefetchScalarGridSpec(
            num_scalar_prefetch=1,
            grid=(QUARTERS,),
            in_specs=[
                wire(896), wire(896), wire(128), wire(128), wire(384), wire(384),
                in_order((2 * R, 8)), in_order((8, 2 * R), 1),
                in_order((2 * R, 128)), in_order((2 * R, 128)), whole((8, 640)), whole((8, 128)), whole((8, 384)),
            ],
            out_specs=[
                wire(384), wire(384), wire(640), wire(640), in_order((2, NS, 384)), whole((1, t)),
                in_order((2 * R, 128)), in_order((2 * R, 128)),
            ],
            scratch_shapes=[pltpu.VMEM((NS, 384), F32), pltpu.VMEM((8, 640), F32)],
        ),
        out_shape=[
            sds((n, 384), BF16), sds((n, 384), BF16), far_out((n, 640), BF16), far_out((n, 640), BF16),
            far_out((2 * QUARTERS, NS, 384), BF16), sds((1, t), F32), sds((t, 128), BF16), sds((t, 128), BF16),
        ],
        compiler_params=pltpu.CompilerParams(
            dimension_semantics=("arbitrary",), vmem_limit_bytes=VMEM_BYTES
        ),
        cost_estimate=pl.CostEstimate(
            flops=4 * 10**9, bytes_accessed=20 * 2**20, transcendentals=3 * 10**6
        ),
        name="ssm_forward",
    )(rank, *pa, *raw, *ps, tok, seg_rows, cos, sin, taps, par, skip)


def ssm_bwd_chunk(
    pa, raw, ps, pre_r, y_r, st_r, dyn_r, r2, coef, dq, dkv, tok, seg_row, taps, par, skip, gain,
    da_o, ds_o, gt_o, gc_o, gh_o, dstate, nxt, own_first,
):
    row, lane = iota((R, R), 0), iota((R, R), 1)
    half = lane < PH
    sub = iota((8, R), 0)
    pre = pre_r[...].astype(F32)
    sg = jax.nn.sigmoid(pre)
    act = pre * sg
    b, c, bb, cb, dt, cum, cum_t, dt_t, okay, inner, enter, tail = chunk_terms(
        act, raw[...], tok, seg_row, par
    )
    tail_dt = tail * dt
    keep = enter[R - 1 : R]
    c_t = c.T.astype(BF16)
    db = jnp.zeros((R, R), F32)
    dc = jnp.zeros((R, R), F32)
    dinner = jnp.zeros((R, R), F32)
    dcum = jnp.zeros((R, R), F32)
    extra = jnp.zeros((R, R), F32)
    col_sum = jnp.zeros((8, R), F32)
    last_row = jnp.zeros((1, R), F32)
    dx_parts = []
    for p in range(3):
        cols = slice(128 * p, 128 * p + 128)
        z = pa[:, 128 + 128 * p : 256 + 128 * p].astype(F32)
        y, dyn = y_r[:, cols].astype(F32), dyn_r[:, cols]
        zs = jax.nn.sigmoid(z)
        sz = z * zs
        u = y * sz
        dn = dyn * r2
        gc_o[0:1, cols] += jnp.sum(dn * u, axis=0, keepdims=True)
        du = gain[0:1, cols] * dn - u * coef
        da_o[:, 128 + 128 * p : 256 + 128 * p] = (
            du * y * zs * (1.0 + z * (1.0 - zs))
        ).astype(BF16)
        dy = du * sz
        dyb = dy.astype(BF16)
        xp = act[:, cols]
        xb = xp.astype(BF16)
        gc_o[1:2, cols] += jnp.sum(dy * xp, axis=0, keepdims=True)
        sb = st_r[:, cols]
        sp = sb.astype(F32)
        dsp = dstate[:, cols]
        dsb = dsp.astype(BF16)
        h0, h1 = 2 * p, 2 * p + 1
        ep = jnp.where(half, enter[:, h0 : h0 + 1], enter[:, h1 : h1 + 1])
        tp = jnp.where(half, tail_dt[:, h0 : h0 + 1], tail_dt[:, h1 : h1 + 1])
        kp = jnp.where(half[0:1], keep[:, h0 : h0 + 1], keep[:, h1 : h1 + 1])
        cdb = (ep * dy).astype(BF16)
        through = dy * ep * dot_nn(cb, sb)
        bds = dot_nn(bb, dsb)
        qx = xp * bds
        kept = jnp.sum(dsp * sp, axis=0, keepdims=True) * kp
        dxi = []
        for h in (h0, h1):
            mine = half if h == h0 else ~half
            gap = jnp.minimum(cum[:, h : h + 1] - cum_t[h : h + 1], 0.0)
            decay = jnp.where(okay, jnp.exp(gap), 0.0)
            dt_row = dt_t[h : h + 1]
            dg = dot_nt(jnp.where(mine, dy, 0.0).astype(BF16), xb)
            t1 = dg * decay
            dinner = dinner + t1 * dt_row
            w0 = t1 * inner
            col_sum = col_sum + jnp.where(sub == h, jnp.sum(w0, axis=0, keepdims=True), 0.0)
            w1 = w0 * dt_row + jnp.where(mine, through, 0.0)
            dcum = dcum + jnp.where(lane == h, jnp.sum(w1, axis=1, keepdims=True), 0.0)
            e = jnp.sum(jnp.where(mine, qx, 0.0), axis=1, keepdims=True)
            extra = extra + jnp.where(lane == h, e, 0.0)
            k = jnp.sum(jnp.where(mine[0:1], kept, 0.0), axis=1, keepdims=True)
            last_row = last_row + jnp.where(lane[0:1] == h, k, 0.0)
            dxi.append(dot_tn((decay * inner * dt_row).astype(BF16), dyb))
        dx_parts.append(jnp.where(half, dxi[0], dxi[1]) + tp * bds + skip[0:1, cols] * dy)
        dc = dc + dot_nt(cdb, sb)
        db = db + dot_nt((tp * xp).astype(BF16), dsb)
        dstate[:, cols] = kp * dsp + dot_nn(c_t, cdb)
    col_sum = jnp.concatenate([col_sum, jnp.zeros((R - 8, R), F32)], axis=0).T
    moved = tail_dt * extra
    last_row = last_row + jnp.sum(moved, axis=0, keepdims=True)
    dcum = dcum - col_sum * dt - moved + jnp.where(row == R - 1, last_row, 0.0)
    dlog = dot_nn((row <= lane).astype(F32), dcum, precision=EXACT)
    ddt = col_sum + tail * extra + par[0:1] * dlog
    gh_o[0:1] += jnp.sum(dt * dlog, axis=0, keepdims=True)
    ddr = ddt * jax.nn.sigmoid(raw[...] + par[1:2])
    gh_o[1:2] += jnp.sum(ddr, axis=0, keepdims=True)
    da_o[:, 896:1024] = ddr.astype(BF16)
    dib = dinner.astype(BF16)
    dc = dc + dot_nn(dib, bb)
    db = db + dot_tn(dib, cb)
    dact = jnp.concatenate([*dx_parts, db, dc], axis=1)
    dpre = dact * sg * (1.0 + pre * (1.0 - sg))
    xin = jnp.concatenate([pa[:, 512:896], ps[:, 128:384]], axis=1).astype(F32)
    dxin = dpre * taps[3:4]
    gt_o[3:4] += jnp.sum(dpre * xin, axis=0, keepdims=True)
    gt_o[4:5] += jnp.sum(dpre, axis=0, keepdims=True)
    for k in (1, 2, 3):
        zk = dpre * tok[:, k - 1 : k]
        later = nxt.at[k - 1]
        moved_up = jnp.concatenate([zk, later[...]], axis=0)[k : k + R]
        later[...] = zk[0:8]
        dxin = dxin + moved_up * taps[3 - k : 4 - k]
        gt_o[3 - k : 4 - k] += jnp.sum(moved_up * xin, axis=0, keepdims=True)
    da_o[:, 512:896] = dxin[:, 0:384].astype(BF16)
    ds_o[:, 256:512] = dxin[:, 384:640].astype(BF16)
    da_o[:, 0:128] = dq
    other = pltpu.roll(dkv, HD, 1)
    mine = half == own_first
    ds_o[:, 0:128] = jnp.where(mine, jnp.where(half, dkv, other), 0.0).astype(BF16)
    ds_o[:, 128:256] = jnp.where(mine, jnp.where(half, other, dkv), 0.0).astype(BF16)


def ssm_bwd_kernel(
    rank, oh, pa0, pa1, raw0, raw1, ps0, ps1, pre0, pre1, y0, y1, st_r, dyn0, dyn1, fac_r, coef_r, dq_r, dkv_r,
    tok_r, seg_r, taps, par, skip, gain,
    da0, da1, ds0, ds1, gt_o, gc_o, gh_o, dstate, nxt,
):
    i = pl.program_id(0)

    @pl.when(i == 0)
    def _():
        dstate[...] = jnp.zeros_like(dstate)
        nxt[...] = jnp.zeros_like(nxt)
        gt_o[...] = jnp.zeros_like(gt_o)
        gc_o[...] = jnp.zeros_like(gc_o)
        gh_o[...] = jnp.zeros_like(gh_o)

    quarter = QUARTERS - 1 - i
    halves = (
        (pa0, raw0, ps0, pre0, y0, dyn0, da0, ds0),
        (pa1, raw1, ps1, pre1, y1, dyn1, da1, ds1),
    )
    for half in (1, 0):
        pa, raw, ps, pre, y, dyn, da, ds = halves[half]
        rows = slice(half * R, (half + 1) * R)
        start = half * QUARTERS * R + quarter * R
        ssm_bwd_chunk(
            pa, raw, ps, pre, y, st_r.at[half], dyn, column(fac_r, start), column(coef_r, start),
            dq_r[rows], dkv_r[rows].astype(F32), tok_r[rows], seg_r[0:1, rows], taps, par, skip, gain,
            da, ds, gt_o, gc_o, gh_o, dstate, nxt, oh[0] == 0,
        )


def ssm_backward(
    rank, oh, pa, raw, ps, pre, y, states, dyn, fac, coef, dq, dkv, tok, seg_rows, taps, par, skip, gain
):
    n = QUARTERS * R
    t = 2 * n
    back = {"reverse": True}
    return pl.pallas_call(
        lambda r, *refs: ssm_bwd_kernel(r, *refs),
        grid_spec=pltpu.PrefetchScalarGridSpec(
            num_scalar_prefetch=1,
            grid=(QUARTERS,),
            in_specs=[
                SCALAR, wire(896, **back), wire(896, **back), wire(128, **back), wire(128, **back),
                wire(384, **back), wire(384, **back),
                wire(640, **back), wire(640, **back), wire(384, **back), wire(384, **back),
                in_order((2, NS, 384), **back), wire(384, **back), wire(384, **back),
                whole((1, t)), whole((1, t)), in_order((2 * R, 128), **back), in_order((2 * R, 128), **back),
                in_order((2 * R, 8), **back), in_order((8, 2 * R), 1, **back),
                whole((8, 640)), whole((8, 128)), whole((8, 384)), whole((8, 384)),
            ],
            out_specs=[
                wire(1024, **back), wire(1024, **back), wire(512, **back), wire(512, **back),
                whole((8, 640)), whole((8, 384)), whole((8, 128)),
            ],
            scratch_shapes=[pltpu.VMEM((NS, 384), F32), pltpu.VMEM((3, 8, 640), F32)],
        ),
        out_shape=[
            far_out((n, 1024), BF16), far_out((n, 1024), BF16), far_out((n, 512), BF16), far_out((n, 512), BF16),
            sds((8, 640), F32), sds((8, 384), F32), sds((8, 128), F32),
        ],
        compiler_params=pltpu.CompilerParams(
            dimension_semantics=("arbitrary",), vmem_limit_bytes=VMEM_BYTES
        ),
        cost_estimate=pl.CostEstimate(
            flops=8 * 10**9, bytes_accessed=30 * 2**20, transcendentals=4 * 10**6
        ),
        name="ssm_backward",
    )(
        rank, oh, *hbm(pa), *hbm(raw), *hbm(ps), *hbm(pre), *hbm(y), hbm(states), *hbm(dyn), fac, coef, dq, dkv, tok, seg_rows, taps, par, skip, gain
    )


def head_views(kv, lane):
    zero = jnp.zeros_like(kv)
    left = lane < HD
    k0 = jnp.where(left, kv, zero)
    v1 = jnp.where(left, zero, kv)
    k1 = pltpu.roll(k0.astype(F32), HD, 1).astype(BF16)
    v0 = pltpu.roll(v1.astype(F32), HD, 1).astype(BF16)
    return (k0, k1), (v0, v1)


def allowed_keys(tok_r, seg_r, start, rows, keys):
    return (iota((rows, keys), 1) <= start + iota((rows, keys), 0)) & (
        tok_r[start : start + rows, 5:6] == seg_r[0:1, 0:keys]
    )


def attend_fwd_kernel(rank, q_r, kv_r, tok_r, seg_r, o0, o1, lse_o):
    n = q_r.shape[0]
    ks, vs = head_views(kv_r[...], iota((n, 2 * HD), 1))
    lane = iota((2 * R, 128), 1)
    for quarter in range(QUARTERS):
        start, keys = quarter * 2 * R, (quarter + 1) * 2 * R
        q = q_r[start:keys]
        okay = allowed_keys(tok_r, seg_r, start, 2 * R, keys)
        out = jnp.zeros((2 * R, 2 * HD), F32)
        stats = []
        for h in range(2):
            s = jnp.where(okay, dot_nt(q, ks[h][0:keys]) * HD**-0.5, NEG)
            top = jnp.max(s, axis=1, keepdims=True)
            e = jnp.exp(s - top)
            total = jnp.sum(e, axis=1, keepdims=True)
            out = out + dot_nn((e * (1.0 / total)).astype(BF16), vs[h][0:keys])
            stats.append(top + jnp.log(total))
        at = pl.ds(pl.multiple_of(block_of(quarter, rank[0]) * R, R), R)
        o0[at] = out[0:R].astype(BF16)
        o1[at] = out[R:].astype(BF16)
        lse_o[start:keys] = jnp.where(lane == 0, stats[0], stats[1])


def attend_bwd_kernel(
    rank, q_r, kv_r, do0, do1, lse_r, tok_r, seg_r, cos_r, sin_r, dq_o, dkv_o, dk_acc, dv_acc
):
    n = q_r.shape[0]
    ks, vs = head_views(kv_r[...], iota((n, 2 * HD), 1))
    lane = iota((2 * R, 128), 1)
    left = lane < HD
    dk_acc[...] = jnp.zeros_like(dk_acc)
    dv_acc[...] = jnp.zeros_like(dv_acc)
    for quarter in range(QUARTERS):
        start, keys = quarter * 2 * R, (quarter + 1) * 2 * R
        q = q_r[start:keys]
        at = pl.ds(pl.multiple_of(block_of(quarter, rank[0]) * R, R), R)
        do = jnp.concatenate([do0[at], do1[at]], axis=0)
        okay = allowed_keys(tok_r, seg_r, start, 2 * R, keys)
        lse = lse_r[start:keys]
        zero = jnp.zeros_like(q)
        dq = jnp.zeros((2 * R, 2 * HD), F32)
        for h in range(2):
            mine = left if h == 0 else ~left
            s = dot_nt(q, ks[h][0:keys]) * HD**-0.5
            p = jnp.where(okay, jnp.exp(s - lse[:, h : h + 1]), 0.0)
            dp = dot_nt(do, vs[h][0:keys])
            dot_sum = jnp.sum(p * dp, axis=1, keepdims=True)
            ds = (p * (dp - dot_sum)).astype(BF16)
            dq = dq + dot_nn(ds, ks[h][0:keys])
            dk_acc[0:keys] += dot_tn(ds, jnp.where(mine, q, zero))
            dv_acc[0:keys] += dot_tn(p.astype(BF16), jnp.where(mine, do, zero))
        dq = dq * HD**-0.5
        dq_o[start:keys] = (
            dq * cos_r[start:keys] - partner(dq, lane) * sin_r[start:keys]
        ).astype(BF16)
    for start in range(0, n, 2 * R):
        rows = slice(start, start + 2 * R)
        dk, dv = dk_acc[rows], dv_acc[rows]
        dk = (dk + pltpu.roll(dk, HD, 1)) * HD**-0.5
        dv = dv + pltpu.roll(dv, HD, 1)
        dk = dk * cos_r[rows] - partner(dk, lane) * sin_r[rows]
        dkv_o[rows] = jnp.where(left, dk, dv).astype(BF16)


def attend_forward(rank, q, kv, tok, seg_rows):
    t = q.shape[0]
    return call(
        attend_fwd_kernel,
        "attend_forward",
        [SCALAR, whole((t, 128)), whole((t, 128)), whole((t, 8)), whole((8, t))],
        [sds((t // 2, 128), BF16), sds((t // 2, 128), BF16), far_out((t, 128), F32)],
        2 * 10**9,
    )(rank, q, kv, tok, seg_rows)


def attend_backward(rank, q, kv, do, lse, tok, seg_rows, cos, sin, deps=()):
    t = q.shape[0]
    full = whole((t, 128))
    return call(
        attend_bwd_kernel,
        "attend_backward",
        [SCALAR, full, full, whole((t // 2, 128)), whole((t // 2, 128)), full,
         whole((t, 8)), whole((8, t)), full, full],
        [sds((t, 128), BF16), sds((t, 128), BF16)],
        4 * 10**9,
        [pltpu.VMEM((t, 128), F32), pltpu.VMEM((t, 128), F32)],
        deps,
    )(rank, hbm(q), hbm(kv), *do, hbm(lse), tok, seg_rows, cos, sin)


def swap(values, axis, distance):
    size = lax.axis_size(axis)
    return lax.ppermute(values, axis, [(i, i ^ distance) for i in range(size)])


def bits_of(axis):
    size = lax.axis_size(axis)
    return [1 << b for b in range(size.bit_length() - 1)]


def sum_over(values, axes):
    for axis in axes:
        for bit in bits_of(axis):
            values = values + swap(values, axis, bit)
    return values


def sum_rows(values):
    return values + sum(swap(values, "tensor", d) for d in (1, 2, 3))


def gather_half(own):
    far = swap(own, "tensor", 2)
    near = swap(own, "tensor", 1)
    return near, swap(far, "tensor", 1), own, far


def scatter_half(send, keep, on_the_way):
    got = swap(send, "tensor", 1)
    given = (keep[R:].astype(F32) + got[R:].astype(F32)).astype(BF16)
    on_the_way.append(given)
    return keep, got, swap(given, "tensor", 2)


def gather_everywhere(own):
    held = own[:, None]
    for axis in ("dp", "tensor"):
        place = lax.axis_index(axis)
        for bit in bits_of(axis):
            upper = (place & bit) != 0
            other = swap(held, axis, bit)
            low, high = jnp.where(upper, other, held), jnp.where(upper, held, other)
            held = jnp.concatenate([low, high], axis=0 if axis == "dp" else 1)
    return held.reshape(-1, *own.shape[1:])


def gather_dp(v):
    return lax.all_gather(v, "dp", axis=0, tiled=True)


def scatter_dp(v):
    return lax.psum_scatter(v, "dp", scatter_dimension=0, tiled=True)


def pairs_of_dp(share):
    size = lax.axis_size("dp")
    return share % 128 == 0 and size % 2 == 0 and size >= 4


def merge_kernel(a, b, o):
    o[...] = (a[...].astype(F32) + b[...].astype(F32)).astype(BF16)


def merge(a, b, deps):
    return call(merge_kernel, "merge", [whole(a.shape)] * 2, [far_out(a.shape, BF16)], 10**6, deps=deps)(
        hbm(a), hbm(b)
    )[0]


def scatter_lines(v):
    size = lax.axis_size("dp")
    lines = [[i for i in range(size) if i % 2 == s] for s in range(2)]
    return lax.psum_scatter(v, "dp", scatter_dimension=0, tiled=True, axis_index_groups=lines)


def pad_rows(v, rows=8):
    return jnp.pad(v, ((0, rows - v.shape[0]), (0, 0)))


def body(
    inputs, cotangent, segment_ids, norm_gains, w_query, key_value_weight, w_gate_in, w_state_in,
    w_step, ssm_channel, conv_state, head_params, w_attn_out, w_ssm_out, w_gate_up, w_down,
):
    width = inputs.shape[2]
    n = segment_ids.shape[1]
    tp_size = lax.axis_size("tensor")
    tensor = lax.axis_index("tensor")
    slot = lax.axis_index("dp") * tp_size + tensor
    kv_cols = key_value_weight.shape[2]
    kv_heads = kv_cols // (2 * HD)
    own_head = tensor * (w_query.shape[2] // HD) // (HQ // kv_heads)
    ssm_heads = w_step.shape[2]
    channels = ssm_heads * PH
    hidden = w_gate_up.shape[3]
    depth = w_query.shape[1]
    rank = tensor.reshape(1).astype(jnp.int32)
    oh = own_head.reshape(1).astype(jnp.int32)

    halves = [inputs[0, :R], inputs[0, R:]]
    x_pieces = [gather_half(v) for v in halves]

    shared = jnp.concatenate([key_value_weight, w_state_in], axis=2)
    sq, wide = shared.shape[1:]
    shares = [
        shared[layer].reshape(sq, wide // 128, 128).swapaxes(0, 1).reshape(depth, 128)
        for layer in range(LAYERS)
    ]

    def exchange(share):
        far = swap(share, "tensor", 2)
        return share, swap(share, "tensor", 1), far, swap(far, "tensor", 1)

    w_first, w_second, w_shared = [], [], []
    for layer in range(LAYERS):
        first = [
            w_query[layer],
            w_gate_in[layer].reshape(depth, 2 * channels),
            jnp.pad(w_step[layer], ((0, 0), (0, 128 - ssm_heads))),
            w_attn_out[layer].T,
            w_ssm_out[layer].T,
        ]
        second = [w_gate_up[layer].reshape(depth, 2 * hidden), w_down[layer].T]
        first = gather_dp(jnp.concatenate(first + (shares if layer == 0 else []), axis=1))
        if layer == 0:
            w_shared = [exchange(first[:, c : c + 128]) for c in range(1536, 1536 + 128 * LAYERS, 128)]
        w_first.append(first)
        w_second.append(gather_dp(jnp.concatenate(second, axis=1)))

    small = jnp.concatenate([norm_gains.reshape(-1), conv_state.reshape(-1)])[None, :]
    small_all = gather_everywhere(small).astype(F32)
    gain_count = norm_gains.size
    gains = (
        small_all[:, :gain_count]
        .reshape(-1, LAYERS, 2, norm_gains.shape[2])
        .transpose(1, 2, 0, 3)
        .reshape(LAYERS, 2, width)
    )
    conv_flat = (
        small_all[:, gain_count : gain_count + conv_state.size]
        .reshape(-1, LAYERS, conv_state.shape[1])
        .transpose(1, 0, 2)
        .reshape(LAYERS, 5, 2 * NS)
    )

    seg = segment_ids[0]
    segf = seg.astype(F32)
    index = jnp.arange(n, dtype=jnp.int32)
    places = index - jnp.sum((seg[None, :] < seg[:, None]).astype(jnp.int32), axis=1)
    freq = ROPE_BASE ** (-jnp.arange(HD // 2, dtype=F32) / (HD // 2))
    angle = places.astype(F32)[:, None] * freq[None, :]
    cos_one, sin_one = jnp.cos(angle), jnp.sin(angle)
    cos = jnp.concatenate([cos_one] * 4, axis=1)
    sin = jnp.concatenate([-sin_one, sin_one] * 2, axis=1)
    shifted = [
        (jnp.pad(seg, (k, 0), constant_values=-1)[:n] == seg).astype(F32) for k in (1, 2, 3)
    ]
    ends = seg.reshape(-1, R)[:, -1]
    before = jnp.concatenate([jnp.full((1,), -1, jnp.int32), ends[:-1]])
    enters = (seg.reshape(-1, R) == before[:, None]).astype(F32).reshape(-1)
    leaves = (seg.reshape(-1, R) == ends[:, None]).astype(F32).reshape(-1)
    tok = jnp.stack([*shifted, enters, leaves, segf, segf, segf], axis=1)
    seg_rows = jnp.broadcast_to(segf[None, :], (8, n))

    residual, last_parts, sent_on = halves, [], []
    pieces = x_pieces
    saved = []
    for layer in range(LAYERS):
        channel, head = ssm_channel[layer], head_params[layer]
        taps = pad_rows(jnp.concatenate([channel[:5], conv_flat[layer]], axis=1))
        rate = -jnp.exp(head[0])
        par = pad_rows(jnp.pad(jnp.stack([rate, head[1]]), ((0, 0), (0, 128 - ssm_heads))))
        skip = pad_rows(jnp.repeat(head[2], PH)[None, :])
        gain_row = pad_rows(channel[5:6])
        gain_one = pad_rows(gains[layer, 0:1])
        gain_two = pad_rows(gains[layer, 1:2])
        wf, ws, wh = w_first[layer], w_second[layer], w_shared[layer]
        ins = functools.partial(project_in, layer == 0, depth, rank, oh)
        w_all, *half_0 = ins(pieces[0], gain_one, wf, wh)
        w_shared[layer] = w_all
        h, pa, raw, ps = zip(half_0, ins(pieces[1], gain_one, wf, w_all))
        y0, y1, pre0, pre1, states, sq, q_rot, kv_rot = ssm_forward(
            rank, pa, raw, ps, tok, seg_rows, cos, sin, taps, par, skip
        )
        y, pre = (y0, y1), (pre0, pre1)
        total = sum_rows(sq)
        o0, o1, lse = attend_forward(rank, q_rot, kv_rot, tok, seg_rows)
        factor = lax.rsqrt(total / (HS * PH) + EPS)
        mixed, middle, h2, gu, act, result, pieces = [], [], [], [], [], [], []
        parts = []
        for i, o in enumerate((o0, o1)):
            m, send, keep = mix(i, rank, o, y[i], pa[i], factor, gain_row, wf)
            mixed.append(m)
            parts.append(scatter_half(send, keep, sent_on))
        gathered = []
        for i in range(2):
            x1, low = take_step(residual[i], *parts[i], gain_two)
            middle.append(x1)
            gathered.append(gather_half(low))
        parts = []
        for i in range(2):
            h2_i, gu_i, act_i, send, keep = ffn(gathered[i], ws)
            h2.append(h2_i)
            gu.append(gu_i)
            act.append(act_i)
            parts.append(scatter_half(send, keep, sent_on))
        for i in range(2):
            if layer + 1 < LAYERS:
                x2, low = take_step(middle[i], *parts[i], pad_rows(gains[layer + 1, 0:1]))
                result.append(x2)
                pieces.append(gather_half(low))
            else:
                last_parts.append((middle[i], *parts[i], None))
        saved.append(
            (residual, middle, h, pa, raw, ps, y, pre, states, q_rot, kv_rot, lse, factor, mixed, h2, gu, act,
             taps, par, skip, gain_row, gain_one, gain_two, rate)
        )
        residual = result

    grad = [cotangent[0, :R], cotangent[0, R:]]
    low = list(grad)
    big, small_grads = [None] * LAYERS, [None] * LAYERS
    for layer in reversed(range(LAYERS)):
        (first_in, middle, h, pa, raw, ps, y, pre, states, q_rot, kv_rot, lse, factor, mixed, h2, gu, act,
         taps, par, skip, gain_row, gain_one, gain_two, rate) = saved[layer]
        wf, ws, wh = w_first[layer], w_second[layer], w_shared[layer]
        gathered = [gather_half(v) for v in low]
        df, dgu, dm, do, dyn, cross, parts = [], [], [], [], [], [], []
        deps = (big[layer + 1][0],) if layer + 1 < LAYERS else ()
        for i in range(2):
            df_i, dgu_i, send, keep = ffn_back(gathered[i], gu[i], ws, deps)
            df.append(df_i)
            dgu.append(dgu_i)
            parts.append(scatter_half(send, keep, sent_on))
        groups = [(h2, dgu), (df, act)]
        paired = layer == 0 and pairs_of_dp(depth)
        if paired:
            side = (lax.axis_index("dp") % 2).reshape(1).astype(jnp.int32)
            given = weight_grads("grads_one_sent", groups, sent_on[-2:], depth, 1 - side)
            kept = weight_grads("grads_one_kept", groups, (given,), depth, side)
            sent = swap(given, "dp", 1)
            early = [(given,), ()]
        else:
            g1 = weight_grads("grads_one", groups, sent_on[-2:])
            early = [(g1,), ()]
        gathered, dx1, dgain2, dgain1 = [], [], 0.0, 0.0
        for i in range(2):
            dx, low_i, gg = back_step(grad[i], middle[i], *parts[i], gain_two, early[i])
            dx1.append(dx)
            dgain2 = dgain2 + gg[0]
            gathered.append(gather_half(low_i))
        for i in range(2):
            dm_i, do_i, dyn_i, cross_i = mix_back(rank, gathered[i], y[i], pa[i], gain_row, wf)
            dm.append(dm_i)
            do.append(do_i)
            dyn.append(dyn_i)
            cross.append(cross_i)
        cross = sum_rows(jnp.concatenate(cross, axis=1))
        dq, dkv = attend_backward(
            rank, q_rot, kv_rot, do, lse, tok, seg_rows, cos, sin
        )
        coef = factor**3 * cross / (HS * PH)
        da0, da1, ds0, ds1, g_taps, g_chan, g_head = ssm_backward(
            rank, oh, pa, raw, ps, pre, y, states, dyn, factor, coef, dq, dkv, tok, seg_rows, taps, par, skip,
            gain_row,
        )
        groups = [(h, (da0, da1)), (dm, mixed)]
        shared_sum = shared_grads(depth, rank, h, (ds0, ds1))
        before = ()
        if layer == 0:
            g2 = weight_grads("grads_two", groups, (big[layer + 1][1],), room=128)
            if paired:
                g1 = scatter_lines(merge(kept, sent, tuple(do)))
                before = (g1,)
            g2 = insert_shared(g2, shared_sum, depth, before)
        sums = [project_in_back(da, ds, wf, wh) for da, ds in ((da0, ds0), (da1, ds1))]
        parts = [scatter_half(*v, sent_on) for v in sums]
        deps = ()
        if layer > 0:
            g2 = weight_grads("grads_two", groups, sent_on[-2:], room=128)
            g2 = insert_shared(g2, shared_sum, depth)
            deps = (g2,)
        grad, low = [], []
        for i in range(2):
            g, low_i, gg = back_step(dx1[i], first_in[i], *parts[i], gain_one, () if i else deps)
            grad.append(g)
            low.append(low_i)
            dgain1 = dgain1 + gg[0]
        chan_grad = jnp.concatenate([g_taps[:5, :channels], g_chan[0:1]], axis=0)
        head_grad = jnp.stack(
            [
                g_head[0, :ssm_heads] * rate,
                g_head[1, :ssm_heads],
                jnp.sum(g_chan[1].reshape(ssm_heads, PH), axis=1),
            ]
        )
        big[layer] = (g1 if paired else scatter_dp(g1), scatter_dp(g2))
        small_grads[layer] = (
            jnp.concatenate([dgain1, dgain2, g_taps[:5, channels:].reshape(-1)]),
            jnp.concatenate([chan_grad.reshape(-1), head_grad.reshape(-1)]),
        )
    input_grad = jnp.concatenate(grad, axis=0)
    output = jnp.concatenate([take_step(*v, (da0,)) for v in last_parts], axis=0)

    wide_small = jnp.concatenate([small_grads[l][0] for l in range(LAYERS)])
    local_small = jnp.concatenate([small_grads[l][1] for l in range(LAYERS)])
    total = sum_over(jnp.concatenate([wide_small, local_small])[None, :], ("dp",))[0]
    wide_small = sum_over(total[None, : wide_small.shape[0]], ("tensor",))[0]
    wide_small = wide_small.reshape(LAYERS, -1)
    local_small = total[wide_small.size :].reshape(LAYERS, -1)
    gain_share = norm_gains.shape[2]
    conv_share = conv_state.shape[1]
    grad_gains = lax.dynamic_slice_in_dim(
        wide_small[:, : 2 * width].reshape(LAYERS, 2, width), slot * gain_share, gain_share, 2
    )
    grad_conv = lax.dynamic_slice_in_dim(wide_small[:, 2 * width :], slot * conv_share, conv_share, 1)
    grad_channel = local_small[:, : 6 * channels].reshape(LAYERS, 6, channels)
    grad_head = local_small[:, 6 * channels :].reshape(LAYERS, 3, ssm_heads)

    gu, down, q, gate_in, step, attn, ssm, kv, state = finish(*zip(*big))
    return (
        output[None], input_grad[None], grad_gains, q, kv, gate_in.reshape(LAYERS, depth, 2, channels),
        state, step[:, :, :ssm_heads], grad_channel, grad_conv, grad_head, attn, ssm,
        gu.reshape(LAYERS, depth, 2, hidden), down,
    )


def solution(mesh):
    split = (
        P("dp", "tensor", None),
        P("dp", "tensor", None),
        P("dp", None),
        P(None, None, ("dp", "tensor")),
        P(None, "dp", "tensor"),
        P(None, ("dp", "tensor"), None),
        P(None, "dp", None, "tensor"),
        P(None, ("dp", "tensor"), None),
        P(None, "dp", "tensor"),
        P(None, None, "tensor"),
        P(None, ("dp", "tensor")),
        P(None, None, "tensor"),
        P(None, "tensor", "dp"),
        P(None, "tensor", "dp"),
        P(None, "dp", None, "tensor"),
        P(None, "tensor", "dp"),
    )
    out_split = split[:2] + split[3:]
    return jax.shard_map(body, mesh=mesh, in_specs=split, out_specs=out_split, check_vma=False)
```
